32 devices in a mesh: seq: 8 (over z, y), ch: 4 (over x, core).
Axes of the slice: x: 2, y: 2, z: 4, core: 2. Of those that a mesh axis runs over, the one named last changes fastest.
Arguments:
- inputs: float32 [8, 4096, 512], P('seq', None, 'ch'), may hold values from -6 to 6
- cotangent: float32 [8, 4096, 512], P('seq', 'ch'), may hold values from -6 to 6
- norm_gain: float32 [512], replicated, may hold values from 0.5 to 1.5
- delta: float32 [512, 16], replicated, may hold values from -4 to 4
- alpha: float32 [512, 16], replicated, may hold values from -4 to 4
- beta: float32 [512, 16], replicated, may hold values from -4 to 4
- eta: float32 [512, 16], replicated, may hold values from -4 to 4
- omega: float32 [512], replicated, may hold values from -1 to 1
- w_value: float32 [512, 1024], replicated, may hold values from -0.25 to 0.25
- w_base: float32 [512, 2176], replicated, may hold values from -0.25 to 0.25
- qk_scale: float32 [2, 128], replicated, may hold values from 1 to 3
- qk_shift: float32 [2, 128], replicated, may hold values from -0.5 to 0.5
- w_hidden: float32 [1024, 512], replicated, may hold values from -0.046875 to 0.046875
- ffn_gain: float32 [512], replicated, may hold values from 0.5 to 1.5
- w_up: float32 [512, 1024], replicated, may hold values from -0.25 to 0.25
- w_down: float32 [1024, 512], replicated, may hold values from -0.1875 to 0.1875
- lengths: int32 [8], P('seq'), may hold values from 2049 to 4095, as said below
- key_mask: int32 [8, 128], P('seq'), may hold values 0 or 1
Outputs:
- output: float32 [8, 4096, 512], P('seq', 'ch')
- input_grad: float32 [8, 4096, 512], P('seq', None, 'ch')
- norm_gain_grad: float32 [512], replicated
- delta_grad: float32 [512, 16], replicated
- alpha_grad: float32 [512, 16], replicated
- beta_grad: float32 [512, 16], replicated
- eta_grad: float32 [512, 16], replicated
- omega_grad: float32 [512], replicated
- w_value_grad: float32 [512, 1024], replicated
- w_base_grad: float32 [512, 2176], replicated
- qk_scale_grad: float32 [2, 128], replicated
- qk_shift_grad: float32 [2, 128], replicated
- w_hidden_grad: float32 [1024, 512], replicated
- ffn_gain_grad: float32 [512], replicated
- w_up_grad: float32 [512, 1024], replicated
- w_down_grad: float32 [1024, 512], replicated
The draws below stay inside these ranges and needn't reach their ends.
Inputs may be any that keep to these rules, and one draw needn't show every extreme that they name: `lengths`: no length is a multiple of 128; of the one sequence in a row one is longer than 3072; the first sequence has length 4095.
All inputs are finite; a program needn't handle non-finite values. No bound on the sum of `key_mask` on one device may be relied on, other than what follows from the above.
Results may differ from the reference program's by a relative error of at most 0.0003.
Values sent between devices are 32-bit elements; how exact they have to be, the bound alone decides.
No kernel may reach another device: no remote copies, remote signals or barrier semaphores. Data moves between devices by JAX's collectives and lax.ppermute only.
A program may use at most 192 MiB of HBM per device.

```python
import math
import jax
import jax.numpy as jnp
from jax import lax

D = 512
QUERY_KEY_WIDTH = 128
VALUE_WIDTH = 1024
NDIM = 16
BLOCK_LENGTH = 128
FF = 1024
SLOT_LENGTH = 4096
SEQ_GRP = 1
SEQS = 8


def draw_lengths(key, part):
    key = jax.random.fold_in(key, 11)
    key_short, key_long, key_pick, key_rest = jax.random.split(key, 4)
    blocks_all = SLOT_LENGTH // BLOCK_LENGTH
    shorter = jax.random.randint(key_short, (SEQS,), blocks_all // 2, blocks_all)
    longer = jax.random.randint(key_long, (SEQS,), 3 * blocks_all // 4, blocks_all)
    pick = jax.random.randint(key_pick, (SEQS // SEQ_GRP,), 0, SEQ_GRP)
    chosen = jnp.arange(SEQS) % SEQ_GRP == jnp.repeat(pick, SEQ_GRP)
    block_count = jnp.where(chosen, longer, shorter)
    remainder = jax.random.randint(key_rest, (SEQS,), 1, BLOCK_LENGTH)
    drawn = (block_count * BLOCK_LENGTH + remainder).astype(jnp.int32)
    return drawn.at[0].set(SLOT_LENGTH - 1).astype(jnp.int32)


def with_ends(array, rng, smallest, top_value):
    longest = array.shape.index(max(array.shape))
    spots = []
    for shift in (0, 1):
        where = [jax.random.randint(jax.random.fold_in(rng, axis), (), 0, length) for axis, length in enumerate(array.shape)]
        where[longest] = (where[longest] + shift) % array.shape[longest]
        spots.append(tuple(where))
    return array.at[spots[0]].set(smallest).at[spots[1]].set(top_value)


def level_of(key, shape, pieces, least, high):
    level = 1.0
    for dim, shards_of in pieces:
        steps = jax.random.uniform(jax.random.fold_in(jax.random.fold_in(key, 6), dim), (shards_of,), jnp.float32, least / len(pieces), high / len(pieces))
        level = level * jnp.repeat(jnp.exp(steps), shape[dim] // shards_of).reshape((-1,) + (1,) * (len(shape) - 1 - dim))
    return level


def centred(rng, extent, spread, bound, cuts=(), kind=jnp.bfloat16):
    values = spread * jax.random.normal(rng, extent, jnp.float32)
    if cuts:
        values = values * level_of(rng, extent, cuts, -0.22, 0.18)
    return jnp.clip(values, -bound, bound).astype(kind)


def setup_inputs(seed: int = 0) -> dict:
    keys = jax.random.split(jax.random.key(seed), 19)
    return {
        "inputs": centred(keys[0], (SEQS, SLOT_LENGTH, D), 1.0, 6.0, ((0, 8), (2, 4)), jnp.float32),
        "cotangent": centred(keys[1], (SEQS, SLOT_LENGTH, D), 1.0, 6.0, ((0, 8), (1, 4)), jnp.float32),
        "norm_gain": jnp.clip(1.0 + 0.1 * jax.random.normal(keys[2], (D,), jnp.float32), 0.5, 1.5),
        "delta": jnp.clip(jax.random.uniform(keys[3], (D, NDIM), jnp.float32, -4.0, 4.0), -4.0, 4.0),
        "alpha": jnp.clip(jax.random.uniform(keys[4], (D, NDIM), jnp.float32, -4.0, 4.0), -4.0, 4.0),
        "beta": centred(keys[5], (D, NDIM), 1.0, 4.0, (), jnp.float32),
        "eta": centred(keys[6], (D, NDIM), 1.0, 4.0, (), jnp.float32),
        "omega": jnp.clip(jax.random.uniform(keys[7], (D,), jnp.float32, -1.0, 1.0), -1.0, 1.0),
        "w_value": centred(keys[8], (D, VALUE_WIDTH), D ** -0.5, 0.25, (), jnp.float32),
        "w_base": centred(keys[9], (D, 2 * D + QUERY_KEY_WIDTH + VALUE_WIDTH), D ** -0.5, 0.25, (), jnp.float32),
        "qk_scale": jnp.clip(jax.random.uniform(keys[10], (2, QUERY_KEY_WIDTH), jnp.float32, 1.0, 3.0), 1.0, 3.0),
        "qk_shift": jnp.clip(jax.random.uniform(keys[11], (2, QUERY_KEY_WIDTH), jnp.float32, -0.5, 0.5), -0.5, 0.5),
        "w_hidden": centred(keys[12], (VALUE_WIDTH, D), (VALUE_WIDTH * BLOCK_LENGTH // 8) ** -0.5, 0.046875, (), jnp.float32),
        "ffn_gain": jnp.clip(1.0 + 0.1 * jax.random.normal(keys[13], (D,), jnp.float32), 0.5, 1.5),
        "w_up": centred(keys[14], (D, FF), D ** -0.5, 0.25, (), jnp.float32),
        "w_down": centred(keys[15], (FF, D), FF ** -0.5, 0.1875, (), jnp.float32),
        "lengths": draw_lengths(jax.random.fold_in(keys[18], 71), 0),
        "key_mask": with_ends((jax.random.randint(keys[17], (SEQS, BLOCK_LENGTH), 0, 4) < 3).astype(jnp.int32), jax.random.fold_in(keys[17], 1), 0, 1),
    }


EPS = 1e-05
CENTER = math.sqrt(0.5)
SPREAD = math.sqrt(0.25 / math.pi)
HIGH_PRECISION = lax.Precision.HIGHEST

def laplace(score_matrix):
    return 0.5 * (1.0 + jax.scipy.special.erf((score_matrix - CENTER) / (SPREAD * math.sqrt(2.0))))

def layer_norm(value_rows, gain):
    mean = lax.optimization_barrier(jnp.mean(value_rows, -1, keepdims=True))
    variance = lax.optimization_barrier(jnp.mean(value_rows * value_rows, -1, keepdims=True)) - mean * mean
    return (value_rows - mean) * lax.rsqrt(variance + EPS) * gain

def sequence_forward(tokens, norm_gain, delta, alpha, beta, eta, omega, w_value, w_base, qk_scale, qk_shift, w_hidden, ffn_gain, w_up, w_down, live, valid):
    normed = layer_norm(tokens, norm_gain)
    gate = jax.nn.sigmoid(delta)
    keep = 1.0 - gate * jax.nn.sigmoid(alpha)
    inject = gate * beta
    readout = eta / math.sqrt(NDIM)

    def advance(state, column):
        state = keep * state + inject * column[:, None]
        return (state, lax.optimization_barrier(jnp.sum(readout * state, -1)))

    def block_scan(state, columns):
        return lax.scan(advance, state, columns)
    start_state = jnp.zeros((D, NDIM), jnp.float32)
    final_state, smoothed = lax.scan(jax.checkpoint(block_scan), start_state, normed.reshape(SLOT_LENGTH // BLOCK_LENGTH, BLOCK_LENGTH, D))
    mixed = jax.nn.silu(smoothed.reshape(SLOT_LENGTH, D) + omega * normed)
    value_rows = jax.nn.silu(jnp.dot(normed, w_value, precision=HIGH_PRECISION))
    base = jnp.dot(mixed, w_base, precision=HIGH_PRECISION)
    update = jax.nn.sigmoid(base[:, :D])
    shared = jax.nn.silu(base[:, D:D + QUERY_KEY_WIDTH + VALUE_WIDTH])
    zpart = shared[:, :QUERY_KEY_WIDTH]
    reset = shared[:, QUERY_KEY_WIDTH:]
    hidden_in = base[:, D + QUERY_KEY_WIDTH + VALUE_WIDTH:]
    query_rows = zpart * qk_scale[0] + qk_shift[0]
    key_rows = zpart * qk_scale[1] + qk_shift[1]
    block_count = SLOT_LENGTH // BLOCK_LENGTH
    valid_blocks = valid.reshape(block_count, BLOCK_LENGTH)
    position_counts = jnp.maximum(lax.optimization_barrier(jnp.sum(valid_blocks, -1)), 1.0)
    score_matrix = jnp.einsum('xig,xng->xin', query_rows.reshape(block_count, BLOCK_LENGTH, QUERY_KEY_WIDTH), key_rows.reshape(block_count, BLOCK_LENGTH, QUERY_KEY_WIDTH), precision=HIGH_PRECISION) / position_counts[:, None, None]
    causal = jnp.tril(jnp.ones((BLOCK_LENGTH, BLOCK_LENGTH), jnp.float32))
    attention_weights = laplace(score_matrix) * causal[None] * valid_blocks[:, None, :]
    attended_values = jnp.einsum('yja,yaw->yjw', attention_weights, value_rows.reshape(block_count, BLOCK_LENGTH, VALUE_WIDTH), precision=HIGH_PRECISION).reshape(SLOT_LENGTH, VALUE_WIDTH)
    hidden = jax.nn.silu(hidden_in + jnp.dot(attended_values * reset, w_hidden, precision=HIGH_PRECISION))
    gated = tokens + update * (hidden - tokens)
    ffn_in = layer_norm(gated, ffn_gain)
    result = gated + jnp.dot(jax.nn.silu(jnp.dot(ffn_in, w_up, precision=HIGH_PRECISION)), w_down, precision=HIGH_PRECISION)
    return result * live[:, None]

def reference(inputs, cotangent, norm_gain, delta, alpha, beta, eta, omega, w_value, w_base, qk_scale, qk_shift, w_hidden, ffn_gain, w_up, w_down, lengths, key_mask):
    params = (norm_gain, delta, alpha, beta, eta, omega, w_value, w_base, qk_scale, qk_shift, w_hidden, ffn_gain, w_up, w_down)
    positions = jnp.arange(SLOT_LENGTH, dtype=jnp.int32)

    def per_sequence(totals, item):
        tokens, cotan, length, flags = item
        inside = positions < length
        live = inside.astype(jnp.float32)
        final = (length - 1) // BLOCK_LENGTH
        tiled = jnp.tile(flags, SLOT_LENGTH // BLOCK_LENGTH)
        valid = (inside & ((positions // BLOCK_LENGTH != final) | (tiled == 1))).astype(jnp.float32)

        def forward(tokens, *weights):
            return sequence_forward(tokens, *weights, live, valid)
        result, pullback = jax.vjp(forward, tokens, *params)
        grads = pullback(cotan)
        totals = tuple((left + right for left, right in zip(totals, grads[1:])))
        return (totals, (result, grads[0]))
    zeros = tuple((jnp.zeros_like(weight) for weight in params))
    totals, outs = lax.scan(per_sequence, zeros, (inputs, cotangent, lengths, key_mask))
    return (outs[0], outs[1], totals[0], totals[1], totals[2], totals[3], totals[4], totals[5], totals[6], totals[7], totals[8], totals[9], totals[10], totals[11], totals[12], totals[13])
```

```python
import math

import jax
import jax.numpy as jnp
from jax import lax
from jax.experimental import pallas as pl
from jax.experimental.pallas import tpu as pltpu
from jax.sharding import PartitionSpec as P

EPS = 1e-05
CENTER = math.sqrt(0.5)
SPREAD = math.sqrt(0.25 / math.pi)
F32 = jnp.float32
BF16 = jnp.bfloat16
NN = ((1,), (0,))
NT = ((1,), (1,))
TN = ((0,), (0,))
LANES = 128
SUBS = 8
TILE = 256
VMEM = pl.BlockSpec(memory_space=pltpu.VMEM)
SMEM = pl.BlockSpec(memory_space=pltpu.SMEM)


def params(mib):
    return pltpu.CompilerParams(vmem_limit_bytes=mib << 20)


def split(value):
    high = value.astype(BF16)
    return high, (value - high.astype(F32)).astype(BF16)


def dot(left, right, dims):
    return lax.dot_general(left, right, (dims, ((), ())), preferred_element_type=F32)


def mm3(left, right, dims):
    return (
        dot(left[0], right[0], dims)
        + dot(left[1], right[0], dims)
        + dot(left[0], right[1], dims)
    )


def mm3_short(left, right, dims):
    (left_axis,), (right_axis,) = dims
    return dot(
        jnp.concatenate([left[0], left[1], left[0]], left_axis),
        jnp.concatenate([right[0], right[0], right[1]], right_axis),
        dims,
    )


def sigmoid(value):
    return 0.5 * jnp.tanh(0.5 * value) + 0.5


def rows_sum(value):
    return jnp.sum(value, -1, keepdims=True)


def split_kernel(*refs):
    count = len(refs) // 3
    for index in range(count):
        high, low = split(refs[index][...])
        refs[count + 2 * index][...] = high
        refs[count + 2 * index + 1][...] = low


def split_weights(weights, steps=8):
    def spec(weight):
        return pl.BlockSpec((weight.shape[0] // steps, weight.shape[1]), lambda i: (i, 0))

    out = pl.pallas_call(
        split_kernel,
        grid=(steps,),
        in_specs=[spec(w) for w in weights],
        out_specs=[spec(w) for w in weights for _ in range(2)],
        out_shape=[jax.ShapeDtypeStruct(w.shape, BF16) for w in weights for _ in range(2)],
        compiler_params=params(40),
        cost_estimate=pl.CostEstimate(
            flops=4 * sum(w.size for w in weights),
            bytes_accessed=8 * sum(w.size for w in weights),
            transcendentals=0,
        ),
        name="split_weights",
    )(*weights)
    return [(out[2 * i], out[2 * i + 1]) for i in range(len(weights))]


def scan_ends(read, keep_ref, states, span, reverse):
    keeps = [jnp.broadcast_to(keep_ref[n : n + 1, :], (SUBS, LANES)) for n in range(states)]

    def step(i, state):
        t = span - 1 - i if reverse else i
        fresh = read(t)
        return tuple(k * s + fresh for k, s in zip(keeps, state))

    zero = jnp.zeros((SUBS, LANES), F32)
    return lax.fori_loop(0, span, step, (zero,) * states, unroll=4)


def fold_ends(ends_ref, group, chunk_keep, states, order):
    total = jnp.zeros((states, LANES), F32)
    for chunk in order:
        total = chunk_keep * total + ends_ref[group, pl.ds(chunk, states, stride=SUBS), :]
    return total


def norm_kernel(x_ref, gain_ref, keep_ref, chunk_keep_ref, normed_ref, ends_ref, final_ref):
    groups, rows, _ = x_ref.shape
    states = keep_ref.shape[1]
    span = rows // SUBS
    width = groups * LANES

    def normalise(i, carry):
        here = pl.ds(pl.multiple_of(i * 128, 128), 128)
        pieces = [x_ref[g, here, :] for g in range(groups)]
        mean = rows_sum(sum(pieces)) / width
        square = rows_sum(sum(p * p for p in pieces)) / width
        scale = lax.rsqrt(square - mean * mean + EPS)
        for g in range(groups):
            normed_ref[g, here, :] = (pieces[g] - mean) * scale * gain_ref[g]
        return carry

    lax.fori_loop(0, rows // 128, normalise, 0)
    for g in range(groups):
        ends = scan_ends(
            lambda t: normed_ref[g, pl.ds(t, SUBS, stride=span), :],
            keep_ref.at[g],
            states,
            span,
            False,
        )
        for n in range(states):
            ends_ref[g, n * SUBS : (n + 1) * SUBS, :] = ends[n]
        final_ref[g] = fold_ends(ends_ref, g, chunk_keep_ref[g], states, range(SUBS))


def mix_kernel(
    place_ref,
    normed_ref,
    ends_ref,
    finals_ref,
    keep_ref,
    coef_ref,
    chunk_keep_ref,
    device_keep_ref,
    omega_ref,
    total_ref,
    start_ref,
):
    groups, rows, _ = normed_ref.shape
    states = keep_ref.shape[1]
    span = rows // SUBS
    ways = finals_ref.shape[0]
    place = place_ref[0]
    for g in range(groups):
        state = jnp.zeros((states, LANES), F32)
        for d in range(ways):
            state = jnp.where(d < place, device_keep_ref[g] * state + finals_ref[d, g], state)
        for chunk in range(SUBS):
            start_ref[g, pl.ds(chunk, states, stride=SUBS), :] = state
            state = chunk_keep_ref[g] * state + ends_ref[g, pl.ds(chunk, states, stride=SUBS), :]
        keeps = [jnp.broadcast_to(keep_ref[g, n : n + 1, :], (SUBS, LANES)) for n in range(states)]
        coefs = [jnp.broadcast_to(coef_ref[g, n : n + 1, :], (SUBS, LANES)) for n in range(states)]
        omega = jnp.broadcast_to(omega_ref[g], (SUBS, LANES))

        def step(t, state):
            here = pl.ds(t, SUBS, stride=span)
            fresh = normed_ref[g, here, :]
            state = tuple(k * s + fresh for k, s in zip(keeps, state))
            parts = [c * s for c, s in zip(coefs, state)] + [omega * fresh]
            while len(parts) > 1:
                parts = [sum(parts[i : i + 2]) for i in range(0, len(parts), 2)]
            total_ref[g, here, :] = parts[0]
            return state

        first = tuple(start_ref[g, n * SUBS : (n + 1) * SUBS, :] for n in range(states))
        lax.fori_loop(0, span, step, first, unroll=4)


def back_ends_kernel(grad_ref, keep_ref, chunk_keep_ref, ends_ref, final_ref):
    groups, rows, _ = grad_ref.shape
    states = keep_ref.shape[1]
    span = rows // SUBS
    for g in range(groups):
        ends = scan_ends(
            lambda t: grad_ref[g, pl.ds(t, SUBS, stride=span), :],
            keep_ref.at[g],
            states,
            span,
            True,
        )
        for n in range(states):
            ends_ref[g, n * SUBS : (n + 1) * SUBS, :] = ends[n]
        final_ref[g] = fold_ends(ends_ref, g, chunk_keep_ref[g], states, reversed(range(SUBS)))


def back_kernel(
    place_ref,
    grad_ref,
    ends_ref,
    finals_ref,
    start_ref,
    normed_ref,
    x_ref,
    direct_ref,
    part_ref,
    keep_ref,
    coef_ref,
    chunk_keep_ref,
    device_keep_ref,
    gain_ref,
    out_ref,
    coef_grad_ref,
    keep_grad_ref,
    gain_grad_ref,
    sum_ref,
    init_ref,
):
    groups, rows, _ = grad_ref.shape
    states = keep_ref.shape[1]
    span = rows // SUBS
    ways = finals_ref.shape[0]
    place = place_ref[0]
    half = states // 2
    zero = jnp.zeros((SUBS, LANES), F32)
    for g in range(groups):
        state = jnp.zeros((states, LANES), F32)
        for d in reversed(range(ways)):
            state = jnp.where(d > place, device_keep_ref[g] * state + finals_ref[d, g], state)
        for chunk in reversed(range(SUBS)):
            init_ref[pl.ds(chunk, states, stride=SUBS), :] = state
            state = chunk_keep_ref[g] * state + ends_ref[g, pl.ds(chunk, states, stride=SUBS), :]
        for part in range(2):
            these = range(part * half, (part + 1) * half)
            keeps = [jnp.broadcast_to(keep_ref[g, n : n + 1, :], (SUBS, LANES)) for n in these]
            coefs = [jnp.broadcast_to(coef_ref[g, n : n + 1, :], (SUBS, LANES)) for n in these]

            def step(i, carry):
                lam, second, coef_acc, keep_acc = carry
                here = pl.ds(span - 1 - i, SUBS, stride=span)
                fresh = grad_ref[g, here, :]
                source = normed_ref[g, here, :]
                keep_acc = tuple(a + v * source for a, v in zip(keep_acc, second))
                lam = tuple(k * l + fresh for k, l in zip(keeps, lam))
                coef_acc = tuple(a + l * source for a, l in zip(coef_acc, lam))
                second = tuple(l + k * v for l, k, v in zip(lam, keeps, second))
                parts = [c * l for c, l in zip(coefs, lam)]
                while len(parts) > 1:
                    parts = [sum(parts[j : j + 2]) for j in range(0, len(parts), 2)]
                before = part_ref[g, here, :] if part == 0 else sum_ref[g, here, :]
                sum_ref[g, here, :] = before + parts[0]
                return lam, second, coef_acc, keep_acc

            first = tuple(init_ref[n * SUBS : (n + 1) * SUBS, :] for n in these)
            nothing = (zero,) * half
            lam, second, coef_acc, keep_acc = lax.fori_loop(
                0, span, step, (first, nothing, nothing, nothing), unroll=2
            )
            for j, n in enumerate(these):
                start = start_ref[g, n * SUBS : (n + 1) * SUBS, :]
                keep_acc_n = keep_acc[j] + start * second[j]
                coef_grad_ref[g, n : n + 1, :] = jnp.sum(coef_acc[j], 0, keepdims=True)
                keep_grad_ref[g, n : n + 1, :] = jnp.sum(keep_acc_n, 0, keepdims=True)
        gain_grad_ref[g] = jnp.zeros((1, LANES), F32)

    width = groups * LANES

    def finish(i, carry):
        here = pl.ds(pl.multiple_of(i * 128, 128), 128)
        pieces = [x_ref[g, here, :] for g in range(groups)]
        mean = rows_sum(sum(pieces)) / width
        square = rows_sum(sum(p * p for p in pieces)) / width
        scale = lax.rsqrt(square - mean * mean + EPS)
        centered = [(p - mean) * scale for p in pieces]
        grads = [sum_ref[g, here, :] for g in range(groups)]
        for g in range(groups):
            gain_grad_ref[g] += jnp.sum(grads[g] * centered[g], 0, keepdims=True)
        scaled = [grads[g] * gain_ref[g] for g in range(groups)]
        plain = rows_sum(sum(scaled)) / width
        cross = rows_sum(sum(s * c for s, c in zip(scaled, centered))) / width
        for g in range(groups):
            out_ref[g, here, :] = direct_ref[g, here, :] + scale * (
                scaled[g] - plain - centered[g] * cross
            )
        return carry

    lax.fori_loop(0, rows // 128, finish, 0)


def block_kernel(
    info_ref,
    mask_ref,
    x_ref,
    normed_ref,
    total_ref,
    cot_ref,
    scale_ref,
    shift_ref,
    gain_ref,
    wv_h,
    wv_l,
    wb_h,
    wb_l,
    wh_h,
    wh_l,
    wu_h,
    wu_l,
    wd_h,
    wd_l,
    out_ref,
    direct_ref,
    n_h,
    n_l,
    m_h,
    m_l,
    gr_h,
    gr_l,
    f_h,
    f_l,
    a_h,
    a_l,
    do_h,
    do_l,
    du_h,
    du_l,
    dv_h,
    dv_l,
    bu_h,
    bu_l,
    bz_h,
    bz_l,
    br_h,
    br_l,
    bh_h,
    bh_l,
    gain_grad_ref,
    qk_grad_ref,
    v_h,
    v_l,
    vsil,
    upd,
    rst,
    rsil,
    att,
    hpre,
    hsil,
    usil,
    da_h,
    da_l,
):
    tile = pl.program_id(0)
    groups = x_ref.shape[0]
    width = groups * LANES
    zwidth = scale_ref.shape[1]
    values = wv_h.shape[1]
    hidden_units = wu_h.shape[1]
    span = mask_ref.shape[1]
    rows = x_ref.shape[1]
    start, length = info_ref[0], info_ref[1]
    base_row = start + tile * rows

    @pl.when(tile == 0)
    def _():
        gain_grad_ref[...] = jnp.zeros_like(gain_grad_ref)
        qk_grad_ref[...] = jnp.zeros_like(qk_grad_ref)

    def put(high_ref, low_ref, where, value):
        high, low = split(value)
        high_ref[where] = high
        low_ref[where] = low
        return high, low

    def columns(total, step=512):
        return [slice(i, min(i + step, total)) for i in range(0, total, step)]

    every = slice(None)

    normed = jnp.concatenate([normed_ref[g] for g in range(groups)], 1)
    n_pair = put(n_h, n_l, (every, every), normed)
    total = jnp.concatenate([total_ref[g] for g in range(groups)], 1)
    m_pair = put(m_h, m_l, (every, every), total * sigmoid(total))
    for c in columns(values):
        pre = mm3(n_pair, (wv_h[:, c], wv_l[:, c]), NN)
        s = sigmoid(pre)
        act = pre * s
        put(v_h, v_l, (every, c), act)
        vsil[:, c] = s + act * (1.0 - s)
    c = slice(0, width)
    upd[...] = sigmoid(mm3(m_pair, (wb_h[:, c], wb_l[:, c]), NN))
    c = slice(width, width + zwidth)
    pre = mm3(m_pair, (wb_h[:, c], wb_l[:, c]), NN)
    s = sigmoid(pre)
    z = pre * s
    zsil = s + z * (1.0 - s)
    for c in columns(values):
        w = slice(width + zwidth + c.start, width + zwidth + c.stop)
        pre = mm3(m_pair, (wb_h[:, w], wb_l[:, w]), NN)
        s = sigmoid(pre)
        act = pre * s
        rst[:, c] = act
        rsil[:, c] = s + act * (1.0 - s)
    w = slice(width + zwidth + values, width + zwidth + values + width)
    hpre[...] = mm3(m_pair, (wb_h[:, w], wb_l[:, w]), NN)
    query = z * scale_ref[0:1, :] + shift_ref[0:1, :]
    key = z * scale_ref[1:2, :] + shift_ref[1:2, :]
    q_pair = split(query)
    k_pair = split(key)
    lane = lax.broadcasted_iota(jnp.int32, (1, span), 1)
    causal = lax.broadcasted_iota(jnp.int32, (span, span), 0) >= lax.broadcasted_iota(
        jnp.int32, (span, span), 1
    )
    slopes, weights = [], []
    for b in range(rows // span):
        r = slice(b * span, (b + 1) * span)
        position = base_row + b * span + lane
        last_block = (base_row + b * span) // span == (length - 1) // span
        kept = (position < length) & (jnp.logical_not(last_block) | (mask_ref[...] == 1))
        valid = jnp.where(kept, 1.0, 0.0)
        count = jnp.maximum(rows_sum(valid), 1.0)
        mask = jnp.where(causal, valid, 0.0)
        scores = (
            mm3_short((q_pair[0][r], q_pair[1][r]), (k_pair[0][r], k_pair[1][r]), NT) / count
        )
        spot = scores - CENTER
        weight = split(
            (0.5 + 0.5 * lax.erf(spot * (1.0 / (SPREAD * math.sqrt(2.0))))) * mask
        )
        slopes.append(
            jnp.exp(spot * spot * (-1.0 / (2.0 * SPREAD * SPREAD)))
            * (mask / count)
            * (1.0 / (SPREAD * math.sqrt(2.0 * math.pi)))
        )
        weights.append(weight)
        for c in columns(values):
            got = mm3_short(weight, (v_h[r, c], v_l[r, c]), NN)
            att[r, c] = got
            put(gr_h, gr_l, (r, c), got * rst[r, c])
    pre = hpre[...] + mm3((gr_h[...], gr_l[...]), (wh_h[...], wh_l[...]), NN)
    s = sigmoid(pre)
    hidden = pre * s
    hsil[...] = s + hidden * (1.0 - s)
    x = jnp.concatenate([x_ref[g] for g in range(groups)], 1)
    update = upd[...]
    apart = hidden - x
    gated = x + update * apart
    mean = rows_sum(gated) / width
    square = rows_sum(gated * gated) / width
    scale = lax.rsqrt(square - mean * mean + EPS)
    centered = (gated - mean) * scale
    f_pair = put(f_h, f_l, (every, every), centered * gain_ref[...])
    for c in columns(hidden_units):
        pre = mm3(f_pair, (wu_h[:, c], wu_l[:, c]), NN)
        s = sigmoid(pre)
        act = pre * s
        put(a_h, a_l, (every, c), act)
        usil[:, c] = s + act * (1.0 - s)
    live = (
        base_row + lax.broadcasted_iota(jnp.int32, (rows, 1), 0) < length
    ).astype(F32)
    out_ref[...] = (gated + mm3((a_h[...], a_l[...]), (wd_h[...], wd_l[...]), NN)) * live

    grad_out = cot_ref[...] * live
    do_pair = put(do_h, do_l, (every, every), grad_out)
    for c in columns(hidden_units):
        put(
            du_h,
            du_l,
            (every, c),
            mm3(do_pair, (wd_h[c, :], wd_l[c, :]), NT) * usil[:, c],
        )
    grad_f = mm3((du_h[...], du_l[...]), (wu_h[...], wu_l[...]), NT)
    gain_grad_ref[...] += jnp.sum(grad_f * centered, 0, keepdims=True)
    scaled = grad_f * gain_ref[...]
    grad_gated = grad_out + scale * (
        scaled - rows_sum(scaled) / width - centered * (rows_sum(scaled * centered) / width)
    )
    put(bu_h, bu_l, (every, every), grad_gated * apart * update * (1.0 - update))
    direct = grad_gated * (1.0 - update)
    for g in range(groups):
        direct_ref[g] = direct[:, g * LANES : (g + 1) * LANES]
    h_pair = put(bh_h, bh_l, (every, every), grad_gated * update * hsil[...])
    for c in columns(values):
        got = mm3(h_pair, (wh_h[c, :], wh_l[c, :]), NT)
        put(da_h, da_l, (every, c), got * rst[:, c])
        put(br_h, br_l, (every, c), got * att[:, c] * rsil[:, c])
    for b in range(rows // span):
        r = slice(b * span, (b + 1) * span)
        grad_scores = split(mm3((da_h[r, :], da_l[r, :]), (v_h[r, :], v_l[r, :]), NT) * slopes[b])
        for c in columns(values):
            got = mm3_short(weights[b], (da_h[r, c], da_l[r, c]), TN)
            put(dv_h, dv_l, (r, c), got * vsil[r, c])
        grad_q = mm3_short(grad_scores, (k_pair[0][r], k_pair[1][r]), NN)
        grad_k = mm3_short(grad_scores, (q_pair[0][r], q_pair[1][r]), TN)
        qk_grad_ref[0:1, :] += jnp.sum(grad_q * z[r], 0, keepdims=True)
        qk_grad_ref[1:2, :] += jnp.sum(grad_k * z[r], 0, keepdims=True)
        qk_grad_ref[2:3, :] += jnp.sum(grad_q, 0, keepdims=True)
        qk_grad_ref[3:4, :] += jnp.sum(grad_k, 0, keepdims=True)
        grad_z = (grad_q * scale_ref[0:1, :] + grad_k * scale_ref[1:2, :]) * zsil[r]
        put(bz_h, bz_l, (r, every), grad_z)


def block_call(info, key_mask, x4, normed4, total4, cot, qk_scale, qk_shift, ffn_gain, pairs):
    groups, rows, _ = x4.shape
    width = groups * LANES
    wv, wb, wh, wu, wd = pairs
    values, units, zwidth = wv[0].shape[1], wu[0].shape[1], qk_scale.shape[1]
    flat = [part for pair in pairs for part in pair]
    by_group = pl.BlockSpec((groups, TILE, LANES), lambda i: (0, i, 0))

    def by_row(columns):
        return pl.BlockSpec((TILE, columns), lambda i: (i, 0))

    halves = [width, width, values, width, units, width, units, values, width, zwidth, values, width]
    out_shape = [
        jax.ShapeDtypeStruct((rows, width), F32),
        jax.ShapeDtypeStruct((groups, rows, LANES), F32),
    ]
    out_specs = [by_row(width), by_group]
    for columns in halves:
        out_shape += [jax.ShapeDtypeStruct((rows, columns), BF16)] * 2
        out_specs += [by_row(columns)] * 2
    out_shape += [
        jax.ShapeDtypeStruct((1, width), F32),
        jax.ShapeDtypeStruct((8, zwidth), F32),
    ]
    out_specs += [
        pl.BlockSpec((1, width), lambda i: (0, 0)),
        pl.BlockSpec((8, zwidth), lambda i: (0, 0)),
    ]
    macs = rows * (2 * wv[0].size + 2 * wb[0].size + 3 * wh[0].size)
    out = pl.pallas_call(
        block_kernel,
        grid=(rows // TILE,),
        in_specs=[SMEM, VMEM, by_group, by_group, by_group, by_row(width), VMEM, VMEM, VMEM]
        + [VMEM] * len(flat),
        out_specs=out_specs,
        out_shape=out_shape,
        scratch_shapes=[
            pltpu.VMEM((TILE, values), BF16),
            pltpu.VMEM((TILE, values), BF16),
            pltpu.VMEM((TILE, values), F32),
            pltpu.VMEM((TILE, width), F32),
            pltpu.VMEM((TILE, values), F32),
            pltpu.VMEM((TILE, values), F32),
            pltpu.VMEM((TILE, values), F32),
            pltpu.VMEM((TILE, width), F32),
            pltpu.VMEM((TILE, width), F32),
            pltpu.VMEM((TILE, units), F32),
            pltpu.VMEM((TILE, values), BF16),
            pltpu.VMEM((TILE, values), BF16),
        ],
        compiler_params=params(60),
        cost_estimate=pl.CostEstimate(flops=6 * macs, bytes_accessed=60 << 20, transcendentals=0),
        name="blocks",
    )(info, key_mask, x4, normed4, total4, cot, qk_scale, qk_shift, ffn_gain, *flat)
    out = list(out)
    pairs_out = [(out[2 + 2 * i], out[3 + 2 * i]) for i in range(len(halves))]
    return out[0], out[1], pairs_out, out[-2], out[-1]


def weight_kernel(x_h, x_l, y_h, y_l, out_ref):
    out_ref[...] = mm3((x_h[...], x_l[...]), (y_h[...], y_l[...]), TN)


def weight_grad(x, y, name, step=256):
    rows, left = x[0].shape
    right = y[0].shape[1]
    step = min(step, right)
    whole = pl.BlockSpec((rows, left), lambda i: (0, 0))
    part = pl.BlockSpec((rows, step), lambda i: (0, i))
    return pl.pallas_call(
        weight_kernel,
        grid=(right // step,),
        in_specs=[whole, whole, part, part],
        out_specs=pl.BlockSpec((left, step), lambda i: (0, i)),
        out_shape=jax.ShapeDtypeStruct((left, right), F32),
        compiler_params=params(40),
        cost_estimate=pl.CostEstimate(
            flops=6 * rows * left * right,
            bytes_accessed=4 * (rows * (left + right) + left * right),
            transcendentals=0,
        ),
        name=name,
    )(x[0], x[1], y[0], y[1])


def input_kernel(
    total_ref,
    normed_ref,
    omega_ref,
    dv_h,
    dv_l,
    bu_h,
    bu_l,
    bz_h,
    bz_l,
    br_h,
    br_l,
    bh_h,
    bh_l,
    wv_h,
    wv_l,
    wb_h,
    wb_l,
    grad_ref,
    part_ref,
    omega_grad_ref,
):
    groups = total_ref.shape[0]

    @pl.when(pl.program_id(0) == 0)
    def _():
        omega_grad_ref[...] = jnp.zeros_like(omega_grad_ref)

    grad = None
    at = 0
    for high, low in ((bu_h, bu_l), (bz_h, bz_l), (br_h, br_l), (bh_h, bh_l)):
        w = slice(at, at + high.shape[1])
        at = w.stop
        one = mm3 if high.shape[1] > 128 else mm3_short
        got = one((high[...], low[...]), (wb_h[:, w], wb_l[:, w]), NT)
        grad = got if grad is None else grad + got
    grad_n = mm3((dv_h[...], dv_l[...]), (wv_h[...], wv_l[...]), NT)
    for g in range(groups):
        lanes = slice(g * LANES, (g + 1) * LANES)
        total = total_ref[g]
        s = sigmoid(total)
        got = grad[:, lanes] * (s + total * s * (1.0 - s))
        grad_ref[g] = got
        part_ref[g] = grad_n[:, lanes] + got * omega_ref[g]
        omega_grad_ref[g] += jnp.sum(got * normed_ref[g], 0, keepdims=True)


def input_call(total4, normed4, omega, dv, parts, wv, wb):
    groups, rows, _ = total4.shape
    by_group = pl.BlockSpec((groups, TILE, LANES), lambda i: (0, i, 0))
    halves = [half for pair in (dv,) + tuple(parts) for half in pair]
    return pl.pallas_call(
        input_kernel,
        grid=(rows // TILE,),
        in_specs=[by_group, by_group, VMEM]
        + [pl.BlockSpec((TILE, h.shape[1]), lambda i: (i, 0)) for h in halves]
        + [VMEM] * 4,
        out_specs=[by_group, by_group, pl.BlockSpec((groups, 1, LANES), lambda i: (0, 0, 0))],
        out_shape=[
            jax.ShapeDtypeStruct(total4.shape, F32),
            jax.ShapeDtypeStruct(total4.shape, F32),
            jax.ShapeDtypeStruct((groups, 1, LANES), F32),
        ],
        compiler_params=params(48),
        cost_estimate=pl.CostEstimate(
            flops=6 * rows * (wv[0].size + wb[0].size), bytes_accessed=32 << 20, transcendentals=0
        ),
        name="input_grads",
    )(total4, normed4, omega, *halves, wv[0], wv[1], wb[0], wb[1])


def swap(value, axis, distance):
    size = lax.axis_size(axis)
    return lax.ppermute(value, axis, [(i, i ^ distance) for i in range(size)])


def side(axis, distance):
    return (lax.axis_index(axis) // distance) % 2


def halve(value, axis, distance):
    half = value.shape[0] // 2
    own = side(axis, distance)
    send = lax.dynamic_slice_in_dim(value, (1 - own) * half, half, 0)
    keep = lax.dynamic_slice_in_dim(value, own * half, half, 0)
    return keep + swap(send, axis, distance)


def double(value, axis, distance):
    got = swap(value, axis, distance)
    own = side(axis, distance)
    half = value.shape[0]
    out = jnp.zeros((2 * half,) + value.shape[1:], value.dtype)
    out = lax.dynamic_update_slice_in_dim(out, value, own * half, 0)
    return lax.dynamic_update_slice_in_dim(out, got, (1 - own) * half, 0)


def device_steps():
    def bits(axis):
        size = lax.axis_size(axis)
        return [(axis, 1 << i) for i in range(size.bit_length() - 1)]

    return bits("ch"), bits("seq")


def orders():
    ch, seq = device_steps()
    first, rest = ch[0], [ch[1:], seq[:1], seq[1:2]]
    tail = seq[2:]
    out = []
    for turn in range(3):
        turned = rest[turn:] + rest[:turn]
        out.append([first] + [step for group in turned for step in group] + tail)
    return out


def sum_group(parts, plans):
    parts = list(parts)
    for s in range(len(plans[0])):
        parts = [halve(part, *plan[s]) for part, plan in zip(parts, plans)]
    for s in reversed(range(len(plans[0]))):
        parts = [double(part, *plan[s]) for part, plan in zip(parts, plans)]
    return parts


def sum_small(value):
    ch, seq = device_steps()
    for axis, distance in ch + seq:
        value = value + swap(value, axis, distance)
    return value


def local(
    inputs,
    cotangent,
    norm_gain,
    delta,
    alpha,
    beta,
    eta,
    omega,
    w_value,
    w_base,
    qk_scale,
    qk_shift,
    w_hidden,
    ffn_gain,
    w_up,
    w_down,
    lengths,
    key_mask,
):
    ways = lax.axis_size("ch")
    place = lax.axis_index("ch").astype(jnp.int32)
    _, length, narrow = inputs.shape
    rows = length // ways
    width = narrow * ways
    groups = width // LANES
    states = delta.shape[1]
    span = rows // SUBS

    x4 = lax.all_to_all(inputs.reshape(ways, rows, narrow), "ch", 0, 0)
    pairs = split_weights((w_value, w_base, w_hidden, w_up, w_down))

    def grouped(table):
        return jnp.transpose(table.reshape(groups, LANES, states), (0, 2, 1))

    gate = jax.nn.sigmoid(delta)
    decay = jax.nn.sigmoid(alpha)
    keep = 1.0 - gate * decay
    root = math.sqrt(states)
    keep4 = grouped(keep)
    coef4 = grouped(gate * beta * (eta / root))
    log_keep = jnp.log(keep4)
    chunk_keep = jnp.exp(span * log_keep)
    device_keep = jnp.exp(rows * log_keep)
    gain4 = norm_gain.reshape(groups, 1, LANES)
    omega4 = omega.reshape(groups, 1, LANES)
    place_info = place.reshape(1)

    ends_shape = jax.ShapeDtypeStruct((groups, states * SUBS, LANES), F32)
    final_shape = jax.ShapeDtypeStruct((groups, states, LANES), F32)
    big = jax.ShapeDtypeStruct((groups, rows, LANES), F32)
    normed4, ends, final = pl.pallas_call(
        norm_kernel,
        in_specs=[VMEM] * 4,
        out_specs=[VMEM] * 3,
        out_shape=[big, ends_shape, final_shape],
        compiler_params=params(24),
        name="norm",
    )(x4, gain4, keep4, chunk_keep)
    finals = lax.all_gather(final, "ch", axis=0)
    total4, starts = pl.pallas_call(
        mix_kernel,
        in_specs=[SMEM] + [VMEM] * 8,
        out_specs=[VMEM] * 2,
        out_shape=[big, ends_shape],
        compiler_params=params(24),
        name="mix",
    )(place_info, normed4, ends, finals, keep4, coef4, chunk_keep, device_keep, omega4)

    info = jnp.stack([place * rows, lengths[0].astype(jnp.int32)])
    output, direct4, halves, ffn_gain_part, qk_part = block_call(
        info,
        key_mask,
        x4,
        normed4,
        total4,
        cotangent.reshape(rows, width),
        qk_scale,
        qk_shift,
        ffn_gain.reshape(1, width),
        pairs,
    )
    n, m, gr, f, a, do, du, dv, bu, bz, br, bh = halves
    up_part = weight_grad(f, du, "up_grad")
    down_part = weight_grad(a, do, "down_grad")
    hidden_part = weight_grad(gr, bh, "hidden_grad")
    plans = orders()
    up_grad, down_grad, hidden_grad = sum_group((up_part, down_part, hidden_part), plans)
    value_part = weight_grad(n, dv, "value_grad")
    base_u = weight_grad(m, bu, "base_update_grad")
    base_z = weight_grad(m, bz, "base_z_grad")
    base_r = weight_grad(m, br, "base_reset_grad")
    base_h = weight_grad(m, bh, "base_hidden_grad")
    last = jnp.concatenate([base_u, base_z, base_h], 1)
    value_grad, reset_grad, rest_grad = sum_group((value_part, base_r, last), plans)
    zwidth = qk_scale.shape[1]
    base_grad = jnp.concatenate(
        [rest_grad[:, : width + zwidth], reset_grad, rest_grad[:, width + zwidth :]], 1
    )

    grad4, part4, omega_part = input_call(
        total4, normed4, omega4, dv, (bu, bz, br, bh), pairs[0], pairs[1]
    )
    back_ends, back_final = pl.pallas_call(
        back_ends_kernel,
        in_specs=[VMEM] * 3,
        out_specs=[VMEM] * 2,
        out_shape=[ends_shape, final_shape],
        compiler_params=params(24),
        name="back_ends",
    )(grad4, keep4, chunk_keep)
    back_finals = lax.all_gather(back_final, "ch", axis=0)
    row_shape = jax.ShapeDtypeStruct((groups, 1, LANES), F32)
    back4, coef_part, keep_part, gain_part = pl.pallas_call(
        back_kernel,
        in_specs=[SMEM] + [VMEM] * 13,
        out_specs=[VMEM] * 4,
        out_shape=[big, final_shape, final_shape, row_shape],
        scratch_shapes=[
            pltpu.VMEM((groups, rows, LANES), F32),
            pltpu.VMEM((states * SUBS, LANES), F32),
        ],
        compiler_params=params(40),
        name="back",
    )(
        place_info,
        grad4,
        back_ends,
        back_finals,
        starts,
        normed4,
        x4,
        direct4,
        part4,
        keep4,
        coef4,
        chunk_keep,
        device_keep,
        gain4,
    )
    input_grad = lax.all_to_all(back4, "ch", 0, 0).reshape(inputs.shape)

    def flat(value):
        return value.reshape(-1, LANES)

    smalls = [coef_part, keep_part, gain_part, omega_part, ffn_gain_part, qk_part]
    counts = [flat(s).shape[0] for s in smalls]
    packed = sum_small(jnp.concatenate([flat(s) for s in smalls], 0))
    pieces = []
    at = 0
    for count in counts:
        pieces.append(packed[at : at + count])
        at += count

    def ungrouped(piece):
        return jnp.transpose(piece.reshape(groups, states, LANES), (0, 2, 1)).reshape(width, states)

    coef_grad, keep_grad = ungrouped(pieces[0]), ungrouped(pieces[1])
    gate_grad = coef_grad * beta * (eta / root) - keep_grad_scaled(keep_grad, gate, beta, eta, root) * decay
    delta_grad = gate_grad * gate * (1.0 - gate)
    alpha_grad = (
        -keep_grad_scaled(keep_grad, gate, beta, eta, root) * gate * decay * (1.0 - decay)
    )
    beta_grad = coef_grad * gate * (eta / root)
    eta_grad = coef_grad * gate * beta / root
    qk = pieces[5].reshape(8, zwidth)
    return (
        output.reshape(cotangent.shape),
        input_grad,
        pieces[2].reshape(width),
        delta_grad,
        alpha_grad,
        beta_grad,
        eta_grad,
        pieces[3].reshape(width),
        value_grad,
        base_grad,
        qk[0:2],
        qk[2:4],
        hidden_grad,
        pieces[4].reshape(width),
        up_grad,
        down_grad,
    )


def keep_grad_scaled(keep_grad, gate, beta, eta, root):
    return keep_grad * gate * beta * (eta / root)


def solution(mesh):
    whole = P()
    placed = (
        (P("seq", None, "ch"), P("seq", "ch", None))
        + (whole,) * 14
        + (P("seq"), P("seq", None))
    )
    return jax.shard_map(
        local,
        mesh=mesh,
        in_specs=placed,
        out_specs=(P("seq", "ch", None), P("seq", None, "ch")) + (whole,) * 14,
        check_vma=False,
    )
```

```python
import math

import jax
import jax.numpy as jnp
from jax import lax
from jax.experimental import pallas as pl
from jax.experimental.pallas import tpu as pltpu
from jax.sharding import PartitionSpec as P

EPS = 1e-05
CENTER = math.sqrt(0.5)
SPREAD = math.sqrt(0.25 / math.pi)
F32 = jnp.float32
BF16 = jnp.bfloat16
NN = ((1,), (0,))
NT = ((1,), (1,))
TN = ((0,), (0,))
LANES = 128
SUBS = 8
TILE = 256
SMALL = 32
NORM_MIB = 24
FORWARD_MIB = 46
BACKWARD_MIB = 46
VMEM = pl.BlockSpec(memory_space=pltpu.VMEM)
SMEM = pl.BlockSpec(memory_space=pltpu.SMEM)
HBM = pl.BlockSpec(memory_space=pltpu.HBM)


def params(mib):
    return pltpu.CompilerParams(vmem_limit_bytes=mib << 20)


def ordered_call(kernel, tokens, *, in_specs, prefetch=0, grid=None, out_specs, scratch_shapes=(), **rest):
    count, extra = prefetch + len(in_specs), len(tokens)

    def body(*refs):
        kernel(*refs[:count], *refs[count + extra :])

    spec = pltpu.PrefetchScalarGridSpec(
        num_scalar_prefetch=prefetch,
        grid=grid or (1,),
        in_specs=list(in_specs) + [VMEM] * extra,
        out_specs=out_specs,
        scratch_shapes=scratch_shapes,
    )
    run = pl.pallas_call(body, grid_spec=spec, **rest)
    return lambda *args: run(*args, *tokens)


def shape_of(*shape, dtype=F32):
    return jax.ShapeDtypeStruct(shape, dtype)


def split(value):
    high = value.astype(BF16)
    return high, (value - high.astype(F32)).astype(BF16)


def dot(left, right, dims):
    return lax.dot_general(left, right, (dims, ((), ())), preferred_element_type=F32)


def mm3(left, right, dims):
    return (
        dot(left[0], right[0], dims)
        + dot(left[1], right[0], dims)
        + dot(left[0], right[1], dims)
    )


def mm3_short(left, right, dims):
    (left_axis,), (right_axis,) = dims
    return dot(
        jnp.concatenate([left[0], left[1], left[0]], left_axis),
        jnp.concatenate([right[0], right[0], right[1]], right_axis),
        dims,
    )


def sigmoid(value):
    return 0.5 * jnp.tanh(0.5 * value) + 0.5


def rows_sum(value):
    return jnp.sum(value, -1, keepdims=True)


def split_kernel(*refs):
    count = len(refs) // 3
    for index in range(count):
        high, low = split(refs[index][...])
        refs[count + 2 * index][...] = high
        refs[count + 2 * index + 1][...] = low


def split_weights(weights, steps=8):
    def spec(weight):
        return pl.BlockSpec((weight.shape[0] // steps, weight.shape[1]), lambda i: (i, 0))

    out = pl.pallas_call(
        split_kernel,
        grid=(steps,),
        in_specs=[spec(w) for w in weights],
        out_specs=[spec(w) for w in weights for _ in range(2)],
        out_shape=[jax.ShapeDtypeStruct(w.shape, BF16) for w in weights for _ in range(2)],
        compiler_params=params(SMALL),
        cost_estimate=pl.CostEstimate(
            flops=4 * sum(w.size for w in weights),
            bytes_accessed=8 * sum(w.size for w in weights),
            transcendentals=0,
        ),
        name="split_weights",
    )(*weights)
    return [(out[2 * i], out[2 * i + 1]) for i in range(len(weights))]


def turned(value):
    return jnp.transpose(value, (1, 0, 2))


def take_steps(ref, g, span, t):
    rows = jnp.stack([ref[g, pl.ds(c * span + t, SUBS), :] for c in range(SUBS)])
    rows = turned(rows)
    return [rows[i] for i in range(SUBS)]


def put_steps(ref, g, span, t, values):
    rows = turned(jnp.stack(values))
    for c in range(SUBS):
        ref[g, pl.ds(c * span + t, SUBS), :] = rows[c]


def rows_of(ref, g, these):
    return [jnp.broadcast_to(ref[g, n : n + 1, :], (SUBS, LANES)) for n in these]


def tree_sum(parts):
    while len(parts) > 1:
        parts = [sum(parts[i : i + 2]) for i in range(0, len(parts), 2)]
    return parts[0]


def scan_ends(source_ref, g, keep_ref, states, span, reverse):
    keeps = rows_of(keep_ref, g, range(states))

    def steps(i, state):
        t = pl.multiple_of((span // SUBS - 1 - i if reverse else i) * SUBS, SUBS)
        fresh = take_steps(source_ref, g, span, t)
        for value in reversed(fresh) if reverse else fresh:
            state = tuple(k * s + value for k, s in zip(keeps, state))
        return state

    zero = jnp.zeros((SUBS, LANES), F32)
    return lax.fori_loop(0, span // SUBS, steps, (zero,) * states, unroll=2)


def fold_ends(ends_ref, group, chunk_keep, states, order):
    total = jnp.zeros((states, LANES), F32)
    for chunk in order:
        total = chunk_keep * total + ends_ref[group, pl.ds(chunk, states, stride=SUBS), :]
    return total


def norm_kernel(x_ref, gain_ref, keep_ref, chunk_keep_ref, normed_ref, ends_ref, final_ref):
    groups, rows, _ = x_ref.shape
    states = keep_ref.shape[1]
    span = rows // SUBS
    width = groups * LANES

    def normalise(i, carry):
        here = pl.ds(pl.multiple_of(i * LANES, LANES), LANES)
        pieces = [x_ref[g, here, :] for g in range(groups)]
        mean = rows_sum(sum(pieces)) / width
        square = rows_sum(sum(p * p for p in pieces)) / width
        scale = lax.rsqrt(square - mean * mean + EPS)
        for g in range(groups):
            normed_ref[g, here, :] = (pieces[g] - mean) * scale * gain_ref[g]
        return carry

    lax.fori_loop(0, rows // LANES, normalise, 0)
    for g in range(groups):
        ends = scan_ends(normed_ref, g, keep_ref, states, span, False)
        for n in range(states):
            ends_ref[g, n * SUBS : (n + 1) * SUBS, :] = ends[n]
        final_ref[g] = fold_ends(ends_ref, g, chunk_keep_ref[g], states, range(SUBS))


def mix_kernel(
    place_ref,
    normed_ref,
    ends_ref,
    finals_ref,
    keep_ref,
    coef_ref,
    chunk_keep_ref,
    device_keep_ref,
    omega_ref,
    total_ref,
    start_ref,
):
    groups, rows, _ = normed_ref.shape
    states = keep_ref.shape[1]
    span = rows // SUBS
    ways = finals_ref.shape[0]
    place = place_ref[0]
    for g in range(groups):
        state = jnp.zeros((states, LANES), F32)
        for d in range(ways):
            state = jnp.where(d < place, device_keep_ref[g] * state + finals_ref[d, g], state)
        for chunk in range(SUBS):
            start_ref[g, pl.ds(chunk, states, stride=SUBS), :] = state
            state = chunk_keep_ref[g] * state + ends_ref[g, pl.ds(chunk, states, stride=SUBS), :]
        keeps = rows_of(keep_ref, g, range(states))
        coefs = rows_of(coef_ref, g, range(states))
        omega = jnp.broadcast_to(omega_ref[g], (SUBS, LANES))

        def steps(i, state):
            t = pl.multiple_of(i * SUBS, SUBS)
            totals = []
            for fresh in take_steps(normed_ref, g, span, t):
                state = tuple(k * s + fresh for k, s in zip(keeps, state))
                totals.append(tree_sum([c * s for c, s in zip(coefs, state)] + [omega * fresh]))
            put_steps(total_ref, g, span, t, totals)
            return state

        first = tuple(start_ref[g, n * SUBS : (n + 1) * SUBS, :] for n in range(states))
        lax.fori_loop(0, span // SUBS, steps, first, unroll=2)


def back_ends_kernel(grad_ref, keep_ref, chunk_keep_ref, ends_ref, final_ref):
    _, rows, _ = grad_ref.shape
    states = keep_ref.shape[1]
    span = rows // SUBS
    for g in range(1):
        ends = scan_ends(grad_ref, g, keep_ref, states, span, True)
        for n in range(states):
            ends_ref[g, n * SUBS : (n + 1) * SUBS, :] = ends[n]
        final_ref[g] = fold_ends(ends_ref, g, chunk_keep_ref[g], states, reversed(range(SUBS)))


def back_kernel(
    place_ref,
    grad_ref,
    ends_ref,
    finals_ref,
    start_ref,
    normed_ref,
    part_ref,
    keep_ref,
    coef_ref,
    chunk_keep_ref,
    device_keep_ref,
    sum_ref,
    coef_grad_ref,
    keep_grad_ref,
    init_ref,
):
    _, rows, _ = grad_ref.shape
    states = keep_ref.shape[1]
    span = rows // SUBS
    ways = finals_ref.shape[0]
    place = place_ref[0]
    half = states // 2
    zero = jnp.zeros((SUBS, LANES), F32)
    for g in range(1):
        whole_g = 0
        state = jnp.zeros((states, LANES), F32)
        for d in reversed(range(ways)):
            state = jnp.where(
                d > place, device_keep_ref[whole_g] * state + finals_ref[d, whole_g], state
            )
        for chunk in reversed(range(SUBS)):
            init_ref[pl.ds(chunk, states, stride=SUBS), :] = state
            state = (
                chunk_keep_ref[whole_g] * state
                + ends_ref[whole_g, pl.ds(chunk, states, stride=SUBS), :]
            )
        for part in range(2):
            these = range(part * half, (part + 1) * half)
            keeps = rows_of(keep_ref, whole_g, these)
            coefs = rows_of(coef_ref, whole_g, these)

            def steps(i, carry):
                lam, second, coef_acc, keep_acc = carry
                t = pl.multiple_of((span // SUBS - 1 - i) * SUBS, SUBS)
                fresh = take_steps(grad_ref, g, span, t)
                source = take_steps(normed_ref, g, span, t)
                outs = [None] * SUBS
                for j in reversed(range(SUBS)):
                    keep_acc = tuple(a + v * source[j] for a, v in zip(keep_acc, second))
                    lam = tuple(k * l + fresh[j] for k, l in zip(keeps, lam))
                    coef_acc = tuple(a + l * source[j] for a, l in zip(coef_acc, lam))
                    second = tuple(l + k * v for l, k, v in zip(lam, keeps, second))
                    outs[j] = tree_sum([c * l for c, l in zip(coefs, lam)])
                rows = turned(jnp.stack(outs))
                before = part_ref if part == 0 else sum_ref
                for c in range(SUBS):
                    here = pl.ds(c * span + t, SUBS)
                    sum_ref[g, here, :] = before[g, here, :] + rows[c]
                return lam, second, coef_acc, keep_acc

            first = tuple(init_ref[n * SUBS : (n + 1) * SUBS, :] for n in these)
            nothing = (zero,) * half
            lam, second, coef_acc, keep_acc = lax.fori_loop(
                0, span // SUBS, steps, (first, nothing, nothing, nothing)
            )
            for j, n in enumerate(these):
                start = start_ref[whole_g, n * SUBS : (n + 1) * SUBS, :]
                keep_acc_n = keep_acc[j] + start * second[j]
                coef_grad_ref[g, n : n + 1, :] = jnp.sum(coef_acc[j], 0, keepdims=True)
                keep_grad_ref[g, n : n + 1, :] = jnp.sum(keep_acc_n, 0, keepdims=True)


def unnorm_kernel(
    x_ref,
    sum_a,
    sum_b,
    direct_ref,
    gain_ref,
    coef_a,
    coef_b,
    keep_a,
    keep_b,
    omega_ref,
    ffn_ref,
    qk_ref,
    out_ref,
    small_ref,
    gain_grad,
):
    groups, rows, _ = x_ref.shape
    width = groups * LANES
    share = sum_a.shape[0]
    tile = pl.program_id(0)

    @pl.when(tile == 0)
    def _():
        gain_grad[...] = jnp.zeros_like(gain_grad)

    pieces = [x_ref[g] for g in range(groups)]
    mean = rows_sum(sum(pieces)) / width
    square = rows_sum(sum(p * p for p in pieces)) / width
    scale = lax.rsqrt(square - mean * mean + EPS)
    centered = [(p - mean) * scale for p in pieces]
    grads = [(sum_a, sum_b)[g // share][g % share] for g in range(groups)]
    for g in range(groups):
        gain_grad[g : g + 1, :] += jnp.sum(grads[g] * centered[g], 0, keepdims=True)
    scaled = [grads[g] * gain_ref[g] for g in range(groups)]
    plain = rows_sum(sum(scaled)) / width
    cross = rows_sum(sum(s * c for s, c in zip(scaled, centered))) / width
    for g in range(groups):
        out_ref[g] = direct_ref[g] + scale * (scaled[g] - plain - centered[g] * cross)

    @pl.when(tile == pl.num_programs(0) - 1)
    def _():
        states = coef_a.shape[1]
        for i, refs in enumerate(((coef_a, coef_b), (keep_a, keep_b))):
            for g in range(groups):
                at = slice(g * states, (g + 1) * states)
                small_ref[at, i * LANES : (i + 1) * LANES] = refs[g // share][g % share]
        at = groups * states
        small_ref[at:, :] = jnp.zeros((small_ref.shape[0] - at, 2 * LANES), F32)
        small_ref[at : at + groups, :LANES] = gain_grad[:groups]
        for g in range(groups):
            here = slice(at + groups + g, at + groups + g + 1)
            small_ref[here, :LANES] = omega_ref[g]
            small_ref[here, LANES:] = ffn_ref[:, g * LANES : (g + 1) * LANES]
        small_ref[at : at + 4, LANES:] = qk_ref[0:4, :]


def group_spec(array, lowest=0):
    axis = array.ndim - 3
    block = array.shape[:axis] + (1,) + array.shape[axis + 1 :]
    return pl.BlockSpec(block, lambda g: (0,) * axis + (lowest + g, 0, 0))


def scan_call(kernel, name, scalars, arrays, outs, tokens=(), lowest=0, count=None, scratch=(), work=4):
    count = count or arrays[0].shape[-3]
    states, rows = outs[-1].shape[-2], arrays[0].shape[-2]
    return ordered_call(
        kernel,
        tokens,
        grid=(count,),
        in_specs=[SMEM] * len(scalars) + [group_spec(v, lowest) for v in arrays],
        out_specs=[group_spec(v) for v in outs],
        scratch_shapes=scratch,
        out_shape=outs,
        compiler_params=params(SMALL),
        cost_estimate=pl.CostEstimate(
            flops=work * rows * count * LANES * 16,
            bytes_accessed=12 * rows * count * LANES,
            transcendentals=0,
        ),
        name=name,
    )(*scalars, *arrays)


def back_call(lowest, count, place_info, grad4, ends, finals, starts, normed4, part4, tables, tokens):
    rows, states = grad4.shape[1], starts.shape[1] // SUBS
    arrays = [grad4, ends, finals, starts, normed4, part4, *tables]
    outs = [shape_of(count, rows, LANES)] + [shape_of(count, states, LANES)] * 2
    return scan_call(
        back_kernel,
        "back",
        [place_info],
        arrays,
        outs,
        tokens,
        lowest,
        count,
        [pltpu.VMEM((states * SUBS, LANES), F32)],
        10,
    )


def unnorm_call(x4, sums, direct4, gain4, coefs, keeps, omega, ffn, qk, tokens):
    groups, rows, _ = x4.shape
    states = coefs[0].shape[1]
    by_group = pl.BlockSpec((groups, TILE, LANES), lambda i: (0, i, 0))
    halves = [pl.BlockSpec((s.shape[0], TILE, LANES), lambda i: (0, i, 0)) for s in sums]
    height = -(-(groups * states + 2 * groups) // 16) * 16
    return ordered_call(
        unnorm_kernel,
        tokens,
        grid=(rows // TILE,),
        in_specs=[by_group] + halves + [by_group] + [VMEM] * 8,
        out_specs=[by_group, pl.BlockSpec((height, 2 * LANES), lambda i: (0, 0))],
        out_shape=[shape_of(*x4.shape), shape_of(height, 2 * LANES)],
        scratch_shapes=[pltpu.VMEM((SUBS, LANES), F32)],
        compiler_params=params(SMALL),
        cost_estimate=pl.CostEstimate(
            flops=20 * x4.size, bytes_accessed=16 * x4.size, transcendentals=0
        ),
        name="unnorm",
    )(x4, *sums, direct4, gain4, *coefs, *keeps, omega, ffn, qk)


def small_kernel(
    part_a,
    part_b,
    part_c,
    part_d,
    gate_ref,
    decay_ref,
    beta_ref,
    eta_ref,
    gain_out,
    delta_out,
    alpha_out,
    beta_out,
    eta_out,
    omega_out,
    ffn_out,
    scale_out,
    shift_out,
):
    groups, states, _ = gate_ref.shape
    root = math.sqrt(states)
    at = groups * states
    height = -(-(groups * states + 2 * groups) // 16) * 16
    tails = [ref[ref.shape[0] - height :, :] for ref in (part_a, part_b, part_c, part_d)]
    total = (tails[0] + tails[1]) + (tails[2] + tails[3])
    for g in range(groups):
        here = slice(g * states, (g + 1) * states)
        coef, keep = total[here, :LANES], total[here, LANES:]
        gate, decay, beta, eta = gate_ref[g], decay_ref[g], beta_ref[g], eta_ref[g]
        keep = keep * gate * beta * (eta / root)
        gate_grad = coef * beta * (eta / root) - keep * decay
        lanes = slice(g * LANES, (g + 1) * LANES)
        delta_out[:, lanes] = gate_grad * gate * (1.0 - gate)
        alpha_out[:, lanes] = -keep * gate * decay * (1.0 - decay)
        beta_out[:, lanes] = coef * gate * (eta / root)
        eta_out[:, lanes] = coef * gate * beta / root
    gain_out[...] = total[at : at + groups, :LANES]
    omega_out[...] = total[at + groups : at + 2 * groups, :LANES]
    ffn_out[...] = total[at + groups : at + 2 * groups, LANES:]
    scale_out[...] = total[at : at + 2, LANES:]
    shift_out[...] = total[at + 2 : at + 4, LANES:]


def small_call(parts, tables):
    groups, states, _ = tables[0].shape
    row, table = shape_of(groups, LANES), shape_of(states, groups * LANES)
    two = shape_of(2, LANES)
    return pl.pallas_call(
        small_kernel,
        in_specs=[VMEM] * 8,
        out_specs=[VMEM] * 9,
        out_shape=[row, table, table, table, table, row, row, two, two],
        compiler_params=params(SMALL),
        name="small_grads",
    )(*parts, *tables)


QUARTER = 256
EVERY = slice(None)


def columns(total, step=512):
    return [slice(i, min(i + step, total)) for i in range(0, total, step)]


def joined(ref):
    return jnp.concatenate([ref[g] for g in range(ref.shape[0])], 1)


def silu_slope(act, gate):
    return gate + act * (1.0 - gate)


class Attention:
    def __init__(self, z, scale_ref, shift_ref, mask_ref, base_row, length):
        rows, span = z.shape[0], mask_ref.shape[1]
        blocks = rows // span
        self.query = split(z * scale_ref[0:1, :] + shift_ref[0:1, :])
        self.key = split(z * scale_ref[1:2, :] + shift_ref[1:2, :])
        lane = lax.broadcasted_iota(jnp.int32, (1, span), 1)
        valids, counts = [], []
        for b in range(blocks):
            position = base_row + b * span + lane
            last_block = (base_row + b * span) // span == (length - 1) // span
            kept = (position < length) & (jnp.logical_not(last_block) | (mask_ref[...] == 1))
            valid = jnp.where(kept, 1.0, 0.0)
            count = jnp.maximum(rows_sum(valid), 1.0)
            valids.append(valid)
            counts.append(jnp.broadcast_to(count, (1, span)))
        row = lax.broadcasted_iota(jnp.int32, (rows, rows), 0)
        column = lax.broadcasted_iota(jnp.int32, (rows, rows), 1)
        near = (row >= column) & (row // span == column // span)
        self.mask = jnp.where(near, jnp.concatenate(valids, 1), 0.0)
        self.count = jnp.concatenate(counts, 1)
        self.spot = mm3_short(self.query, self.key, NT) / self.count - CENTER

    def weight(self):
        curve = lax.erf(self.spot * (1.0 / (SPREAD * math.sqrt(2.0))))
        return split((0.5 + 0.5 * curve) * self.mask)

    def slope(self):
        return (
            jnp.exp(self.spot * self.spot * (-1.0 / (2.0 * SPREAD * SPREAD)))
            * (self.mask / self.count)
            * (1.0 / (SPREAD * math.sqrt(2.0 * math.pi)))
        )


def add_to(total_ref, quarter, at, pieces, first):
    for piece in pieces:
        here = slice(at, at + piece.shape[0])
        at += piece.shape[0]
        total_ref[quarter, here, :] = jnp.where(first, 0.0, total_ref[quarter, here, :]) + piece
    return at


def packed_rows(value):
    return [value[:, i : i + QUARTER] for i in range(0, value.shape[1], QUARTER)]


class HandOut:
    def __init__(self, own, total, send, keep, sems, last):
        self.own, self.total, self.send, self.keep = own, total, send, keep
        self.sems, self.last = sems, last

    def each(self, quarter, act):
        apart = quarter ^ self.own

        @pl.when(self.last & (apart >= 2))
        def _():
            act(
                pltpu.make_async_copy(
                    self.total.at[quarter], self.send.at[3 - apart], self.sems.at[quarter]
                )
            )

        @pl.when(self.last & (apart < 2))
        def _():
            act(
                pltpu.make_async_copy(
                    self.total.at[quarter], self.keep.at[1 - apart], self.sems.at[quarter]
                )
            )

    def start(self, quarter):
        self.each(quarter, lambda copy: copy.start())

    def wait(self):
        for quarter in range(4):
            self.each(quarter, lambda copy: copy.wait())


def forward_kernel(
    info_ref,
    place_ref,
    mask_ref,
    x_ref,
    normed_ref,
    total_ref,
    cot_ref,
    scale_ref,
    shift_ref,
    gain_ref,
    wv_h,
    wv_l,
    wb_h,
    wb_l,
    wh_h,
    wh_l,
    wu_h,
    wu_l,
    wd_h,
    wd_l,
    out_ref,
    direct_ref,
    vpre,
    rpre,
    zpre,
    grad_u_ref,
    grad_h_ref,
    gain_grad_ref,
    send_a,
    keep_a,
    send_b,
    keep_b,
    v_h,
    v_l,
    upd,
    hpre,
    gr_h,
    gr_l,
    a_h,
    a_l,
    usil,
    du_h,
    du_l,
    acc_a,
    acc_b,
    sems_a,
    sems_b,
):
    tile = pl.program_id(0)
    first = tile == 0
    groups, rows, _ = x_ref.shape
    width = groups * LANES
    zwidth = scale_ref.shape[1]
    values = wv_h.shape[1]
    units = wu_h.shape[1]
    base_row, length = info_ref[0] + tile * rows, info_ref[1]
    last = tile == pl.num_programs(0) - 1
    out_a = HandOut(place_ref[0], acc_a, send_a, keep_a, sems_a, last)
    out_b = HandOut(place_ref[1], acc_b, send_b, keep_b, sems_b, last)

    @pl.when(first)
    def _():
        gain_grad_ref[...] = jnp.zeros_like(gain_grad_ref)

    def put(high_ref, low_ref, where, value):
        high, low = split(value)
        high_ref[where] = high
        low_ref[where] = low
        return high, low

    n_pair = split(joined(normed_ref))
    total = joined(total_ref)
    m_pair = split(total * sigmoid(total))
    for c in columns(values):
        pre = mm3(n_pair, (wv_h[:, c], wv_l[:, c]), NN)
        vpre[:, c] = pre
        put(v_h, v_l, (EVERY, c), pre * sigmoid(pre))
    c = slice(width, width + zwidth)
    pre = mm3(m_pair, (wb_h[:, c], wb_l[:, c]), NN)
    zpre[...] = pre
    attention = Attention(
        pre * sigmoid(pre), scale_ref, shift_ref, mask_ref, base_row, length
    )
    c = slice(0, width)
    upd[...] = sigmoid(mm3(m_pair, (wb_h[:, c], wb_l[:, c]), NN))
    for c in columns(values):
        w = slice(width + zwidth + c.start, width + zwidth + c.stop)
        rpre[:, c] = mm3(m_pair, (wb_h[:, w], wb_l[:, w]), NN)
    w = slice(width + zwidth + values, width + zwidth + values + width)
    hpre[...] = mm3(m_pair, (wb_h[:, w], wb_l[:, w]), NN)
    weight = attention.weight()
    for c in columns(values):
        got = mm3(weight, (v_h[:, c], v_l[:, c]), NN)
        pre = rpre[:, c]
        put(gr_h, gr_l, (EVERY, c), got * (pre * sigmoid(pre)))
    pre = hpre[...] + mm3((gr_h[...], gr_l[...]), (wh_h[...], wh_l[...]), NN)
    s = sigmoid(pre)
    hidden = pre * s
    hpre[...] = silu_slope(hidden, s)
    x = joined(x_ref)
    update = upd[...]
    apart = hidden - x
    gated = x + update * apart
    mean = rows_sum(gated) / width
    square = rows_sum(gated * gated) / width
    scale = lax.rsqrt(square - mean * mean + EPS)
    centered = (gated - mean) * scale
    f_pair = split(centered * gain_ref[...])
    for c in columns(units):
        pre = mm3(f_pair, (wu_h[:, c], wu_l[:, c]), NN)
        s = sigmoid(pre)
        act = pre * s
        put(a_h, a_l, (EVERY, c), act)
        usil[:, c] = silu_slope(act, s)
    live = (base_row + lax.broadcasted_iota(jnp.int32, (rows, 1), 0) < length).astype(F32)
    out_ref[...] = (gated + mm3((a_h[...], a_l[...]), (wd_h[...], wd_l[...]), NN)) * live

    grad_out = cot_ref[...] * live
    do_pair = split(grad_out)
    for c in columns(units):
        put(du_h, du_l, (EVERY, c), mm3(do_pair, (wd_h[c, :], wd_l[c, :]), NT) * usil[:, c])
    grad_f = mm3((du_h[...], du_l[...]), (wu_h[...], wu_l[...]), NT)
    gain_grad_ref[...] += jnp.sum(grad_f * centered, 0, keepdims=True)
    scaled = grad_f * gain_ref[...]
    grad_gated = grad_out + scale * (
        scaled - rows_sum(scaled) / width - centered * (rows_sum(scaled * centered) / width)
    )
    grad_u_ref[...] = grad_gated * apart * update * (1.0 - update)
    grad_h = grad_gated * update * hpre[...]
    grad_h_ref[...] = grad_h
    h_pair = split(grad_h)
    direct = grad_gated * (1.0 - update)
    for g in range(groups):
        direct_ref[g] = direct[:, g * LANES : (g + 1) * LANES]
    for q in range(4):
        c = slice(q * QUARTER, (q + 1) * QUARTER)
        at_a = add_to(acc_a, q, 0, [mm3(f_pair, (du_h[:, c], du_l[:, c]), TN)], first)
        at_b = add_to(acc_b, q, 0, packed_rows(mm3((a_h[:, c], a_l[:, c]), do_pair, TN)), first)
        packed = packed_rows(mm3((gr_h[:, c], gr_l[:, c]), h_pair, TN))
        add_to(acc_a, q, at_a, packed[: len(packed) // 2], first)
        add_to(acc_b, q, at_b, packed[len(packed) // 2 :], first)
        out_a.start(q)
        out_b.start(q)
    out_a.wait()
    out_b.wait()


def backward_kernel(
    info_ref,
    place_ref,
    mask_ref,
    normed_ref,
    total_ref,
    vpre,
    rpre,
    zpre,
    grad_u_ref,
    grad_h_ref,
    scale_ref,
    shift_ref,
    omega_ref,
    wv_h,
    wv_l,
    wb_h,
    wb_l,
    wh_h,
    wh_l,
    grad_ref,
    part_ref,
    qk_grad_ref,
    omega_grad_ref,
    send_b,
    keep_b,
    send_c,
    keep_c,
    v_h,
    v_l,
    vsil,
    rst,
    att,
    da_h,
    da_l,
    dv_h,
    dv_l,
    bz_h,
    bz_l,
    br_h,
    br_l,
    acc_b,
    acc_c,
    sems_b,
    sems_c,
):
    tile = pl.program_id(0)
    first = tile == 0
    groups, rows, _ = normed_ref.shape
    width = groups * LANES
    zwidth = scale_ref.shape[1]
    values = wv_h.shape[1]
    base_row, length = info_ref[0] + tile * rows, info_ref[1]
    last = tile == pl.num_programs(0) - 1
    out_b = HandOut(place_ref[0], acc_b, send_b, keep_b, sems_b, last)
    out_c = HandOut(place_ref[1], acc_c, send_c, keep_c, sems_c, last)

    @pl.when(first)
    def _():
        qk_grad_ref[...] = jnp.zeros_like(qk_grad_ref)
        omega_grad_ref[...] = jnp.zeros_like(omega_grad_ref)

    def put(high_ref, low_ref, where, value):
        high, low = split(value)
        high_ref[where] = high
        low_ref[where] = low
        return high, low

    for c in columns(values):
        pre = vpre[:, c]
        s = sigmoid(pre)
        act = pre * s
        put(v_h, v_l, (EVERY, c), act)
        vsil[:, c] = silu_slope(act, s)
    pre = zpre[...]
    s = sigmoid(pre)
    z = pre * s
    zsil = silu_slope(z, s)
    attention = Attention(z, scale_ref, shift_ref, mask_ref, base_row, length)
    weight = attention.weight()
    for c in columns(values):
        got = mm3(weight, (v_h[:, c], v_l[:, c]), NN)
        pre = rpre[:, c]
        s = sigmoid(pre)
        act = pre * s
        rst[:, c] = act
        att[:, c] = got * silu_slope(act, s)
    u_pair = split(grad_u_ref[...])
    h_pair = split(grad_h_ref[...])
    for c in columns(values):
        got = mm3(h_pair, (wh_h[c, :], wh_l[c, :]), NT)
        put(da_h, da_l, (EVERY, c), got * rst[:, c])
        put(br_h, br_l, (EVERY, c), got * att[:, c])
    grad_scores = split(
        mm3((da_h[...], da_l[...]), (v_h[...], v_l[...]), NT) * attention.slope()
    )
    for c in columns(values):
        got = mm3(weight, (da_h[:, c], da_l[:, c]), TN)
        put(dv_h, dv_l, (EVERY, c), got * vsil[:, c])
    grad_q = mm3(grad_scores, attention.key, NN)
    grad_k = mm3(grad_scores, attention.query, TN)
    qk_grad_ref[0:1, :] += jnp.sum(grad_q * z, 0, keepdims=True)
    qk_grad_ref[1:2, :] += jnp.sum(grad_k * z, 0, keepdims=True)
    qk_grad_ref[2:3, :] += jnp.sum(grad_q, 0, keepdims=True)
    qk_grad_ref[3:4, :] += jnp.sum(grad_k, 0, keepdims=True)
    put(
        bz_h,
        bz_l,
        (EVERY, EVERY),
        (grad_q * scale_ref[0:1, :] + grad_k * scale_ref[1:2, :]) * zsil,
    )

    n_pair = split(joined(normed_ref))
    total = joined(total_ref)
    gate = sigmoid(total)
    mixed = total * gate
    m_pair = split(mixed)
    for q in range(4):
        c = slice(q * QUARTER, (q + 1) * QUARTER)
        at_b = add_to(acc_b, q, 0, [mm3(n_pair, (dv_h[:, c], dv_l[:, c]), TN)], first)
        w = slice(q * width // 4, (q + 1) * width // 4)
        got = mm3((m_pair[0][:, w], m_pair[1][:, w]), (bz_h[...], bz_l[...]), TN)
        half = got.shape[0] // 2
        at_b = add_to(acc_b, q, at_b, [jnp.concatenate([got[:half], got[half:]], 1)], first)
        at_c = add_to(acc_c, q, 0, [mm3(m_pair, (br_h[:, c], br_l[:, c]), TN)], first)
        side_pair = u_pair if q < 2 else h_pair
        c = slice(q % 2 * QUARTER, (q % 2 + 1) * QUARTER)
        got = mm3(m_pair, (side_pair[0][:, c], side_pair[1][:, c]), TN)
        half = got.shape[0] // 2
        add_to(acc_b, q, at_b, [got[:half]], first)
        add_to(acc_c, q, at_c, [got[half:]], first)
        out_b.start(q)
        out_c.start(q)

    grad_n = mm3((dv_h[...], dv_l[...]), (wv_h[...], wv_l[...]), NT)
    at = [0, width, width + zwidth, width + zwidth + values, 2 * width + zwidth + values]
    w = [slice(i, j) for i, j in zip(at[:-1], at[1:])]
    grad = (
        mm3(u_pair, (wb_h[:, w[0]], wb_l[:, w[0]]), NT)
        + mm3_short((bz_h[...], bz_l[...]), (wb_h[:, w[1]], wb_l[:, w[1]]), NT)
        + mm3((br_h[...], br_l[...]), (wb_h[:, w[2]], wb_l[:, w[2]]), NT)
        + mm3(h_pair, (wb_h[:, w[3]], wb_l[:, w[3]]), NT)
    ) * silu_slope(mixed, gate)
    for g in range(groups):
        lanes = slice(g * LANES, (g + 1) * LANES)
        got = grad[:, lanes]
        grad_ref[g] = got
        part_ref[g] = grad_n[:, lanes] + got * omega_ref[g]
        omega_grad_ref[g] += jnp.sum(got * normed_ref[g], 0, keepdims=True)

    out_b.wait()
    out_c.wait()


def by_row(count):
    return pl.BlockSpec((TILE, count), lambda i: (i, 0))


def forward_call(info, place, key_mask, x4, normed4, total4, cot, qk_scale, qk_shift, ffn_gain, pairs, heights):
    groups, rows, _ = x4.shape
    width = groups * LANES
    wv, wb, wh, wu, wd = pairs
    values, units, zwidth = wv[0].shape[1], wu[0].shape[1], qk_scale.shape[1]
    flat = [part for pair in pairs for part in pair]
    by_group = pl.BlockSpec((groups, TILE, LANES), lambda i: (0, i, 0))
    macs = rows * (wv[0].size + wb[0].size + wh[0].size + 3 * wu[0].size + 3 * wd[0].size)
    return pl.pallas_call(
        forward_kernel,
        grid=(rows // TILE,),
        in_specs=[SMEM, SMEM, VMEM, by_group, by_group, by_group, by_row(width)]
        + [VMEM] * (3 + len(flat)),
        out_specs=[
            by_row(width),
            by_group,
            by_row(values),
            by_row(values),
            by_row(zwidth),
            by_row(width),
            by_row(width),
            pl.BlockSpec((1, width), lambda i: (0, 0)),
            HBM,
            HBM,
            HBM,
            HBM,
        ],
        out_shape=[
            shape_of(rows, width),
            shape_of(groups, rows, LANES),
            shape_of(rows, values),
            shape_of(rows, values),
            shape_of(rows, zwidth),
            shape_of(rows, width),
            shape_of(rows, width),
            shape_of(1, width),
        ]
        + [shape_of(2, height, QUARTER) for height in heights for _ in range(2)],
        scratch_shapes=[
            pltpu.VMEM((TILE, values), BF16),
            pltpu.VMEM((TILE, values), BF16),
            pltpu.VMEM((TILE, width), F32),
            pltpu.VMEM((TILE, width), F32),
            pltpu.VMEM((TILE, values), BF16),
            pltpu.VMEM((TILE, values), BF16),
            pltpu.VMEM((TILE, units), BF16),
            pltpu.VMEM((TILE, units), BF16),
            pltpu.VMEM((TILE, units), F32),
            pltpu.VMEM((TILE, units), BF16),
            pltpu.VMEM((TILE, units), BF16),
        ]
        + [pltpu.VMEM((4, height, QUARTER), F32) for height in heights]
        + [pltpu.SemaphoreType.DMA((4,))] * 2,
        compiler_params=params(FORWARD_MIB),
        cost_estimate=pl.CostEstimate(flops=6 * macs, bytes_accessed=48 << 20, transcendentals=0),
        name="forward",
    )(info, place, key_mask, x4, normed4, total4, cot, qk_scale, qk_shift, ffn_gain, *flat)


def backward_call(
    info, place, key_mask, normed4, total4, saved, qk_scale, qk_shift, omega4, pairs, heights, tokens
):
    groups, rows, _ = normed4.shape
    width = groups * LANES
    wv, wb, wh = pairs[:3]
    values, zwidth = wv[0].shape[1], qk_scale.shape[1]
    flat = [part for pair in pairs[:3] for part in pair]
    by_group = pl.BlockSpec((groups, TILE, LANES), lambda i: (0, i, 0))
    macs = 2 * rows * (wv[0].size + wb[0].size + wh[0].size)
    quarters = [shape_of(2, height, QUARTER) for height in heights for _ in range(2)]
    return ordered_call(
        backward_kernel,
        tokens,
        grid=(rows // TILE,),
        in_specs=[SMEM, SMEM, VMEM, by_group, by_group]
        + [by_row(s.shape[1]) for s in saved]
        + [VMEM] * (3 + len(flat)),
        out_specs=[
            by_group,
            by_group,
            pl.BlockSpec((8, zwidth), lambda i: (0, 0)),
            pl.BlockSpec((groups, 1, LANES), lambda i: (0, 0, 0)),
        ]
        + [HBM] * 4,
        out_shape=[
            shape_of(groups, rows, LANES),
            shape_of(groups, rows, LANES),
            shape_of(8, zwidth),
            shape_of(groups, 1, LANES),
        ]
        + quarters,
        scratch_shapes=[
            pltpu.VMEM((TILE, values), BF16),
            pltpu.VMEM((TILE, values), BF16),
            pltpu.VMEM((TILE, values), F32),
            pltpu.VMEM((TILE, values), F32),
            pltpu.VMEM((TILE, values), F32),
            pltpu.VMEM((TILE, values), BF16),
            pltpu.VMEM((TILE, values), BF16),
            pltpu.VMEM((TILE, values), BF16),
            pltpu.VMEM((TILE, values), BF16),
            pltpu.VMEM((TILE, zwidth), BF16),
            pltpu.VMEM((TILE, zwidth), BF16),
            pltpu.VMEM((TILE, values), BF16),
            pltpu.VMEM((TILE, values), BF16),
        ]
        + [pltpu.VMEM((4, height, QUARTER), F32) for height in heights]
        + [pltpu.SemaphoreType.DMA((4,))] * 2,
        compiler_params=params(BACKWARD_MIB),
        cost_estimate=pl.CostEstimate(flops=6 * macs, bytes_accessed=40 << 20, transcendentals=0),
        name="backward",
    )(info, place, key_mask, normed4, total4, *saved, qk_scale, qk_shift, omega4, *flat)


def swap(value, step):
    axis, distance = step
    size = lax.axis_size(axis)
    return lax.ppermute(value, axis, [(i, i ^ distance) for i in range(size)])


def side(step):
    axis, distance = step
    return (lax.axis_index(axis) // distance) % 2


def device_steps():
    def bits(axis):
        size = lax.axis_size(axis)
        return [(axis, 1 << i) for i in range(size.bit_length() - 1)]

    return bits("ch"), bits("seq")


def orders():
    ch, seq = device_steps()
    x, y, z, rest = ch[1:], seq[:1], seq[1:2], seq[2:]
    out = [y + z + x, z + y + x, x + z + y, y + x + z]
    back = [y + x + z, x + z + y, y + z + x, z + x + y]
    return [(ch[:1] + go + rest, rest[::-1] + come + ch[:1]) for go, come in zip(out, back)]


TOKEN = shape_of(SUBS, LANES)


def gate(value, token):
    return lax.optimization_barrier((value, token))


def halve_kernel(own_ref, keep_ref, got_ref, send_ref, next_ref, token_ref):
    own = own_ref[0]
    send_ref[...] = keep_ref[1 - own] + got_ref[1 - own]
    next_ref[...] = keep_ref[own] + got_ref[own]
    token_ref[...] = jnp.zeros_like(token_ref)


def halve(keep, got, own, tokens):
    rows, width = keep.shape[-2] * (keep.shape[0] if keep.ndim == 3 else 1) // 2, keep.shape[-1]
    keep, got = keep.reshape(2, rows, width), got.reshape(2, rows, width)
    return ordered_call(
        halve_kernel,
        tokens,
        in_specs=[SMEM, VMEM, VMEM],
        out_specs=[VMEM] * 3,
        out_shape=[shape_of(rows, width)] * 2 + [TOKEN],
        compiler_params=params(SMALL),
        cost_estimate=pl.CostEstimate(
            flops=2 * rows * width, bytes_accessed=1 << 10, transcendentals=0
        ),
        name="halve",
    )(own.reshape(1), keep, got)


def add_kernel(left_ref, right_ref, out_ref, token_ref):
    out_ref[...] = left_ref[...] + right_ref[...]
    token_ref[...] = jnp.zeros_like(token_ref)


def add(left, right, tokens):
    return ordered_call(
        add_kernel,
        tokens,
        in_specs=[VMEM] * 2,
        out_specs=[VMEM] * 2,
        out_shape=[shape_of(*left.shape), TOKEN],
        compiler_params=params(SMALL),
        cost_estimate=pl.CostEstimate(flops=left.size, bytes_accessed=1 << 10, transcendentals=0),
        name="add",
    )(left, right)


def gather_kernel(counts, riders, *refs):
    parts, refs = refs[: len(counts)], refs[len(counts) :]
    out_ref, token_ref = refs[-2:]
    at = 0
    for part, rows in zip(parts, counts):
        out_ref[at : at + rows, :] = part[:rows, :]
        at += rows
    if riders:
        tails = [ref[ref.shape[0] - riders :, :] for ref in refs[:-2]]
        out_ref[at:, :] = sum(tails)
    token_ref[...] = jnp.zeros_like(token_ref)


def gather_parts(parts, counts, riders, rider_rows, tokens):
    total, width = sum(counts), parts[0].shape[1]
    shape = shape_of(total + (rider_rows if riders else 0), width)
    return ordered_call(
        lambda *refs: gather_kernel(counts, rider_rows if riders else 0, *refs),
        tokens,
        in_specs=[VMEM] * (len(parts) + len(riders)),
        out_specs=[VMEM] * 2,
        out_shape=[shape, TOKEN],
        compiler_params=params(SMALL),
        cost_estimate=pl.CostEstimate(flops=0, bytes_accessed=1 << 10, transcendentals=0),
        name="gather_parts",
    )(*parts, *riders)


def finish_kernel(plans, maps, outs_count, *refs):
    pieces = len(plans)
    places, refs = refs[:pieces], refs[pieces:]
    quarters, refs = refs[: 4 * pieces], refs[4 * pieces :]
    outs, refs = refs[:outs_count], refs[outs_count:]
    scratch, sems = refs[:pieces], refs[pieces:]
    leave = []
    for p, plan in enumerate(plans):
        place_ref, out_sems = places[p], sems[p]
        bits = place_ref.shape[0] - 1
        blocks = 1 << bits
        rows = scratch[p].shape[1] // blocks
        relative = place_ref[1]
        for bit in range(1, bits):
            relative = relative * 2 + place_ref[1 + bit]
        for i in range(4):
            for r in range(blocks):
                quarter, k = maps[p](i, r)
                target = pl.ds(pl.multiple_of((relative ^ k) * rows, SUBS), rows)
                scratch[p][quarter, target, :] = quarters[4 * p + i][r * rows : (r + 1) * rows, :]
        for i in range(4):
            quarter = place_ref[0] ^ i
            number = 0
            for out, moves in plan:
                for row, count, column, width, out_row, out_column in moves(quarter):
                    copy = pltpu.make_async_copy(
                        scratch[p].at[i, pl.ds(row, count), pl.ds(column, width)],
                        outs[out].at[pl.ds(out_row, count), pl.ds(out_column, width)],
                        out_sems.at[i, number],
                    )
                    copy.start()
                    leave.append(copy)
                    number += 1
    for copy in leave:
        copy.wait()


def aligned(value, step):
    return pl.multiple_of(value, step)


def as_columns(first, rows, out_row, out_column):
    return lambda q: [(first, rows, 0, QUARTER, out_row, aligned(out_column(q), LANES))]


def as_rows(first, rows, start, stop):
    def moves(q):
        return [
            (first + (c - start) // QUARTER * rows, rows, 0, QUARTER, aligned(q * rows, SUBS), c)
            for c in range(start, stop, QUARTER)
        ]

    return moves


def as_halves(first, rows, out_column):
    def moves(q):
        at = q * (2 * rows)
        return [
            (first, rows, 0, LANES, aligned(at, SUBS), out_column),
            (first, rows, LANES, LANES, aligned(at + rows, SUBS), out_column),
        ]

    return moves


def finish(pieces, plans, shapes, name, tokens=()):
    args = [v for piece in pieces for v in piece.pair + list(piece.got)]
    places = [piece.place for piece in pieces]
    scratch = [pltpu.VMEM((4,) + piece.quarter_shape(), F32) for piece in pieces]
    sems = []
    for piece, plan in zip(pieces, plans):
        number = sum(len(moves(0)) for _, moves in plan)
        sems.append(pltpu.SemaphoreType.DMA((4, number)))
    return ordered_call(
        lambda *refs: finish_kernel(plans, [p.quarter_and_block for p in pieces], len(shapes), *refs),
        tokens,
        in_specs=[SMEM] * len(places) + [VMEM] * len(args),
        out_specs=[HBM] * len(shapes),
        out_shape=[shape_of(*shape) for shape in shapes],
        scratch_shapes=scratch + sems,
        compiler_params=params(SMALL),
        cost_estimate=pl.CostEstimate(
            flops=0, bytes_accessed=8 * sum(a.size for a in args), transcendentals=0
        ),
        name=name,
    )(*places, *args)


class Piece:
    def __init__(self, plan, back):
        self.plan, self.back = plan, back
        self.sides = [side(step).astype(jnp.int32) for step in plan]
        first, second = self.sides[0], self.sides[1]

        def quarter(a, b):
            return 2 * a + b

        self.own_quarter = quarter(first, second).reshape(1)
        self.place = jnp.concatenate([self.own_quarter, jnp.stack(self.sides[2:])])

    def quarter_and_block(self, array, row):
        apart = {step: (row >> i) & 1 for i, step in enumerate(self.back[:-2])}
        apart[self.back[-2]] = array % 2
        block = 0
        for step in self.plan[2:]:
            block = 2 * block + apart[step]
        return 2 * (array // 2) + apart[self.plan[1]], block

    def open(self, send, keep):
        self.own = keep
        self.got = swap(send, self.plan[0])
        self.rider = None
        self.at = 1
        self.steps = 2 * len(self.plan)

    def quarter_shape(self):
        return (self.pair[0].shape[0] - (0 if self.rider is None else self.rider.shape[0]), QUARTER)

    def step(self, *tokens):
        last = len(self.plan)
        if self.at < last:
            own = self.sides[self.at] if self.at > 1 else jnp.ones((), jnp.int32)
            send, self.own, token = halve(self.own, self.got, own, tokens)
            self.got = swap(send, self.plan[self.at])
            self.at += 1
            return token
        if self.at == last:
            total, token = add(self.own, self.got, tokens)
            self.parts = [total]
            self.riders = [] if self.rider is None else [self.rider]
        else:
            self.parts.append(self.got)
            if self.rider is not None:
                self.riders = [self.whole, self.got]
        index = self.at - last
        self.at += 1
        if index < last - 1:
            rows = self.parts[0].shape[0]
            counts = [rows << max(i - 1, 0) for i in range(len(self.parts))]
            if len(self.parts) == 1 and not self.riders:
                self.whole = self.parts[0]
            else:
                height = 0 if self.rider is None else self.rider.shape[0]
                self.whole, token = gather_parts(
                    self.parts, counts, self.riders, height, tokens
                )
            self.got = swap(self.whole, self.back[index])
            return token
        self.pair = [self.whole, self.parts[-1]]
        self.got = [swap(v, self.plan[0]) for v in self.pair]
        return tokens[0]


def riders_of(piece):
    return piece.pair + piece.got


def run(token, *pieces):
    tokens = token if isinstance(token, tuple) else (token,)
    for piece in pieces:
        if piece.at < piece.steps:
            tokens = (piece.step(*tokens),)
    return tokens[0]


def local(
    inputs,
    cotangent,
    norm_gain,
    delta,
    alpha,
    beta,
    eta,
    omega,
    w_value,
    w_base,
    qk_scale,
    qk_shift,
    w_hidden,
    ffn_gain,
    w_up,
    w_down,
    lengths,
    key_mask,
):
    ways = lax.axis_size("ch")
    place = lax.axis_index("ch").astype(jnp.int32)
    _, length, narrow = inputs.shape
    rows = length // ways
    width = narrow * ways
    groups = width // LANES
    states = delta.shape[1]
    span = rows // SUBS

    x4 = lax.all_to_all(inputs.reshape(ways, rows, narrow), "ch", 0, 0)
    pairs = split_weights((w_value, w_base, w_hidden, w_up, w_down))

    def grouped(table):
        return jnp.transpose(table.reshape(groups, LANES, states), (0, 2, 1))

    gates = jax.nn.sigmoid(delta)
    decay = jax.nn.sigmoid(alpha)
    keep = 1.0 - gates * decay
    root = math.sqrt(states)
    keep4 = grouped(keep)
    coef4 = grouped(gates * beta * (eta / root))
    log_keep = jnp.log(keep4)
    chunk_keep = jnp.exp(span * log_keep)
    device_keep = jnp.exp(rows * log_keep)
    gain4 = norm_gain.reshape(groups, 1, LANES)
    omega4 = omega.reshape(groups, 1, LANES)
    place_info = place.reshape(1)

    ends_shape = jax.ShapeDtypeStruct((groups, states * SUBS, LANES), F32)
    final_shape = jax.ShapeDtypeStruct((groups, states, LANES), F32)
    big = jax.ShapeDtypeStruct((groups, rows, LANES), F32)
    normed4, ends, final = pl.pallas_call(
        norm_kernel,
        in_specs=[VMEM] * 4,
        out_specs=[VMEM] * 3,
        out_shape=[big, ends_shape, final_shape],
        compiler_params=params(NORM_MIB),
        name="norm",
    )(x4, gain4, keep4, chunk_keep)
    finals = lax.all_gather(final, "ch", axis=0)
    total4, starts = pl.pallas_call(
        mix_kernel,
        in_specs=[SMEM] + [VMEM] * 8,
        out_specs=[VMEM] * 2,
        out_shape=[big, ends_shape],
        compiler_params=params(NORM_MIB),
        name="mix",
    )(place_info, normed4, ends, finals, keep4, coef4, chunk_keep, device_keep, omega4)

    info = jnp.stack([place * rows, lengths[0].astype(jnp.int32)])
    zwidth = qk_scale.shape[1]
    plans = orders()
    unit = SUBS << (len(plans[0][0]) - 2)
    one, other, two, three = [Piece(*plan) for plan in plans]

    def height(*counts):
        return -(-sum(counts) // QUARTER // unit) * unit

    quarter_one = height((w_up.size + w_hidden.size // 2) // 4)
    quarter_other = height((w_down.size + w_hidden.size // 2) // 4)
    late = 2 * width * width
    quarter_two = height((w_value.size + width * zwidth + late // 2) // 4)
    quarter_three = height((width * w_value.shape[1] + late // 2) // 4)
    (
        output,
        direct4,
        vpre,
        rpre,
        zpre,
        grad_u,
        grad_h,
        ffn_gain_part,
        *ffn_parts,
    ) = forward_call(
        info,
        jnp.concatenate([one.own_quarter, other.own_quarter]),
        key_mask,
        x4,
        normed4,
        total4,
        cotangent.reshape(rows, width),
        qk_scale,
        qk_shift,
        ffn_gain.reshape(1, width),
        pairs,
        (quarter_one, quarter_other),
    )
    one.open(*ffn_parts[:2])
    other.open(*ffn_parts[2:])
    t = run(ffn_gain_part, one, other)
    grad4, part4, qk_part, omega_part, send_b, keep_b, send_c, keep_c = backward_call(
        info,
        jnp.concatenate([two.own_quarter, three.own_quarter]),
        key_mask,
        normed4,
        total4,
        (vpre, rpre, zpre, grad_u, grad_h),
        qk_scale,
        qk_shift,
        omega4,
        pairs,
        (quarter_two, quarter_three),
        [t],
    )
    t = run(qk_part, one, other)
    (send_b, send_c), t = gate((send_b, send_c), t)
    two.open(send_b, keep_b)
    three.open(send_c, keep_c)
    back_ends, back_final = scan_call(
        back_ends_kernel,
        "back_ends",
        [],
        [grad4, keep4, chunk_keep],
        [ends_shape, final_shape],
        [t],
        work=2,
    )
    back_finals = lax.all_gather(back_final, "ch", axis=0)
    t = run(back_finals, two, three)
    sums, coef_parts, keep_parts = [], [], []
    tables = (keep4, coef4, chunk_keep, device_keep)
    for lowest in range(0, groups, 2):
        done, coef_part, keep_part = back_call(
            lowest, 2, place_info, grad4, back_ends, back_finals, starts, normed4, part4, tables, [t]
        )
        sums.append(done)
        coef_parts.append(coef_part)
        keep_parts.append(keep_part)
        t = run(coef_part, two, three, one, other)
    back4, two.rider = unnorm_call(
        x4,
        sums,
        direct4,
        gain4,
        coef_parts,
        keep_parts,
        omega_part,
        ffn_gain_part,
        qk_part,
        [t],
    )
    back4, t = gate(back4, two.rider[:SUBS, :LANES])
    returned = lax.all_to_all(back4, "ch", 0, 0)
    input_grad = returned.reshape(inputs.shape)
    t = run(t, two, three, one, other)
    t = run(t, two, three, one, other)
    t = run((t, returned[0, :SUBS]), two, three, one, other)
    while three.at < three.steps:
        t = run(t, two, three, one, other)
    up_rows, quarter_rows = w_up.shape[0], w_down.shape[0] // 4
    half = w_hidden.shape[1] // 2
    hidden_rows = w_hidden.shape[0] // 4
    up_grad, down_grad, hidden_grad = finish(
        [one, other],
        [
            [
                (0, as_columns(0, up_rows, 0, lambda q: q * QUARTER)),
                (2, as_rows(up_rows, hidden_rows, 0, half)),
            ],
            [
                (1, as_rows(0, quarter_rows, 0, w_down.shape[1])),
                (
                    2,
                    as_rows(
                        quarter_rows * w_down.shape[1] // QUARTER, hidden_rows, half, 2 * half
                    ),
                ),
            ],
        ],
        [w_up.shape, w_down.shape, w_hidden.shape],
        "finish_one",
        [t],
    )
    z_at, z_rows = w_value.shape[0], width * zwidth // QUARTER // 4
    reset_at = width + zwidth
    hidden_in_at = reset_at + w_value.shape[1]

    def rest_column(q):
        return jnp.where(q < 2, q * QUARTER, hidden_in_at + (q - 2) * QUARTER)

    value_grad, base_grad = finish(
        [two, three],
        [
            [
                (0, as_columns(0, width, 0, lambda q: q * QUARTER)),
                (1, as_halves(z_at, z_rows, width)),
                (1, as_columns(z_at + z_rows, width // 2, 0, rest_column)),
            ],
            [
                (1, as_columns(0, width, 0, lambda q: reset_at + q * QUARTER)),
                (1, as_columns(width, width // 2, width // 2, rest_column)),
            ],
        ],
        [w_value.shape, w_base.shape],
        "finish_rest",
    )

    tables = [grouped(table) for table in (gates, decay, beta, eta)]
    gains = small_call(riders_of(two), tables)
    return (
        output.reshape(cotangent.shape),
        input_grad,
        gains[0].reshape(width),
        gains[1].T,
        gains[2].T,
        gains[3].T,
        gains[4].T,
        gains[5].reshape(width),
        value_grad,
        base_grad,
        gains[7],
        gains[8],
        hidden_grad,
        gains[6].reshape(width),
        up_grad,
        down_grad,
    )


def solution(mesh):
    whole = P()
    placed = (
        (P("seq", None, "ch"), P("seq", "ch", None))
        + (whole,) * 14
        + (P("seq"), P("seq", None))
    )
    return jax.shard_map(
        local,
        mesh=mesh,
        in_specs=placed,
        out_specs=(P("seq", "ch", None), P("seq", None, "ch")) + (whole,) * 14,
        check_vma=False,
    )
```

```python
import math

import jax
import jax.numpy as jnp
from jax import lax
from jax.experimental import pallas as pl
from jax.experimental.pallas import tpu as pltpu
from jax.sharding import PartitionSpec as P

EPS = 1e-05
CENTER = math.sqrt(0.5)
SPREAD = math.sqrt(0.25 / math.pi)
F32 = jnp.float32
BF16 = jnp.bfloat16
NN = ((1,), (0,))
NT = ((1,), (1,))
TN = ((0,), (0,))
LANES = 128
SUBS = 8
TILE = 256
SMALL = 32
NORM_MIB = 24
FORWARD_MIB = 46
BACKWARD_MIB = 46
VMEM = pl.BlockSpec(memory_space=pltpu.VMEM)
SMEM = pl.BlockSpec(memory_space=pltpu.SMEM)
HBM = pl.BlockSpec(memory_space=pltpu.HBM)


def params(mib):
    return pltpu.CompilerParams(vmem_limit_bytes=mib << 20)


def ordered_call(kernel, tokens, *, in_specs, prefetch=0, grid=None, out_specs, scratch_shapes=(), **rest):
    count, extra = prefetch + len(in_specs), len(tokens)

    def body(*refs):
        kernel(*refs[:count], *refs[count + extra :])

    spec = pltpu.PrefetchScalarGridSpec(
        num_scalar_prefetch=prefetch,
        grid=grid or (1,),
        in_specs=list(in_specs) + [VMEM] * extra,
        out_specs=out_specs,
        scratch_shapes=scratch_shapes,
    )
    run = pl.pallas_call(body, grid_spec=spec, **rest)
    return lambda *args: run(*args, *tokens)


def shape_of(*shape, dtype=F32):
    return jax.ShapeDtypeStruct(shape, dtype)


def split(value):
    high = value.astype(BF16)
    return high, (value - high.astype(F32)).astype(BF16)


def dot(left, right, dims):
    return lax.dot_general(left, right, (dims, ((), ())), preferred_element_type=F32)


def mm3(left, right, dims):
    return (
        dot(left[0], right[0], dims)
        + dot(left[1], right[0], dims)
        + dot(left[0], right[1], dims)
    )


def mm3_short(left, right, dims):
    (left_axis,), (right_axis,) = dims
    return dot(
        jnp.concatenate([left[0], left[1], left[0]], left_axis),
        jnp.concatenate([right[0], right[0], right[1]], right_axis),
        dims,
    )


def sigmoid(value):
    return 0.5 * jnp.tanh(0.5 * value) + 0.5


def rows_sum(value):
    return jnp.sum(value, -1, keepdims=True)


def split_kernel(*refs):
    count = len(refs) // 3
    for index in range(count):
        high, low = split(refs[index][...])
        refs[count + 2 * index][...] = high
        refs[count + 2 * index + 1][...] = low


def split_weights(weights, steps=8):
    def spec(weight):
        return pl.BlockSpec((weight.shape[0] // steps, weight.shape[1]), lambda i: (i, 0))

    out = pl.pallas_call(
        split_kernel,
        grid=(steps,),
        in_specs=[spec(w) for w in weights],
        out_specs=[spec(w) for w in weights for _ in range(2)],
        out_shape=[jax.ShapeDtypeStruct(w.shape, BF16) for w in weights for _ in range(2)],
        compiler_params=params(SMALL),
        cost_estimate=pl.CostEstimate(
            flops=4 * sum(w.size for w in weights),
            bytes_accessed=8 * sum(w.size for w in weights),
            transcendentals=0,
        ),
        name="split_weights",
    )(*weights)
    return [(out[2 * i], out[2 * i + 1]) for i in range(len(weights))]


def turned(value):
    return jnp.transpose(value, (1, 0, 2))


def take_steps(ref, g, span, t):
    rows = jnp.stack([ref[g, pl.ds(c * span + t, SUBS), :] for c in range(SUBS)])
    rows = turned(rows)
    return [rows[i] for i in range(SUBS)]


def put_steps(ref, g, span, t, values):
    rows = turned(jnp.stack(values))
    for c in range(SUBS):
        ref[g, pl.ds(c * span + t, SUBS), :] = rows[c]


def rows_of(ref, g, these):
    return [jnp.broadcast_to(ref[g, n : n + 1, :], (SUBS, LANES)) for n in these]


def tree_sum(parts):
    while len(parts) > 1:
        parts = [sum(parts[i : i + 2]) for i in range(0, len(parts), 2)]
    return parts[0]


def scan_ends(source_ref, g, keep_ref, states, span, reverse):
    keeps = rows_of(keep_ref, g, range(states))

    def steps(i, state):
        t = pl.multiple_of((span // SUBS - 1 - i if reverse else i) * SUBS, SUBS)
        fresh = take_steps(source_ref, g, span, t)
        for value in reversed(fresh) if reverse else fresh:
            state = tuple(k * s + value for k, s in zip(keeps, state))
        return state

    zero = jnp.zeros((SUBS, LANES), F32)
    return lax.fori_loop(0, span // SUBS, steps, (zero,) * states, unroll=2)


def fold_ends(ends_ref, group, chunk_keep, states, order):
    total = jnp.zeros((states, LANES), F32)
    for chunk in order:
        total = chunk_keep * total + ends_ref[group, pl.ds(chunk, states, stride=SUBS), :]
    return total


def norm_kernel(x_ref, gain_ref, keep_ref, chunk_keep_ref, normed_ref, ends_ref, final_ref):
    groups, rows, _ = x_ref.shape
    states = keep_ref.shape[1]
    span = rows // SUBS
    width = groups * LANES

    def normalise(i, carry):
        here = pl.ds(pl.multiple_of(i * LANES, LANES), LANES)
        pieces = [x_ref[g, here, :] for g in range(groups)]
        mean = rows_sum(sum(pieces)) / width
        square = rows_sum(sum(p * p for p in pieces)) / width
        scale = lax.rsqrt(square - mean * mean + EPS)
        for g in range(groups):
            normed_ref[g, here, :] = (pieces[g] - mean) * scale * gain_ref[g]
        return carry

    lax.fori_loop(0, rows // LANES, normalise, 0)
    for g in range(groups):
        ends = scan_ends(normed_ref, g, keep_ref, states, span, False)
        for n in range(states):
            ends_ref[g, n * SUBS : (n + 1) * SUBS, :] = ends[n]
        final_ref[g] = fold_ends(ends_ref, g, chunk_keep_ref[g], states, range(SUBS))


def mix_kernel(
    place_ref,
    normed_ref,
    ends_ref,
    finals_ref,
    keep_ref,
    coef_ref,
    chunk_keep_ref,
    device_keep_ref,
    omega_ref,
    total_ref,
    start_ref,
):
    groups, rows, _ = normed_ref.shape
    states = keep_ref.shape[1]
    span = rows // SUBS
    ways = finals_ref.shape[0]
    place = place_ref[0]
    for g in range(groups):
        state = jnp.zeros((states, LANES), F32)
        for d in range(ways):
            state = jnp.where(d < place, device_keep_ref[g] * state + finals_ref[d, g], state)
        for chunk in range(SUBS):
            start_ref[g, pl.ds(chunk, states, stride=SUBS), :] = state
            state = chunk_keep_ref[g] * state + ends_ref[g, pl.ds(chunk, states, stride=SUBS), :]
        keeps = rows_of(keep_ref, g, range(states))
        coefs = rows_of(coef_ref, g, range(states))
        omega = jnp.broadcast_to(omega_ref[g], (SUBS, LANES))

        def steps(i, state):
            t = pl.multiple_of(i * SUBS, SUBS)
            totals = []
            for fresh in take_steps(normed_ref, g, span, t):
                state = tuple(k * s + fresh for k, s in zip(keeps, state))
                totals.append(tree_sum([c * s for c, s in zip(coefs, state)] + [omega * fresh]))
            put_steps(total_ref, g, span, t, totals)
            return state

        first = tuple(start_ref[g, n * SUBS : (n + 1) * SUBS, :] for n in range(states))
        lax.fori_loop(0, span // SUBS, steps, first, unroll=2)


def back_ends_kernel(grad_ref, keep_ref, chunk_keep_ref, ends_ref, final_ref):
    _, rows, _ = grad_ref.shape
    states = keep_ref.shape[1]
    span = rows // SUBS
    for g in range(1):
        ends = scan_ends(grad_ref, g, keep_ref, states, span, True)
        for n in range(states):
            ends_ref[g, n * SUBS : (n + 1) * SUBS, :] = ends[n]
        final_ref[g] = fold_ends(ends_ref, g, chunk_keep_ref[g], states, reversed(range(SUBS)))


def back_kernel(
    place_ref,
    grad_ref,
    ends_ref,
    finals_ref,
    start_ref,
    normed_ref,
    part_ref,
    keep_ref,
    coef_ref,
    chunk_keep_ref,
    device_keep_ref,
    sum_ref,
    coef_grad_ref,
    keep_grad_ref,
    init_ref,
):
    _, rows, _ = grad_ref.shape
    states = keep_ref.shape[1]
    span = rows // SUBS
    ways = finals_ref.shape[0]
    place = place_ref[0]
    half = states // 2
    zero = jnp.zeros((SUBS, LANES), F32)
    for g in range(1):
        whole_g = 0
        state = jnp.zeros((states, LANES), F32)
        for d in reversed(range(ways)):
            state = jnp.where(
                d > place, device_keep_ref[whole_g] * state + finals_ref[d, whole_g], state
            )
        for chunk in reversed(range(SUBS)):
            init_ref[pl.ds(chunk, states, stride=SUBS), :] = state
            state = (
                chunk_keep_ref[whole_g] * state
                + ends_ref[whole_g, pl.ds(chunk, states, stride=SUBS), :]
            )
        for part in range(2):
            these = range(part * half, (part + 1) * half)
            keeps = rows_of(keep_ref, whole_g, these)
            coefs = rows_of(coef_ref, whole_g, these)

            def steps(i, carry):
                lam, second, coef_acc, keep_acc = carry
                t = pl.multiple_of((span // SUBS - 1 - i) * SUBS, SUBS)
                fresh = take_steps(grad_ref, g, span, t)
                source = take_steps(normed_ref, g, span, t)
                outs = [None] * SUBS
                for j in reversed(range(SUBS)):
                    keep_acc = tuple(a + v * source[j] for a, v in zip(keep_acc, second))
                    lam = tuple(k * l + fresh[j] for k, l in zip(keeps, lam))
                    coef_acc = tuple(a + l * source[j] for a, l in zip(coef_acc, lam))
                    second = tuple(l + k * v for l, k, v in zip(lam, keeps, second))
                    outs[j] = tree_sum([c * l for c, l in zip(coefs, lam)])
                rows = turned(jnp.stack(outs))
                before = part_ref if part == 0 else sum_ref
                for c in range(SUBS):
                    here = pl.ds(c * span + t, SUBS)
                    sum_ref[g, here, :] = before[g, here, :] + rows[c]
                return lam, second, coef_acc, keep_acc

            first = tuple(init_ref[n * SUBS : (n + 1) * SUBS, :] for n in these)
            nothing = (zero,) * half
            lam, second, coef_acc, keep_acc = lax.fori_loop(
                0, span // SUBS, steps, (first, nothing, nothing, nothing)
            )
            for j, n in enumerate(these):
                start = start_ref[whole_g, n * SUBS : (n + 1) * SUBS, :]
                keep_acc_n = keep_acc[j] + start * second[j]
                coef_grad_ref[g, n : n + 1, :] = jnp.sum(coef_acc[j], 0, keepdims=True)
                keep_grad_ref[g, n : n + 1, :] = jnp.sum(keep_acc_n, 0, keepdims=True)


def unnorm_kernel(
    calls,
    x_ref,
    *refs,
):
    sums, refs = refs[:calls], refs[calls:]
    direct_ref, gain_ref, refs = refs[0], refs[1], refs[2:]
    coefs, keeps, refs = refs[:calls], refs[calls : 2 * calls], refs[2 * calls :]
    omega_ref, ffn_ref, qk_ref, out_ref, small_ref, gain_grad = refs
    groups, rows, _ = x_ref.shape
    width = groups * LANES
    share = groups // calls
    tile = pl.program_id(0)

    @pl.when(tile == 0)
    def _():
        gain_grad[...] = jnp.zeros_like(gain_grad)

    pieces = [x_ref[g] for g in range(groups)]
    mean = rows_sum(sum(pieces)) / width
    square = rows_sum(sum(p * p for p in pieces)) / width
    scale = lax.rsqrt(square - mean * mean + EPS)
    centered = [(p - mean) * scale for p in pieces]
    grads = [sums[g // share][g % share] for g in range(groups)]
    for g in range(groups):
        gain_grad[g : g + 1, :] += jnp.sum(grads[g] * centered[g], 0, keepdims=True)
    scaled = [grads[g] * gain_ref[g] for g in range(groups)]
    plain = rows_sum(sum(scaled)) / width
    cross = rows_sum(sum(s * c for s, c in zip(scaled, centered))) / width
    for g in range(groups):
        out_ref[g] = direct_ref[g] + scale * (scaled[g] - plain - centered[g] * cross)

    @pl.when(tile == pl.num_programs(0) - 1)
    def _():
        states = coefs[0].shape[1]
        for i, refs in enumerate((coefs, keeps)):
            for g in range(groups):
                at = slice(g * states, (g + 1) * states)
                small_ref[at, i * LANES : (i + 1) * LANES] = refs[g // share][g % share]
        at = groups * states
        small_ref[at:, :] = jnp.zeros((small_ref.shape[0] - at, 2 * LANES), F32)
        small_ref[at : at + groups, :LANES] = gain_grad[:groups]
        for g in range(groups):
            here = slice(at + groups + g, at + groups + g + 1)
            small_ref[here, :LANES] = omega_ref[g]
            small_ref[here, LANES:] = ffn_ref[:, g * LANES : (g + 1) * LANES]
        small_ref[at : at + 4, LANES:] = qk_ref[0:4, :]


def group_spec(array, lowest=0):
    axis = array.ndim - 3
    block = array.shape[:axis] + (1,) + array.shape[axis + 1 :]
    return pl.BlockSpec(block, lambda g: (0,) * axis + (lowest + g, 0, 0))


def scan_call(kernel, name, scalars, arrays, outs, tokens=(), lowest=0, count=None, scratch=(), work=4):
    count = count or arrays[0].shape[-3]
    states, rows = outs[-1].shape[-2], arrays[0].shape[-2]
    return ordered_call(
        kernel,
        tokens,
        grid=(count,),
        in_specs=[SMEM] * len(scalars) + [group_spec(v, lowest) for v in arrays],
        out_specs=[group_spec(v) for v in outs],
        scratch_shapes=scratch,
        out_shape=outs,
        compiler_params=params(SMALL),
        cost_estimate=pl.CostEstimate(
            flops=work * rows * count * LANES * 16,
            bytes_accessed=12 * rows * count * LANES,
            transcendentals=0,
        ),
        name=name,
    )(*scalars, *arrays)


def back_call(lowest, count, place_info, grad4, ends, finals, starts, normed4, part4, tables, tokens):
    rows, states = grad4.shape[1], starts.shape[1] // SUBS
    arrays = [grad4, ends, finals, starts, normed4, part4, *tables]
    outs = [shape_of(count, rows, LANES)] + [shape_of(count, states, LANES)] * 2
    return scan_call(
        back_kernel,
        "back",
        [place_info],
        arrays,
        outs,
        tokens,
        lowest,
        count,
        [pltpu.VMEM((states * SUBS, LANES), F32)],
        10,
    )


def unnorm_call(x4, sums, direct4, gain4, coefs, keeps, omega, ffn, qk, tokens):
    groups, rows, _ = x4.shape
    states = coefs[0].shape[1]
    by_group = pl.BlockSpec((groups, TILE, LANES), lambda i: (0, i, 0))
    halves = [pl.BlockSpec((s.shape[0], TILE, LANES), lambda i: (0, i, 0)) for s in sums]
    height = -(-(groups * states + 2 * groups) // 16) * 16
    return ordered_call(
        lambda *refs: unnorm_kernel(len(sums), *refs),
        tokens,
        grid=(rows // TILE,),
        in_specs=[by_group] + halves + [by_group] + [VMEM] * (4 + 2 * len(sums)),
        out_specs=[by_group, pl.BlockSpec((height, 2 * LANES), lambda i: (0, 0))],
        out_shape=[shape_of(*x4.shape), shape_of(height, 2 * LANES)],
        scratch_shapes=[pltpu.VMEM((SUBS, LANES), F32)],
        compiler_params=params(SMALL),
        cost_estimate=pl.CostEstimate(
            flops=20 * x4.size, bytes_accessed=16 * x4.size, transcendentals=0
        ),
        name="unnorm",
    )(x4, *sums, direct4, gain4, *coefs, *keeps, *omega, ffn, *qk)


def small_kernel(
    part_a,
    part_b,
    part_c,
    part_d,
    gate_ref,
    decay_ref,
    beta_ref,
    eta_ref,
    gain_out,
    delta_out,
    alpha_out,
    beta_out,
    eta_out,
    omega_out,
    ffn_out,
    scale_out,
    shift_out,
):
    groups, states, _ = gate_ref.shape
    root = math.sqrt(states)
    at = groups * states
    height = -(-(groups * states + 2 * groups) // 16) * 16
    tails = [ref[ref.shape[0] - height :, :] for ref in (part_a, part_b, part_c, part_d)]
    total = (tails[0] + tails[1]) + (tails[2] + tails[3])
    for g in range(groups):
        here = slice(g * states, (g + 1) * states)
        coef, keep = total[here, :LANES], total[here, LANES:]
        gate, decay, beta, eta = gate_ref[g], decay_ref[g], beta_ref[g], eta_ref[g]
        keep = keep * gate * beta * (eta / root)
        gate_grad = coef * beta * (eta / root) - keep * decay
        lanes = slice(g * LANES, (g + 1) * LANES)
        delta_out[:, lanes] = gate_grad * gate * (1.0 - gate)
        alpha_out[:, lanes] = -keep * gate * decay * (1.0 - decay)
        beta_out[:, lanes] = coef * gate * (eta / root)
        eta_out[:, lanes] = coef * gate * beta / root
    gain_out[...] = total[at : at + groups, :LANES]
    omega_out[...] = total[at + groups : at + 2 * groups, :LANES]
    ffn_out[...] = total[at + groups : at + 2 * groups, LANES:]
    scale_out[...] = total[at : at + 2, LANES:]
    shift_out[...] = total[at + 2 : at + 4, LANES:]


def small_call(parts, tables):
    groups, states, _ = tables[0].shape
    row, table = shape_of(groups, LANES), shape_of(states, groups * LANES)
    two = shape_of(2, LANES)
    return pl.pallas_call(
        small_kernel,
        in_specs=[VMEM] * 8,
        out_specs=[VMEM] * 9,
        out_shape=[row, table, table, table, table, row, row, two, two],
        compiler_params=params(SMALL),
        name="small_grads",
    )(*parts, *tables)


QUARTER = 256
EVERY = slice(None)


def columns(total, step=512):
    return [slice(i, min(i + step, total)) for i in range(0, total, step)]


def joined(ref):
    return jnp.concatenate([ref[g] for g in range(ref.shape[0])], 1)


def silu_slope(act, gate):
    return gate + act * (1.0 - gate)


class Attention:
    def __init__(self, z, scale_ref, shift_ref, mask_ref, base_row, length):
        rows, span = z.shape[0], mask_ref.shape[1]
        blocks = rows // span
        self.query = split(z * scale_ref[0:1, :] + shift_ref[0:1, :])
        self.key = split(z * scale_ref[1:2, :] + shift_ref[1:2, :])
        lane = lax.broadcasted_iota(jnp.int32, (1, span), 1)
        valids, counts = [], []
        for b in range(blocks):
            position = base_row + b * span + lane
            last_block = (base_row + b * span) // span == (length - 1) // span
            kept = (position < length) & (jnp.logical_not(last_block) | (mask_ref[...] == 1))
            valid = jnp.where(kept, 1.0, 0.0)
            count = jnp.maximum(rows_sum(valid), 1.0)
            valids.append(valid)
            counts.append(jnp.broadcast_to(count, (1, span)))
        row = lax.broadcasted_iota(jnp.int32, (rows, rows), 0)
        column = lax.broadcasted_iota(jnp.int32, (rows, rows), 1)
        near = (row >= column) & (row // span == column // span)
        self.mask = jnp.where(near, jnp.concatenate(valids, 1), 0.0)
        self.count = jnp.concatenate(counts, 1)
        self.spot = mm3_short(self.query, self.key, NT) / self.count - CENTER

    def weight(self):
        curve = lax.erf(self.spot * (1.0 / (SPREAD * math.sqrt(2.0))))
        return split((0.5 + 0.5 * curve) * self.mask)

    def slope(self):
        return (
            jnp.exp(self.spot * self.spot * (-1.0 / (2.0 * SPREAD * SPREAD)))
            * (self.mask / self.count)
            * (1.0 / (SPREAD * math.sqrt(2.0 * math.pi)))
        )


def add_to(total_ref, quarter, at, pieces, first):
    for piece in pieces:
        here = slice(at, at + piece.shape[0])
        at += piece.shape[0]
        total_ref[quarter, here, :] = jnp.where(first, 0.0, total_ref[quarter, here, :]) + piece
    return at


def packed_rows(value):
    return [value[:, i : i + QUARTER] for i in range(0, value.shape[1], QUARTER)]


class Fetch:
    def __init__(self, sources, targets, sems, first):
        self.first = first
        self.copies = [
            pltpu.make_async_copy(source, target, sems.at[i])
            for i, (source, target) in enumerate(zip(sources, targets))
        ]

        @pl.when(first)
        def _():
            for copy in self.copies:
                copy.start()

    def wait(self, *which):
        @pl.when(self.first)
        def _():
            for i in which:
                self.copies[i].wait()


class HandOut:
    def __init__(self, own, total, send, keep, row, sems, last):
        self.own, self.total, self.send, self.keep = own, total, send, keep
        self.rows = pl.ds(row, total.shape[1])
        self.sems, self.last = sems, last

    def each(self, quarter, act):
        apart = quarter ^ self.own

        @pl.when(self.last & (apart >= 2))
        def _():
            act(
                pltpu.make_async_copy(
                    self.total.at[quarter], self.send.at[3 - apart, self.rows], self.sems.at[quarter]
                )
            )

        @pl.when(self.last & (apart < 2))
        def _():
            act(
                pltpu.make_async_copy(
                    self.total.at[quarter], self.keep.at[1 - apart, self.rows], self.sems.at[quarter]
                )
            )

    def start(self, quarter):
        self.each(quarter, lambda copy: copy.start())

    def wait(self):
        for quarter in range(4):
            self.each(quarter, lambda copy: copy.wait())


def forward_kernel(
    info_ref,
    place_ref,
    mask_ref,
    x_ref,
    normed_ref,
    total_ref,
    cot_ref,
    scale_ref,
    shift_ref,
    gain_ref,
    wv_h,
    wv_l,
    wb_h,
    wb_l,
    wh_h,
    wh_l,
    wu_h,
    wu_l,
    wd_h,
    wd_l,
    out_ref,
    direct_ref,
    v_h,
    v_l,
    vsil,
    rst,
    attr,
    weight_h,
    weight_l,
    slope_ref,
    zpre,
    grad_u_ref,
    grad_h_ref,
    gain_grad_ref,
    send_ref,
    keep_ref,
    upd,
    hpre,
    gr_h,
    gr_l,
    a_h,
    a_l,
    usil,
    du_h,
    du_l,
    acc_a,
    acc_b,
    sems_a,
    sems_b,
):
    tile = pl.program_id(0)
    first = tile == 0
    groups, rows, _ = x_ref.shape
    width = groups * LANES
    zwidth = scale_ref.shape[1]
    values = wv_h.shape[1]
    units = wu_h.shape[1]
    base_row, length = info_ref[0] + tile * rows, info_ref[1]
    last = tile == pl.num_programs(0) - 1
    out_a = HandOut(place_ref[0], acc_a, send_ref, keep_ref, 0, sems_a, last)
    out_b = HandOut(place_ref[1], acc_b, send_ref, keep_ref, acc_a.shape[1], sems_b, last)

    @pl.when(first)
    def _():
        gain_grad_ref[...] = jnp.zeros_like(gain_grad_ref)

    def put(high_ref, low_ref, where, value):
        high, low = split(value)
        high_ref[where] = high
        low_ref[where] = low
        return high, low

    n_pair = split(joined(normed_ref))
    total = joined(total_ref)
    m_pair = split(total * sigmoid(total))
    for c in columns(values):
        pre = mm3(n_pair, (wv_h[:, c], wv_l[:, c]), NN)
        s = sigmoid(pre)
        act = pre * s
        put(v_h, v_l, (EVERY, c), act)
        vsil[:, c] = silu_slope(act, s)
    c = slice(width, width + zwidth)
    pre = mm3(m_pair, (wb_h[:, c], wb_l[:, c]), NN)
    zpre[...] = pre
    attention = Attention(
        pre * sigmoid(pre), scale_ref, shift_ref, mask_ref, base_row, length
    )
    c = slice(0, width)
    upd[...] = sigmoid(mm3(m_pair, (wb_h[:, c], wb_l[:, c]), NN))
    for c in columns(values):
        w = slice(width + zwidth + c.start, width + zwidth + c.stop)
        pre = mm3(m_pair, (wb_h[:, w], wb_l[:, w]), NN)
        s = sigmoid(pre)
        act = pre * s
        rst[:, c] = act
        attr[:, c] = silu_slope(act, s)
    w = slice(width + zwidth + values, width + zwidth + values + width)
    hpre[...] = mm3(m_pair, (wb_h[:, w], wb_l[:, w]), NN)
    weight = attention.weight()
    weight_h[...], weight_l[...] = weight
    slope_ref[...] = attention.slope()
    for c in columns(values):
        got = mm3(weight, (v_h[:, c], v_l[:, c]), NN)
        put(gr_h, gr_l, (EVERY, c), got * rst[:, c])
        attr[:, c] = got * attr[:, c]
    pre = hpre[...] + mm3((gr_h[...], gr_l[...]), (wh_h[...], wh_l[...]), NN)
    s = sigmoid(pre)
    hidden = pre * s
    hpre[...] = silu_slope(hidden, s)
    x = joined(x_ref)
    update = upd[...]
    apart = hidden - x
    gated = x + update * apart
    mean = rows_sum(gated) / width
    square = rows_sum(gated * gated) / width
    scale = lax.rsqrt(square - mean * mean + EPS)
    centered = (gated - mean) * scale
    f_pair = split(centered * gain_ref[...])
    for c in columns(units):
        pre = mm3(f_pair, (wu_h[:, c], wu_l[:, c]), NN)
        s = sigmoid(pre)
        act = pre * s
        put(a_h, a_l, (EVERY, c), act)
        usil[:, c] = silu_slope(act, s)
    live = (base_row + lax.broadcasted_iota(jnp.int32, (rows, 1), 0) < length).astype(F32)
    out_ref[...] = (gated + mm3((a_h[...], a_l[...]), (wd_h[...], wd_l[...]), NN)) * live

    grad_out = cot_ref[...] * live
    do_pair = split(grad_out)
    for c in columns(units):
        put(du_h, du_l, (EVERY, c), mm3(do_pair, (wd_h[c, :], wd_l[c, :]), NT) * usil[:, c])
    grad_f = mm3((du_h[...], du_l[...]), (wu_h[...], wu_l[...]), NT)
    gain_grad_ref[...] += jnp.sum(grad_f * centered, 0, keepdims=True)
    scaled = grad_f * gain_ref[...]
    grad_gated = grad_out + scale * (
        scaled - rows_sum(scaled) / width - centered * (rows_sum(scaled * centered) / width)
    )
    grad_u = grad_gated * apart * update * (1.0 - update)
    grad_u_ref[...] = grad_u
    u_pair = split(grad_u)
    grad_h = grad_gated * update * hpre[...]
    grad_h_ref[...] = grad_h
    h_pair = split(grad_h)
    direct = grad_gated * (1.0 - update)
    for g in range(groups):
        direct_ref[g] = direct[:, g * LANES : (g + 1) * LANES]
    for q in range(0, 4, 2):
        c = slice(q * QUARTER, (q + 2) * QUARTER)
        up = mm3(f_pair, (du_h[:, c], du_l[:, c]), TN)
        rest = mm3(m_pair, u_pair if q == 0 else h_pair, TN)
        down = mm3((a_h[:, c], a_l[:, c]), do_pair, TN)
        hid = mm3((gr_h[:, c], gr_l[:, c]), h_pair, TN)
        for i in range(2):
            c = slice(i * QUARTER, (i + 1) * QUARTER)
            at = add_to(acc_a, q + i, 0, [up[:, c]], first)
            add_to(acc_a, q + i, at, [rest[:, c]], first)
            at = add_to(acc_b, q + i, 0, packed_rows(down[c]), first)
            add_to(acc_b, q + i, at, packed_rows(hid[c]), first)
            out_a.start(q + i)
            out_b.start(q + i)
    out_a.wait()
    out_b.wait()


def backward_kernel(
    continued,
    place_ref,
    normed_ref,
    total_ref,
    v_h,
    v_l,
    vsil,
    rst,
    attr,
    weight_h,
    weight_l,
    slope_ref,
    zpre,
    grad_u_ref,
    grad_h_ref,
    scale_ref,
    shift_ref,
    omega_ref,
    wh_h,
    wh_l,
    wv_h_hbm,
    wv_l_hbm,
    wb_h_hbm,
    wb_l_hbm,
    *refs,
):
    (
        grad_ref,
        part_ref,
        qk_grad_ref,
        omega_grad_ref,
        send_ref,
        keep_ref,
        da_h,
        da_l,
        dv_h,
        dv_l,
        bz_h,
        bz_l,
        br_h,
        br_l,
        acc_b,
        acc_c,
        wv_h,
        wv_l,
        wb_h,
        wb_l,
        sems_b,
        sems_c,
        weight_sems,
    ) = refs[2 if continued else 0 :]
    tile = pl.program_id(0)
    first, last = tile == 0, tile == pl.num_programs(0) - 1
    groups = normed_ref.shape[0]
    width = groups * LANES
    zwidth = scale_ref.shape[1]
    values = vsil.shape[1]
    fetch = Fetch(
        [wv_h_hbm, wv_l_hbm, wb_h_hbm, wb_l_hbm],
        [wv_h, wv_l, wb_h, wb_l],
        weight_sems,
        first,
    )
    out_b = HandOut(place_ref[0], acc_b, send_ref, keep_ref, 0, sems_b, last)
    out_c = HandOut(place_ref[1], acc_c, send_ref, keep_ref, acc_b.shape[1], sems_c, last)

    @pl.when(first)
    def _():
        qk_grad_ref[...] = jnp.zeros_like(qk_grad_ref)
        omega_grad_ref[...] = jnp.zeros_like(omega_grad_ref)

    def put(high_ref, low_ref, where, value):
        high, low = split(value)
        high_ref[where] = high
        low_ref[where] = low

    u_pair = split(grad_u_ref[...])
    h_pair = split(grad_h_ref[...])
    for c in columns(values):
        got = mm3(h_pair, (wh_h[c, :], wh_l[c, :]), NT)
        put(da_h, da_l, (EVERY, c), got * rst[:, c])
        put(br_h, br_l, (EVERY, c), got * attr[:, c])
    pre = zpre[...]
    s = sigmoid(pre)
    z = pre * s
    zsil = silu_slope(z, s)
    query = split(z * scale_ref[0:1, :] + shift_ref[0:1, :])
    key = split(z * scale_ref[1:2, :] + shift_ref[1:2, :])
    weight = (weight_h[...], weight_l[...])
    grad_scores = split(mm3((da_h[...], da_l[...]), (v_h[...], v_l[...]), NT) * slope_ref[...])
    for c in columns(values):
        got = mm3(weight, (da_h[:, c], da_l[:, c]), TN)
        put(dv_h, dv_l, (EVERY, c), got * vsil[:, c])
    grad_q = mm3(grad_scores, key, NN)
    grad_k = mm3(grad_scores, query, TN)
    qk_grad_ref[0:1, :] += jnp.sum(grad_q * z, 0, keepdims=True)
    qk_grad_ref[1:2, :] += jnp.sum(grad_k * z, 0, keepdims=True)
    qk_grad_ref[2:3, :] += jnp.sum(grad_q, 0, keepdims=True)
    qk_grad_ref[3:4, :] += jnp.sum(grad_k, 0, keepdims=True)
    put(
        bz_h,
        bz_l,
        (EVERY, EVERY),
        (grad_q * scale_ref[0:1, :] + grad_k * scale_ref[1:2, :]) * zsil,
    )

    n_pair = split(joined(normed_ref))
    total = joined(total_ref)
    gate_here = sigmoid(total)
    mixed = total * gate_here
    m_pair = split(mixed)
    grad_bz = mm3(m_pair, (bz_h[...], bz_l[...]), TN)
    for q in range(0, 4, 2):
        c = slice(q * QUARTER, (q + 2) * QUARTER)
        value = mm3(n_pair, (dv_h[:, c], dv_l[:, c]), TN)
        reset = mm3(m_pair, (br_h[:, c], br_l[:, c]), TN)
        for i in range(2):
            c = slice(i * QUARTER, (i + 1) * QUARTER)
            at = add_to(acc_b, q + i, 0, [value[:, c]], first)
            got = grad_bz[(q + i) * width // 4 : (q + i + 1) * width // 4]
            half = got.shape[0] // 2
            add_to(acc_b, q + i, at, [jnp.concatenate([got[:half], got[half:]], 1)], first)
            add_to(acc_c, q + i, 0, [reset[:, c]], first)
            out_b.start(q + i)
            out_c.start(q + i)

    fetch.wait(0, 1, 2, 3)
    grad_n = mm3((dv_h[...], dv_l[...]), (wv_h[...], wv_l[...]), NT)
    at = [0, width, width + zwidth, width + zwidth + values, 2 * width + zwidth + values]
    w = [slice(i, j) for i, j in zip(at[:-1], at[1:])]
    grad = (
        mm3(u_pair, (wb_h[:, w[0]], wb_l[:, w[0]]), NT)
        + mm3_short((bz_h[...], bz_l[...]), (wb_h[:, w[1]], wb_l[:, w[1]]), NT)
        + mm3((br_h[...], br_l[...]), (wb_h[:, w[2]], wb_l[:, w[2]]), NT)
        + mm3(h_pair, (wb_h[:, w[3]], wb_l[:, w[3]]), NT)
    ) * silu_slope(mixed, gate_here)
    for g in range(groups):
        lanes = slice(g * LANES, (g + 1) * LANES)
        got = grad[:, lanes]
        grad_ref[g] = got
        part_ref[g] = grad_n[:, lanes] + got * omega_ref[g]
        omega_grad_ref[g] += jnp.sum(got * normed_ref[g], 0, keepdims=True)
    out_b.wait()
    out_c.wait()


def by_row(count, lowest=0):
    return pl.BlockSpec((TILE, count), lambda i: (lowest + i, 0))


def forward_call(info, place, key_mask, x4, normed4, total4, cot, qk_scale, qk_shift, ffn_gain, pairs, heights):
    groups, rows, _ = x4.shape
    width = groups * LANES
    wv, wb, wh, wu, wd = pairs
    values, units, zwidth = wv[0].shape[1], wu[0].shape[1], qk_scale.shape[1]
    flat = [part for pair in pairs for part in pair]
    by_group = pl.BlockSpec((groups, TILE, LANES), lambda i: (0, i, 0))
    macs = rows * (wv[0].size + wb[0].size + wh[0].size + 3 * wu[0].size + 3 * wd[0].size)
    return pl.pallas_call(
        forward_kernel,
        grid=(rows // TILE,),
        in_specs=[SMEM, SMEM, VMEM, by_group, by_group, by_group, by_row(width)]
        + [VMEM] * (3 + len(flat)),
        out_specs=[
            by_row(width),
            by_group,
            by_row(values),
            by_row(values),
            by_row(values),
            by_row(values),
            by_row(values),
            by_row(TILE),
            by_row(TILE),
            by_row(TILE),
            by_row(zwidth),
            by_row(width),
            by_row(width),
            pl.BlockSpec((1, width), lambda i: (0, 0)),
            HBM,
            HBM,
        ],
        out_shape=[
            shape_of(rows, width),
            shape_of(groups, rows, LANES),
            shape_of(rows, values, dtype=BF16),
            shape_of(rows, values, dtype=BF16),
            shape_of(rows, values),
            shape_of(rows, values),
            shape_of(rows, values),
            shape_of(rows, TILE, dtype=BF16),
            shape_of(rows, TILE, dtype=BF16),
            shape_of(rows, TILE),
            shape_of(rows, zwidth),
            shape_of(rows, width),
            shape_of(rows, width),
            shape_of(1, width),
        ]
        + [shape_of(2, sum(heights), QUARTER)] * 2,
        scratch_shapes=[
            pltpu.VMEM((TILE, width), F32),
            pltpu.VMEM((TILE, width), F32),
            pltpu.VMEM((TILE, values), BF16),
            pltpu.VMEM((TILE, values), BF16),
            pltpu.VMEM((TILE, units), BF16),
            pltpu.VMEM((TILE, units), BF16),
            pltpu.VMEM((TILE, units), F32),
            pltpu.VMEM((TILE, units), BF16),
            pltpu.VMEM((TILE, units), BF16),
        ]
        + [pltpu.VMEM((4, height, QUARTER), F32) for height in heights]
        + [pltpu.SemaphoreType.DMA((4,))] * 2,
        compiler_params=params(FORWARD_MIB),
        cost_estimate=pl.CostEstimate(flops=6 * macs, bytes_accessed=48 << 20, transcendentals=0),
        name="forward",
    )(info, place, key_mask, x4, normed4, total4, cot, qk_scale, qk_shift, ffn_gain, *flat)


def backward_call(
    place, normed4, total4, saved, qk_scale, qk_shift, omega4, pairs, heights, lowest, tiles, before, tokens
):
    groups, rows, _ = normed4.shape
    width = groups * LANES
    wv, wb, wh = pairs[:3]
    values, zwidth = wv[0].shape[1], qk_scale.shape[1]
    by_group = pl.BlockSpec((groups, TILE, LANES), lambda i: (0, lowest + i, 0))
    fetched = [*wv, *wb]
    args = [place, normed4, total4, *saved, qk_scale, qk_shift, omega4, *wh, *fetched]
    quarters = [shape_of(2, sum(heights), QUARTER)] * 2
    return ordered_call(
        lambda *refs: backward_kernel(bool(before), *refs),
        tokens,
        grid=(tiles,),
        in_specs=[SMEM, by_group, by_group]
        + [by_row(s.shape[1], lowest) for s in saved]
        + [VMEM] * (3 + len(wh))
        + [HBM] * (len(fetched) + len(before)),
        out_specs=[
            by_group,
            by_group,
            pl.BlockSpec((8, zwidth), lambda i: (0, 0)),
            pl.BlockSpec((groups, 1, LANES), lambda i: (0, 0, 0)),
        ]
        + [HBM] * 2,
        out_shape=[
            shape_of(groups, rows, LANES),
            shape_of(groups, rows, LANES),
            shape_of(8, zwidth),
            shape_of(groups, 1, LANES),
        ]
        + quarters,
        input_output_aliases={len(args): 0, len(args) + 1: 1} if before else {},
        scratch_shapes=[pltpu.VMEM((TILE, values), BF16)] * 4
        + [pltpu.VMEM((TILE, zwidth), BF16)] * 2
        + [pltpu.VMEM((TILE, values), BF16)] * 2
        + [pltpu.VMEM((4, height, QUARTER), F32) for height in heights]
        + [pltpu.VMEM(w.shape, BF16) for w in fetched]
        + [pltpu.SemaphoreType.DMA((4,))] * 2
        + [pltpu.SemaphoreType.DMA((len(fetched),))],
        compiler_params=params(BACKWARD_MIB),
        cost_estimate=pl.CostEstimate(
            flops=12 * tiles * TILE * (wv[0].size + wb[0].size + wh[0].size),
            bytes_accessed=40 << 20,
            transcendentals=0,
        ),
        name="backward",
    )(*args, *before)


def swap(value, step):
    axis, distance = step
    size = lax.axis_size(axis)
    return lax.ppermute(value, axis, [(i, i ^ distance) for i in range(size)])


def side(step):
    axis, distance = step
    return (lax.axis_index(axis) // distance) % 2


def device_steps():
    def bits(axis):
        size = lax.axis_size(axis)
        return [(axis, 1 << i) for i in range(size.bit_length() - 1)]

    return bits("ch"), bits("seq")


def orders():
    ch, seq = device_steps()
    x, y, z, rest = ch[1:], seq[:1], seq[1:2], seq[2:]
    out = [
        y + z + x + rest,
        z + y + x + rest,
        z + y + x + rest,
        y + z + x + rest,
    ]
    back = [
        rest[::-1] + z + x + y,
        rest[::-1] + y + x + z,
        rest[::-1] + y + z + x,
        rest[::-1] + z + y + x,
    ]
    return [(ch[:1] + go, come + ch[:1]) for go, come in zip(out, back)]


TOKEN = shape_of(SUBS, LANES)


def gate(value, token):
    return lax.optimization_barrier((value, token))


def halve_kernel(count, first, own_ref, *refs):
    own = own_ref[0]
    parts, (send_ref, next_ref, token_ref) = refs[:count], refs[count:]
    rows = pl.ds(first, send_ref.shape[0])
    send_ref[...] = sum(part[1 - own, rows, :] for part in parts)
    next_ref[...] = sum(part[own, rows, :] for part in parts)
    token_ref[...] = jnp.zeros_like(token_ref)


def halve(parts, window, own, tokens):
    width = parts[0].shape[-1]
    height = parts[0].size // width // 2
    first, rows = window or (0, height)
    parts = [part.reshape(2, height, width) for part in parts]
    return ordered_call(
        lambda *refs: halve_kernel(len(parts), first, *refs),
        tokens,
        in_specs=[SMEM] + [VMEM] * len(parts),
        out_specs=[VMEM] * 3,
        out_shape=[shape_of(rows, width)] * 2 + [TOKEN],
        compiler_params=params(SMALL),
        cost_estimate=pl.CostEstimate(
            flops=2 * rows * width, bytes_accessed=1 << 10, transcendentals=0
        ),
        name="halve",
    )(own.reshape(1), *parts)


def add_kernel(left_ref, right_ref, out_ref, token_ref):
    out_ref[...] = left_ref[...] + right_ref[...]
    token_ref[...] = jnp.zeros_like(token_ref)


def add(left, right, tokens):
    return ordered_call(
        add_kernel,
        tokens,
        in_specs=[VMEM] * 2,
        out_specs=[VMEM] * 2,
        out_shape=[shape_of(*left.shape), TOKEN],
        compiler_params=params(SMALL),
        cost_estimate=pl.CostEstimate(flops=left.size, bytes_accessed=1 << 10, transcendentals=0),
        name="add",
    )(left, right)


def gather_kernel(counts, riders, *refs):
    parts, refs = refs[: len(counts)], refs[len(counts) :]
    out_ref, token_ref = refs[-2:]
    at = 0
    for part, rows in zip(parts, counts):
        out_ref[at : at + rows, :] = part[:rows, :]
        at += rows
    if riders:
        tails = [ref[ref.shape[0] - riders :, :] for ref in refs[:-2]]
        out_ref[at:, :] = sum(tails)
    token_ref[...] = jnp.zeros_like(token_ref)


def gather_parts(parts, counts, riders, rider_rows, tokens):
    total, width = sum(counts), parts[0].shape[1]
    shape = shape_of(total + (rider_rows if riders else 0), width)
    return ordered_call(
        lambda *refs: gather_kernel(counts, rider_rows if riders else 0, *refs),
        tokens,
        in_specs=[VMEM] * (len(parts) + len(riders)),
        out_specs=[VMEM] * 2,
        out_shape=[shape, TOKEN],
        compiler_params=params(SMALL),
        cost_estimate=pl.CostEstimate(flops=0, bytes_accessed=1 << 10, transcendentals=0),
        name="gather_parts",
    )(*parts, *riders)


def finish_kernel(plans, maps, given, outs_count, *refs):
    pieces = len(plans)
    places, refs = refs[:pieces], refs[pieces:]
    quarters, refs = refs[: 4 * pieces], refs[4 * pieces :]
    outs, refs = refs[given : given + outs_count], refs[given + outs_count :]
    token_ref, refs = refs[0], refs[1:]
    token_ref[...] = jnp.zeros_like(token_ref)
    scratch, sems = refs[:pieces], refs[pieces:]
    leave = []
    for p, plan in enumerate(plans):
        place_ref, out_sems = places[p], sems[p]
        bits = place_ref.shape[0] - 1
        blocks = 1 << bits
        rows = scratch[p].shape[1] // blocks
        relative = place_ref[1]
        for bit in range(1, bits):
            relative = relative * 2 + place_ref[1 + bit]
        for i in range(4):
            for r in range(blocks):
                quarter, k = maps[p](i, r)
                target = pl.ds(pl.multiple_of((relative ^ k) * rows, SUBS), rows)
                scratch[p][quarter, target, :] = quarters[4 * p + i][r * rows : (r + 1) * rows, :]
        for i in range(4):
            quarter = place_ref[0] ^ i
            number = 0
            for out, moves in plan:
                for row, count, column, width, out_row, out_column in moves(quarter):
                    copy = pltpu.make_async_copy(
                        scratch[p].at[i, pl.ds(row, count), pl.ds(column, width)],
                        outs[out].at[pl.ds(out_row, count), pl.ds(out_column, width)],
                        out_sems.at[i, number],
                    )
                    copy.start()
                    leave.append(copy)
                    number += 1
    for copy in leave:
        copy.wait()


def aligned(value, step):
    return pl.multiple_of(value, step)


def as_columns(first, rows, out_row, out_column):
    return lambda q: [(first, rows, 0, QUARTER, out_row, aligned(out_column(q), LANES))]


def as_rows(first, rows, start, stop):
    def moves(q):
        return [
            (first + (c - start) // QUARTER * rows, rows, 0, QUARTER, aligned(q * rows, SUBS), c)
            for c in range(start, stop, QUARTER)
        ]

    return moves


def as_halves(first, rows, out_column):
    def moves(q):
        at = q * (2 * rows)
        return [
            (first, rows, 0, LANES, aligned(at, SUBS), out_column),
            (first, rows, LANES, LANES, aligned(at + rows, SUBS), out_column),
        ]

    return moves


def finish(pieces, plans, shapes, name, tokens=(), into=None):
    args = [v for piece in pieces for v in piece.pair + list(piece.got)]
    places = [piece.place for piece in pieces]
    scratch = [pltpu.VMEM((4,) + piece.quarter_shape(), F32) for piece in pieces]
    sems = []
    for piece, plan in zip(pieces, plans):
        number = sum(len(moves(0)) for _, moves in plan)
        sems.append(pltpu.SemaphoreType.DMA((4, number)))
    extra = [] if into is None else [into]
    return ordered_call(
        lambda *refs: finish_kernel(plans, [p.quarter_and_block for p in pieces], len(extra), len(shapes), *refs),
        tokens,
        in_specs=[SMEM] * len(places) + [VMEM] * len(args) + [HBM] * len(extra),
        out_specs=[HBM] * len(shapes) + [VMEM],
        input_output_aliases={len(places) + len(args): len(shapes) - 1} if extra else {},
        out_shape=[shape_of(*shape) for shape in shapes] + [TOKEN],
        scratch_shapes=scratch + sems,
        compiler_params=params(SMALL),
        cost_estimate=pl.CostEstimate(
            flops=0, bytes_accessed=1 << 10, transcendentals=0
        ),
        name=name,
    )(*places, *args, *extra)


class Piece:
    def __init__(self, plan, back):
        self.plan, self.back = plan, back
        self.sides = [side(step).astype(jnp.int32) for step in plan]
        first, second = self.sides[0], self.sides[1]

        def quarter(a, b):
            return 2 * a + b

        self.own_quarter = quarter(first, second).reshape(1)
        self.place = jnp.concatenate([self.own_quarter, jnp.stack(self.sides[2:])])
        self.rider, self.waiting = None, []
        self.at, self.steps = 1, 2 * len(plan)

    def quarter_and_block(self, array, row):
        apart = {step: (row >> i) & 1 for i, step in enumerate(self.back[:-2])}
        apart[self.back[-2]] = array % 2
        block = 0
        for step in self.plan[2:]:
            block = 2 * block + apart[step]
        return 2 * (array // 2) + apart[self.plan[1]], block

    def quarter_shape(self):
        return (self.pair[0].shape[0] - (0 if self.rider is None else self.rider.shape[0]), QUARTER)

    def step(self, *tokens):
        last = len(self.plan)
        if self.at < last:
            own = self.sides[self.at] if self.at > 1 else jnp.ones((), jnp.int32)
            send, self.own, token = halve(self.waiting, self.window if self.at == 1 else None, own, tokens)
            self.got = swap(send, self.plan[self.at])
            self.waiting = [self.own, self.got]
            self.at += 1
            return token
        if self.at == last:
            total, token = add(self.own, self.got, tokens)
            self.parts = [total]
            self.riders = [] if self.rider is None else [self.rider]
        else:
            self.parts.append(self.got)
            if self.rider is not None:
                self.riders = [self.whole, self.got]
        index = self.at - last
        self.at += 1
        if index < last - 1:
            rows = self.parts[0].shape[0]
            counts = [rows << max(i - 1, 0) for i in range(len(self.parts))]
            if len(self.parts) == 1 and not self.riders:
                self.whole = self.parts[0]
            else:
                height = 0 if self.rider is None else self.rider.shape[0]
                self.whole, token = gather_parts(
                    self.parts, counts, self.riders, height, tokens
                )
            self.got = swap(self.whole, self.back[index])
            return token
        self.pair = [self.whole, self.parts[-1]]
        self.got = [swap(v, self.plan[0]) for v in self.pair]
        return tokens[0]


def open_pieces(pieces, heights, send, keep):
    got = swap(send, pieces[0].plan[0])
    first = 0
    for piece, rows in zip(pieces, heights):
        piece.window = (first, rows)
        piece.waiting += [keep, got]
        first += rows


def riders_of(piece):
    return piece.pair + piece.got


def copy_out_kernel(in_ref, out_ref, sem):
    copy = pltpu.make_async_copy(in_ref, out_ref, sem)
    copy.start()
    copy.wait()


def copy_out(value, token):
    return ordered_call(
        copy_out_kernel,
        [token],
        in_specs=[VMEM],
        out_specs=HBM,
        out_shape=shape_of(*value.shape),
        scratch_shapes=[pltpu.SemaphoreType.DMA(())],
        compiler_params=params(SMALL),
        cost_estimate=pl.CostEstimate(flops=0, bytes_accessed=1 << 10, transcendentals=0),
        name="copy_out",
    )(value)


def run(token, *pieces):
    tokens = token if isinstance(token, tuple) else (token,)
    for piece in pieces:
        if piece.at < piece.steps:
            tokens = (piece.step(*tokens),)
    return tokens[0]


def local(
    inputs,
    cotangent,
    norm_gain,
    delta,
    alpha,
    beta,
    eta,
    omega,
    w_value,
    w_base,
    qk_scale,
    qk_shift,
    w_hidden,
    ffn_gain,
    w_up,
    w_down,
    lengths,
    key_mask,
):
    ways = lax.axis_size("ch")
    place = lax.axis_index("ch").astype(jnp.int32)
    _, length, narrow = inputs.shape
    rows = length // ways
    width = narrow * ways
    groups = width // LANES
    states = delta.shape[1]
    span = rows // SUBS

    x4 = lax.all_to_all(inputs.reshape(ways, rows, narrow), "ch", 0, 0)
    pairs = split_weights((w_value, w_base, w_hidden, w_up, w_down))

    def grouped(table):
        return jnp.transpose(table.reshape(groups, LANES, states), (0, 2, 1))

    gates = jax.nn.sigmoid(delta)
    decay = jax.nn.sigmoid(alpha)
    keep = 1.0 - gates * decay
    root = math.sqrt(states)
    keep4 = grouped(keep)
    coef4 = grouped(gates * beta * (eta / root))
    log_keep = jnp.log(keep4)
    chunk_keep = jnp.exp(span * log_keep)
    device_keep = jnp.exp(rows * log_keep)
    gain4 = norm_gain.reshape(groups, 1, LANES)
    omega4 = omega.reshape(groups, 1, LANES)
    place_info = place.reshape(1)

    ends_shape = jax.ShapeDtypeStruct((groups, states * SUBS, LANES), F32)
    final_shape = jax.ShapeDtypeStruct((groups, states, LANES), F32)
    big = jax.ShapeDtypeStruct((groups, rows, LANES), F32)
    normed4, ends, final = pl.pallas_call(
        norm_kernel,
        in_specs=[VMEM] * 4,
        out_specs=[VMEM] * 3,
        out_shape=[big, ends_shape, final_shape],
        compiler_params=params(NORM_MIB),
        name="norm",
    )(x4, gain4, keep4, chunk_keep)
    finals = lax.all_gather(final, "ch", axis=0)
    total4, starts = pl.pallas_call(
        mix_kernel,
        in_specs=[SMEM] + [VMEM] * 8,
        out_specs=[VMEM] * 2,
        out_shape=[big, ends_shape],
        compiler_params=params(NORM_MIB),
        name="mix",
    )(place_info, normed4, ends, finals, keep4, coef4, chunk_keep, device_keep, omega4)

    info = jnp.stack([place * rows, lengths[0].astype(jnp.int32)])
    zwidth = qk_scale.shape[1]
    plans = orders()
    unit = SUBS << (len(plans[0][0]) - 2)
    one, other, two, three = [Piece(*plan) for plan in plans]

    def height(*counts):
        return -(-sum(counts) // QUARTER // unit) * unit

    early_heights = (
        height((w_up.size + 2 * width * width) // 4),
        height((w_down.size + w_hidden.size) // 4),
    )
    late_heights = (
        height((w_value.size + width * zwidth) // 4),
        height(width * w_value.shape[1] // 4),
    )
    (
        output,
        direct4,
        *forward_rest,
    ) = forward_call(
        info,
        jnp.concatenate([one.own_quarter, other.own_quarter]),
        key_mask,
        x4,
        normed4,
        total4,
        cotangent.reshape(rows, width),
        qk_scale,
        qk_shift,
        ffn_gain.reshape(1, width),
        pairs,
        early_heights,
    )
    saved, ffn_gain_part, ffn_parts = forward_rest[:11], forward_rest[11], forward_rest[12:]
    open_pieces((one, other), early_heights, *ffn_parts)
    t = run(ffn_gain_part, one, other)
    own_quarters = jnp.concatenate([two.own_quarter, three.own_quarter])
    before, omega_parts, qk_parts = (), [], []
    tiles = rows // TILE
    for lowest, count in ((0, tiles),):
        *before, qk_part, omega_part, send, keep = backward_call(
            own_quarters,
            normed4,
            total4,
            saved,
            qk_scale,
            qk_shift,
            omega4,
            pairs,
            late_heights,
            lowest,
            count,
            before,
            [t],
        )
        omega_parts.append(omega_part)
        qk_parts.append(qk_part)
        t = run(qk_part, one, other)
        send, t = gate(send, t)
        open_pieces((two, three), late_heights, send, keep)
    grad4, part4 = before
    back_ends, back_final = scan_call(
        back_ends_kernel,
        "back_ends",
        [],
        [grad4, keep4, chunk_keep],
        [ends_shape, final_shape],
        [t],
        work=2,
    )
    back_finals = lax.all_gather(back_final, "ch", axis=0)
    t = run(back_finals, two, one, three, other)
    sums, coef_parts, keep_parts = [], [], []
    tables = (keep4, coef4, chunk_keep, device_keep)
    between = [(), (two, three, one, other), (two, three, one, other), (two, three)]
    for g in range(groups):
        done, coef_part, keep_part = back_call(
            g, 1, place_info, grad4, back_ends, back_finals, starts, normed4, part4, tables, [t]
        )
        sums.append(done)
        coef_parts.append(coef_part)
        keep_parts.append(keep_part)
        t = run((coef_part, t), *between[g % 4])
    back4, two.rider = unnorm_call(
        x4,
        sums,
        direct4,
        gain4,
        coef_parts,
        keep_parts,
        omega_parts,
        ffn_gain_part,
        qk_parts,
        [t],
    )
    back4, t = gate(back4, two.rider[:SUBS, :LANES])
    returned = lax.all_to_all(back4, "ch", 0, 0)
    t = run(t, one, other, two)
    t = run(t, one, other, three)
    t = run(t, two, three)
    t = run(t, two, three)
    t = run(t, one, other, two, three)
    while three.at < three.steps or one.at < one.steps or other.at < other.steps:
        t = run(t, two, three, one, other)
    up_rows, quarter_rows = w_up.shape[0], w_down.shape[0] // 4
    reset_at = width + zwidth
    hidden_in_at = reset_at + w_value.shape[1]

    def rest_column(q):
        return jnp.where(q < 2, q * QUARTER, hidden_in_at + (q - 2) * QUARTER)

    up_grad, down_grad, hidden_grad, base_grad, t = finish(
        [one, other],
        [
            [
                (0, as_columns(0, up_rows, 0, lambda q: q * QUARTER)),
                (3, as_columns(up_rows, width, 0, rest_column)),
            ],
            [
                (1, as_rows(0, quarter_rows, 0, w_down.shape[1])),
                (
                    2,
                    as_rows(
                        quarter_rows * w_down.shape[1] // QUARTER,
                        w_hidden.shape[0] // 4,
                        0,
                        w_hidden.shape[1],
                    ),
                ),
            ],
        ],
        [w_up.shape, w_down.shape, w_hidden.shape, w_base.shape],
        "finish_one",
        [t],
    )
    value_grad, base_grad, t = finish(
        [two, three],
        [
            [
                (0, as_columns(0, width, 0, lambda q: q * QUARTER)),
                (1, as_halves(w_value.shape[0], width * zwidth // QUARTER // 4, width)),
            ],
            [(1, as_columns(0, width, 0, lambda q: reset_at + q * QUARTER))],
        ],
        [w_value.shape, w_base.shape],
        "finish_rest",
        tokens=[t],
        into=base_grad,
    )
    input_grad = copy_out(returned, t).reshape(inputs.shape)

    tables = [grouped(table) for table in (gates, decay, beta, eta)]
    gains = small_call(riders_of(two), tables)
    return (
        output.reshape(cotangent.shape),
        input_grad,
        gains[0].reshape(width),
        gains[1].T,
        gains[2].T,
        gains[3].T,
        gains[4].T,
        gains[5].reshape(width),
        value_grad,
        base_grad,
        gains[7],
        gains[8],
        hidden_grad,
        gains[6].reshape(width),
        up_grad,
        down_grad,
    )


def solution(mesh):
    whole = P()
    placed = (
        (P("seq", None, "ch"), P("seq", "ch", None))
        + (whole,) * 14
        + (P("seq"), P("seq", None))
    )
    return jax.shard_map(
        local,
        mesh=mesh,
        in_specs=placed,
        out_specs=(P("seq", "ch", None), P("seq", None, "ch")) + (whole,) * 14,
        check_vma=False,
    )
```

```python
import math

import jax
import jax.numpy as jnp
from jax import lax
from jax.experimental import pallas as pl
from jax.experimental.pallas import tpu as pltpu
from jax.sharding import PartitionSpec as P

EPS = 1e-05
CENTER = math.sqrt(0.5)
SPREAD = math.sqrt(0.25 / math.pi)
F32 = jnp.float32
BF16 = jnp.bfloat16
NN = ((1,), (0,))
NT = ((1,), (1,))
TN = ((0,), (0,))
LANES = 128
SUBS = 8
TILE = 256
SMALL = 32
NORM_MIB = 24
FORWARD_MIB = 46
BACKWARD_MIB = 46
VMEM = pl.BlockSpec(memory_space=pltpu.VMEM)
SMEM = pl.BlockSpec(memory_space=pltpu.SMEM)
HBM = pl.BlockSpec(memory_space=pltpu.HBM)


def params(mib):
    return pltpu.CompilerParams(vmem_limit_bytes=mib << 20)


def ordered_call(kernel, tokens, *, in_specs, prefetch=0, grid=None, out_specs, scratch_shapes=(), **rest):
    count, extra = prefetch + len(in_specs), len(tokens)

    def body(*refs):
        kernel(*refs[:count], *refs[count + extra :])

    spec = pltpu.PrefetchScalarGridSpec(
        num_scalar_prefetch=prefetch,
        grid=grid or (1,),
        in_specs=list(in_specs) + [VMEM] * extra,
        out_specs=out_specs,
        scratch_shapes=scratch_shapes,
    )
    run = pl.pallas_call(body, grid_spec=spec, **rest)
    return lambda *args: run(*args, *tokens)


def shape_of(*shape, dtype=F32):
    return jax.ShapeDtypeStruct(shape, dtype)


def split(value):
    high = value.astype(BF16)
    return high, (value - high.astype(F32)).astype(BF16)


def dot(left, right, dims):
    return lax.dot_general(left, right, (dims, ((), ())), preferred_element_type=F32)


def mm3(left, right, dims):
    return (
        dot(left[0], right[0], dims)
        + dot(left[1], right[0], dims)
        + dot(left[0], right[1], dims)
    )


def mm3_short(left, right, dims):
    (left_axis,), (right_axis,) = dims
    return dot(
        jnp.concatenate([left[0], left[1], left[0]], left_axis),
        jnp.concatenate([right[0], right[0], right[1]], right_axis),
        dims,
    )


def sigmoid(value):
    return 0.5 * jnp.tanh(0.5 * value) + 0.5


def rows_sum(value):
    return jnp.sum(value, -1, keepdims=True)


def split_kernel(*refs):
    count = len(refs) // 3
    for index in range(count):
        high, low = split(refs[index][...])
        refs[count + 2 * index][...] = high
        refs[count + 2 * index + 1][...] = low


def split_weights(weights, steps=8):
    def spec(weight):
        return pl.BlockSpec((weight.shape[0] // steps, weight.shape[1]), lambda i: (i, 0))

    out = pl.pallas_call(
        split_kernel,
        grid=(steps,),
        in_specs=[spec(w) for w in weights],
        out_specs=[spec(w) for w in weights for _ in range(2)],
        out_shape=[jax.ShapeDtypeStruct(w.shape, BF16) for w in weights for _ in range(2)],
        compiler_params=params(SMALL),
        cost_estimate=pl.CostEstimate(
            flops=4 * sum(w.size for w in weights),
            bytes_accessed=8 * sum(w.size for w in weights),
            transcendentals=0,
        ),
        name="split_weights",
    )(*weights)
    return [(out[2 * i], out[2 * i + 1]) for i in range(len(weights))]


def turned(value):
    return jnp.transpose(value, (1, 0, 2))


def take_steps(ref, g, span, t):
    rows = jnp.stack([ref[g, pl.ds(c * span + t, SUBS), :] for c in range(SUBS)])
    rows = turned(rows)
    return [rows[i] for i in range(SUBS)]


def put_steps(ref, g, span, t, values):
    rows = turned(jnp.stack(values))
    for c in range(SUBS):
        ref[g, pl.ds(c * span + t, SUBS), :] = rows[c]


def rows_of(ref, g, these):
    return [jnp.broadcast_to(ref[g, n : n + 1, :], (SUBS, LANES)) for n in these]


def tree_sum(parts):
    while len(parts) > 1:
        parts = [sum(parts[i : i + 2]) for i in range(0, len(parts), 2)]
    return parts[0]


def scan_ends(source_ref, g, keep_ref, states, span, reverse):
    keeps = rows_of(keep_ref, g, range(states))

    def steps(i, state):
        t = pl.multiple_of((span // SUBS - 1 - i if reverse else i) * SUBS, SUBS)
        fresh = take_steps(source_ref, g, span, t)
        for value in reversed(fresh) if reverse else fresh:
            state = tuple(k * s + value for k, s in zip(keeps, state))
        return state

    zero = jnp.zeros((SUBS, LANES), F32)
    return lax.fori_loop(0, span // SUBS, steps, (zero,) * states, unroll=2)


def fold_ends(ends_ref, group, chunk_keep, states, order):
    total = jnp.zeros((states, LANES), F32)
    for chunk in order:
        total = chunk_keep * total + ends_ref[group, pl.ds(chunk, states, stride=SUBS), :]
    return total


def norm_kernel(x_ref, gain_ref, keep_ref, chunk_keep_ref, normed_ref, ends_ref, final_ref):
    groups, rows, _ = x_ref.shape
    states = keep_ref.shape[1]
    span = rows // SUBS
    width = groups * LANES

    def normalise(i, carry):
        here = pl.ds(pl.multiple_of(i * LANES, LANES), LANES)
        pieces = [x_ref[g, here, :] for g in range(groups)]
        mean = rows_sum(sum(pieces)) / width
        square = rows_sum(sum(p * p for p in pieces)) / width
        scale = lax.rsqrt(square - mean * mean + EPS)
        for g in range(groups):
            normed_ref[g, here, :] = (pieces[g] - mean) * scale * gain_ref[g]
        return carry

    lax.fori_loop(0, rows // LANES, normalise, 0)
    for g in range(groups):
        ends = scan_ends(normed_ref, g, keep_ref, states, span, False)
        for n in range(states):
            ends_ref[g, n * SUBS : (n + 1) * SUBS, :] = ends[n]
        final_ref[g] = fold_ends(ends_ref, g, chunk_keep_ref[g], states, range(SUBS))


def mix_kernel(
    place_ref,
    normed_ref,
    ends_ref,
    finals_ref,
    keep_ref,
    coef_ref,
    chunk_keep_ref,
    device_keep_ref,
    omega_ref,
    total_ref,
    start_ref,
):
    groups, rows, _ = normed_ref.shape
    states = keep_ref.shape[1]
    span = rows // SUBS
    ways = finals_ref.shape[0]
    place = place_ref[0]
    for g in range(groups):
        state = jnp.zeros((states, LANES), F32)
        for d in range(ways):
            state = jnp.where(d < place, device_keep_ref[g] * state + finals_ref[d, g], state)
        for chunk in range(SUBS):
            start_ref[g, pl.ds(chunk, states, stride=SUBS), :] = state
            state = chunk_keep_ref[g] * state + ends_ref[g, pl.ds(chunk, states, stride=SUBS), :]
        keeps = rows_of(keep_ref, g, range(states))
        coefs = rows_of(coef_ref, g, range(states))
        omega = jnp.broadcast_to(omega_ref[g], (SUBS, LANES))

        def steps(i, state):
            t = pl.multiple_of(i * SUBS, SUBS)
            totals = []
            for fresh in take_steps(normed_ref, g, span, t):
                state = tuple(k * s + fresh for k, s in zip(keeps, state))
                totals.append(tree_sum([c * s for c, s in zip(coefs, state)] + [omega * fresh]))
            put_steps(total_ref, g, span, t, totals)
            return state

        first = tuple(start_ref[g, n * SUBS : (n + 1) * SUBS, :] for n in range(states))
        lax.fori_loop(0, span // SUBS, steps, first, unroll=2)


def back_ends_kernel(grad_ref, keep_ref, chunk_keep_ref, ends_ref, final_ref):
    _, rows, _ = grad_ref.shape
    states = keep_ref.shape[1]
    span = rows // SUBS
    for g in range(1):
        ends = scan_ends(grad_ref, g, keep_ref, states, span, True)
        for n in range(states):
            ends_ref[g, n * SUBS : (n + 1) * SUBS, :] = ends[n]
        final_ref[g] = fold_ends(ends_ref, g, chunk_keep_ref[g], states, reversed(range(SUBS)))


def back_kernel(
    place_ref,
    grad_ref,
    ends_ref,
    finals_ref,
    start_ref,
    normed_ref,
    part_ref,
    keep_ref,
    coef_ref,
    chunk_keep_ref,
    device_keep_ref,
    sum_ref,
    coef_grad_ref,
    keep_grad_ref,
    init_ref,
):
    _, rows, _ = grad_ref.shape
    states = keep_ref.shape[1]
    span = rows // SUBS
    ways = finals_ref.shape[0]
    place = place_ref[0]
    half = states // 2
    zero = jnp.zeros((SUBS, LANES), F32)
    for g in range(1):
        whole_g = 0
        state = jnp.zeros((states, LANES), F32)
        for d in reversed(range(ways)):
            state = jnp.where(
                d > place, device_keep_ref[whole_g] * state + finals_ref[d, whole_g], state
            )
        for chunk in reversed(range(SUBS)):
            init_ref[pl.ds(chunk, states, stride=SUBS), :] = state
            state = (
                chunk_keep_ref[whole_g] * state
                + ends_ref[whole_g, pl.ds(chunk, states, stride=SUBS), :]
            )
        for part in range(2):
            these = range(part * half, (part + 1) * half)
            keeps = rows_of(keep_ref, whole_g, these)
            coefs = rows_of(coef_ref, whole_g, these)

            def steps(i, carry):
                lam, second, coef_acc, keep_acc = carry
                t = pl.multiple_of((span // SUBS - 1 - i) * SUBS, SUBS)
                fresh = take_steps(grad_ref, g, span, t)
                source = take_steps(normed_ref, g, span, t)
                outs = [None] * SUBS
                for j in reversed(range(SUBS)):
                    keep_acc = tuple(a + v * source[j] for a, v in zip(keep_acc, second))
                    lam = tuple(k * l + fresh[j] for k, l in zip(keeps, lam))
                    coef_acc = tuple(a + l * source[j] for a, l in zip(coef_acc, lam))
                    second = tuple(l + k * v for l, k, v in zip(lam, keeps, second))
                    outs[j] = tree_sum([c * l for c, l in zip(coefs, lam)])
                rows = turned(jnp.stack(outs))
                before = part_ref if part == 0 else sum_ref
                for c in range(SUBS):
                    here = pl.ds(c * span + t, SUBS)
                    sum_ref[g, here, :] = before[g, here, :] + rows[c]
                return lam, second, coef_acc, keep_acc

            first = tuple(init_ref[n * SUBS : (n + 1) * SUBS, :] for n in these)
            nothing = (zero,) * half
            lam, second, coef_acc, keep_acc = lax.fori_loop(
                0, span // SUBS, steps, (first, nothing, nothing, nothing)
            )
            for j, n in enumerate(these):
                start = start_ref[whole_g, n * SUBS : (n + 1) * SUBS, :]
                keep_acc_n = keep_acc[j] + start * second[j]
                coef_grad_ref[g, n : n + 1, :] = jnp.sum(coef_acc[j], 0, keepdims=True)
                keep_grad_ref[g, n : n + 1, :] = jnp.sum(keep_acc_n, 0, keepdims=True)


def unnorm_kernel(
    calls,
    x_ref,
    *refs,
):
    sums, refs = refs[:calls], refs[calls:]
    direct_ref, gain_ref, refs = refs[0], refs[1], refs[2:]
    coefs, keeps, refs = refs[:calls], refs[calls : 2 * calls], refs[2 * calls :]
    omega_ref, ffn_ref, qk_ref, out_ref, small_ref, gain_grad = refs
    groups, rows, _ = x_ref.shape
    width = groups * LANES
    share = groups // calls
    tile = pl.program_id(0)

    @pl.when(tile == 0)
    def _():
        gain_grad[...] = jnp.zeros_like(gain_grad)

    pieces = [x_ref[g] for g in range(groups)]
    mean = rows_sum(sum(pieces)) / width
    square = rows_sum(sum(p * p for p in pieces)) / width
    scale = lax.rsqrt(square - mean * mean + EPS)
    centered = [(p - mean) * scale for p in pieces]
    grads = [sums[g // share][g % share] for g in range(groups)]
    for g in range(groups):
        gain_grad[g : g + 1, :] += jnp.sum(grads[g] * centered[g], 0, keepdims=True)
    scaled = [grads[g] * gain_ref[g] for g in range(groups)]
    plain = rows_sum(sum(scaled)) / width
    cross = rows_sum(sum(s * c for s, c in zip(scaled, centered))) / width
    for g in range(groups):
        out_ref[g] = direct_ref[g] + scale * (scaled[g] - plain - centered[g] * cross)

    @pl.when(tile == pl.num_programs(0) - 1)
    def _():
        states = coefs[0].shape[1]
        for i, refs in enumerate((coefs, keeps)):
            for g in range(groups):
                at = slice(g * states, (g + 1) * states)
                small_ref[at, i * LANES : (i + 1) * LANES] = refs[g // share][g % share]
        at = groups * states
        small_ref[at:, :] = jnp.zeros((small_ref.shape[0] - at, 2 * LANES), F32)
        small_ref[at : at + groups, :LANES] = gain_grad[:groups]
        for g in range(groups):
            here = slice(at + groups + g, at + groups + g + 1)
            small_ref[here, :LANES] = omega_ref[g]
            small_ref[here, LANES:] = ffn_ref[:, g * LANES : (g + 1) * LANES]
        small_ref[at : at + 4, LANES:] = qk_ref[0:4, :]


def group_spec(array, lowest=0):
    axis = array.ndim - 3
    block = array.shape[:axis] + (1,) + array.shape[axis + 1 :]
    return pl.BlockSpec(block, lambda g: (0,) * axis + (lowest + g, 0, 0))


def scan_call(kernel, name, scalars, arrays, outs, tokens=(), lowest=0, count=None, scratch=(), work=4):
    count = count or arrays[0].shape[-3]
    states, rows = outs[-1].shape[-2], arrays[0].shape[-2]
    return ordered_call(
        kernel,
        tokens,
        grid=(count,),
        in_specs=[SMEM] * len(scalars) + [group_spec(v, lowest) for v in arrays],
        out_specs=[group_spec(v) for v in outs],
        scratch_shapes=scratch,
        out_shape=outs,
        compiler_params=params(SMALL),
        cost_estimate=pl.CostEstimate(
            flops=work * rows * count * LANES * 16,
            bytes_accessed=12 * rows * count * LANES,
            transcendentals=0,
        ),
        name=name,
    )(*scalars, *arrays)


def back_call(lowest, count, place_info, grad4, ends, finals, starts, normed4, part4, tables, tokens):
    rows, states = grad4.shape[1], starts.shape[1] // SUBS
    arrays = [grad4, ends, finals, starts, normed4, part4, *tables]
    outs = [shape_of(count, rows, LANES)] + [shape_of(count, states, LANES)] * 2
    return scan_call(
        back_kernel,
        "back",
        [place_info],
        arrays,
        outs,
        tokens,
        lowest,
        count,
        [pltpu.VMEM((states * SUBS, LANES), F32)],
        10,
    )


def unnorm_call(x4, sums, direct4, gain4, coefs, keeps, omega, ffn, qk, tokens):
    groups, rows, _ = x4.shape
    states = coefs[0].shape[1]
    by_group = pl.BlockSpec((groups, TILE, LANES), lambda i: (0, i, 0))
    halves = [pl.BlockSpec((s.shape[0], TILE, LANES), lambda i: (0, i, 0)) for s in sums]
    height = -(-(groups * states + 2 * groups) // 16) * 16
    return ordered_call(
        lambda *refs: unnorm_kernel(len(sums), *refs),
        tokens,
        grid=(rows // TILE,),
        in_specs=[by_group] + halves + [by_group] + [VMEM] * (4 + 2 * len(sums)),
        out_specs=[by_group, pl.BlockSpec((height, 2 * LANES), lambda i: (0, 0))],
        out_shape=[shape_of(*x4.shape), shape_of(height, 2 * LANES)],
        scratch_shapes=[pltpu.VMEM((SUBS, LANES), F32)],
        compiler_params=params(SMALL),
        cost_estimate=pl.CostEstimate(
            flops=20 * x4.size, bytes_accessed=16 * x4.size, transcendentals=0
        ),
        name="unnorm",
    )(x4, *sums, direct4, gain4, *coefs, *keeps, *omega, ffn, *qk)


def small_kernel(
    part_a,
    part_b,
    part_c,
    part_d,
    gate_ref,
    decay_ref,
    beta_ref,
    eta_ref,
    gain_out,
    delta_out,
    alpha_out,
    beta_out,
    eta_out,
    omega_out,
    ffn_out,
    scale_out,
    shift_out,
):
    groups, states, _ = gate_ref.shape
    root = math.sqrt(states)
    at = groups * states
    height = -(-(groups * states + 2 * groups) // 16) * 16
    tails = [ref[ref.shape[0] - height :, :] for ref in (part_a, part_b, part_c, part_d)]
    total = (tails[0] + tails[1]) + (tails[2] + tails[3])
    for g in range(groups):
        here = slice(g * states, (g + 1) * states)
        coef, keep = total[here, :LANES], total[here, LANES:]
        gate, decay, beta, eta = gate_ref[g], decay_ref[g], beta_ref[g], eta_ref[g]
        keep = keep * gate * beta * (eta / root)
        gate_grad = coef * beta * (eta / root) - keep * decay
        lanes = slice(g * LANES, (g + 1) * LANES)
        delta_out[:, lanes] = gate_grad * gate * (1.0 - gate)
        alpha_out[:, lanes] = -keep * gate * decay * (1.0 - decay)
        beta_out[:, lanes] = coef * gate * (eta / root)
        eta_out[:, lanes] = coef * gate * beta / root
    gain_out[...] = total[at : at + groups, :LANES]
    omega_out[...] = total[at + groups : at + 2 * groups, :LANES]
    ffn_out[...] = total[at + groups : at + 2 * groups, LANES:]
    scale_out[...] = total[at : at + 2, LANES:]
    shift_out[...] = total[at + 2 : at + 4, LANES:]


def small_call(parts, tables):
    groups, states, _ = tables[0].shape
    row, table = shape_of(groups, LANES), shape_of(states, groups * LANES)
    two = shape_of(2, LANES)
    return pl.pallas_call(
        small_kernel,
        in_specs=[VMEM] * 8,
        out_specs=[VMEM] * 9,
        out_shape=[row, table, table, table, table, row, row, two, two],
        compiler_params=params(SMALL),
        name="small_grads",
    )(*parts, *tables)


QUARTER = 256
EVERY = slice(None)


def columns(total, step=512):
    return [slice(i, min(i + step, total)) for i in range(0, total, step)]


def joined(ref):
    return jnp.concatenate([ref[g] for g in range(ref.shape[0])], 1)


def silu_slope(act, gate):
    return gate + act * (1.0 - gate)


class Attention:
    def __init__(self, z, scale_ref, shift_ref, mask_ref, base_row, length):
        rows, span = z.shape[0], mask_ref.shape[1]
        blocks = rows // span
        self.query = split(z * scale_ref[0:1, :] + shift_ref[0:1, :])
        self.key = split(z * scale_ref[1:2, :] + shift_ref[1:2, :])
        lane = lax.broadcasted_iota(jnp.int32, (1, span), 1)
        valids, counts = [], []
        for b in range(blocks):
            position = base_row + b * span + lane
            last_block = (base_row + b * span) // span == (length - 1) // span
            kept = (position < length) & (jnp.logical_not(last_block) | (mask_ref[...] == 1))
            valid = jnp.where(kept, 1.0, 0.0)
            count = jnp.maximum(rows_sum(valid), 1.0)
            valids.append(valid)
            counts.append(jnp.broadcast_to(count, (1, span)))
        row = lax.broadcasted_iota(jnp.int32, (rows, rows), 0)
        column = lax.broadcasted_iota(jnp.int32, (rows, rows), 1)
        near = (row >= column) & (row // span == column // span)
        self.mask = jnp.where(near, jnp.concatenate(valids, 1), 0.0)
        self.count = jnp.concatenate(counts, 1)
        self.spot = mm3_short(self.query, self.key, NT) / self.count - CENTER

    def weight(self):
        curve = lax.erf(self.spot * (1.0 / (SPREAD * math.sqrt(2.0))))
        return split((0.5 + 0.5 * curve) * self.mask)

    def slope(self):
        return (
            jnp.exp(self.spot * self.spot * (-1.0 / (2.0 * SPREAD * SPREAD)))
            * (self.mask / self.count)
            * (1.0 / (SPREAD * math.sqrt(2.0 * math.pi)))
        )


def add_to(total_ref, quarter, at, pieces, first):
    for piece in pieces:
        here = slice(at, at + piece.shape[0])
        at += piece.shape[0]
        total_ref[quarter, here, :] = jnp.where(first, 0.0, total_ref[quarter, here, :]) + piece
    return at


def packed_rows(value):
    return [value[:, i : i + QUARTER] for i in range(0, value.shape[1], QUARTER)]


class Fetch:
    def __init__(self, sources, targets, sems, first):
        self.first = first
        self.copies = [
            pltpu.make_async_copy(source, target, sems.at[i])
            for i, (source, target) in enumerate(zip(sources, targets))
        ]

        @pl.when(first)
        def _():
            for copy in self.copies:
                copy.start()

    def wait(self, *which):
        @pl.when(self.first)
        def _():
            for i in which:
                self.copies[i].wait()


class HandOut:
    def __init__(self, own, total, send, keep, row, sems, last):
        self.own, self.total, self.send, self.keep = own, total, send, keep
        self.rows = pl.ds(row, total.shape[1])
        self.sems, self.last = sems, last

    def each(self, quarter, act):
        apart = quarter ^ self.own

        @pl.when(self.last & (apart >= 2))
        def _():
            act(
                pltpu.make_async_copy(
                    self.total.at[quarter], self.send.at[3 - apart, self.rows], self.sems.at[quarter]
                )
            )

        @pl.when(self.last & (apart < 2))
        def _():
            act(
                pltpu.make_async_copy(
                    self.total.at[quarter], self.keep.at[1 - apart, self.rows], self.sems.at[quarter]
                )
            )

    def start(self, quarter):
        self.each(quarter, lambda copy: copy.start())

    def wait(self):
        for quarter in range(4):
            self.each(quarter, lambda copy: copy.wait())


def forward_kernel(
    info_ref,
    place_ref,
    mask_ref,
    x_ref,
    normed_ref,
    total_ref,
    cot_ref,
    scale_ref,
    shift_ref,
    gain_ref,
    wv_h,
    wv_l,
    wb_h,
    wb_l,
    wh_h,
    wh_l,
    wu_h,
    wu_l,
    wd_h,
    wd_l,
    out_ref,
    direct_ref,
    v_h,
    v_l,
    vsil,
    rst,
    attr,
    weight_h,
    weight_l,
    slope_ref,
    zpre,
    grad_u_ref,
    grad_h_ref,
    gain_grad_ref,
    send_a,
    keep_a,
    send_b,
    keep_b,
    upd,
    hpre,
    gr_h,
    gr_l,
    a_h,
    a_l,
    usil,
    du_h,
    du_l,
    acc_a,
    acc_b,
    sems_a,
    sems_b,
):
    tile = pl.program_id(0)
    first = tile == 0
    groups, rows, _ = x_ref.shape
    width = groups * LANES
    zwidth = scale_ref.shape[1]
    values = wv_h.shape[1]
    units = wu_h.shape[1]
    base_row, length = info_ref[0] + tile * rows, info_ref[1]
    last = tile == pl.num_programs(0) - 1
    out_a = HandOut(place_ref[0], acc_a, send_a, keep_a, 0, sems_a, last)
    out_b = HandOut(place_ref[1], acc_b, send_b, keep_b, 0, sems_b, last)

    @pl.when(first)
    def _():
        gain_grad_ref[...] = jnp.zeros_like(gain_grad_ref)

    def put(high_ref, low_ref, where, value):
        high, low = split(value)
        high_ref[where] = high
        low_ref[where] = low
        return high, low

    n_pair = split(joined(normed_ref))
    total = joined(total_ref)
    m_pair = split(total * sigmoid(total))
    for c in columns(values):
        pre = mm3(n_pair, (wv_h[:, c], wv_l[:, c]), NN)
        s = sigmoid(pre)
        act = pre * s
        put(v_h, v_l, (EVERY, c), act)
        vsil[:, c] = silu_slope(act, s)
    c = slice(width, width + zwidth)
    pre = mm3(m_pair, (wb_h[:, c], wb_l[:, c]), NN)
    zpre[...] = pre
    attention = Attention(
        pre * sigmoid(pre), scale_ref, shift_ref, mask_ref, base_row, length
    )
    c = slice(0, width)
    upd[...] = sigmoid(mm3(m_pair, (wb_h[:, c], wb_l[:, c]), NN))
    for c in columns(values):
        w = slice(width + zwidth + c.start, width + zwidth + c.stop)
        pre = mm3(m_pair, (wb_h[:, w], wb_l[:, w]), NN)
        s = sigmoid(pre)
        act = pre * s
        rst[:, c] = act
        attr[:, c] = silu_slope(act, s)
    w = slice(width + zwidth + values, width + zwidth + values + width)
    hpre[...] = mm3(m_pair, (wb_h[:, w], wb_l[:, w]), NN)
    weight = attention.weight()
    weight_h[...], weight_l[...] = weight
    slope_ref[...] = attention.slope()
    for c in columns(values):
        got = mm3(weight, (v_h[:, c], v_l[:, c]), NN)
        put(gr_h, gr_l, (EVERY, c), got * rst[:, c])
        attr[:, c] = got * attr[:, c]
    pre = hpre[...] + mm3((gr_h[...], gr_l[...]), (wh_h[...], wh_l[...]), NN)
    s = sigmoid(pre)
    hidden = pre * s
    hpre[...] = silu_slope(hidden, s)
    x = joined(x_ref)
    update = upd[...]
    apart = hidden - x
    gated = x + update * apart
    mean = rows_sum(gated) / width
    square = rows_sum(gated * gated) / width
    scale = lax.rsqrt(square - mean * mean + EPS)
    centered = (gated - mean) * scale
    f_pair = split(centered * gain_ref[...])
    for c in columns(units):
        pre = mm3(f_pair, (wu_h[:, c], wu_l[:, c]), NN)
        s = sigmoid(pre)
        act = pre * s
        put(a_h, a_l, (EVERY, c), act)
        usil[:, c] = silu_slope(act, s)
    live = (base_row + lax.broadcasted_iota(jnp.int32, (rows, 1), 0) < length).astype(F32)
    out_ref[...] = (gated + mm3((a_h[...], a_l[...]), (wd_h[...], wd_l[...]), NN)) * live

    grad_out = cot_ref[...] * live
    do_pair = split(grad_out)
    for c in columns(units):
        put(du_h, du_l, (EVERY, c), mm3(do_pair, (wd_h[c, :], wd_l[c, :]), NT) * usil[:, c])
    grad_f = mm3((du_h[...], du_l[...]), (wu_h[...], wu_l[...]), NT)
    gain_grad_ref[...] += jnp.sum(grad_f * centered, 0, keepdims=True)
    scaled = grad_f * gain_ref[...]
    grad_gated = grad_out + scale * (
        scaled - rows_sum(scaled) / width - centered * (rows_sum(scaled * centered) / width)
    )
    grad_u = grad_gated * apart * update * (1.0 - update)
    grad_u_ref[...] = grad_u
    u_pair = split(grad_u)
    grad_h = grad_gated * update * hpre[...]
    grad_h_ref[...] = grad_h
    h_pair = split(grad_h)
    direct = grad_gated * (1.0 - update)
    for g in range(groups):
        direct_ref[g] = direct[:, g * LANES : (g + 1) * LANES]
    for q in range(0, 4, 2):
        c = slice(q * QUARTER, (q + 2) * QUARTER)
        up = mm3(f_pair, (du_h[:, c], du_l[:, c]), TN)
        rest = mm3(m_pair, u_pair if q == 0 else h_pair, TN)
        down = mm3((a_h[:, c], a_l[:, c]), do_pair, TN)
        hid = mm3((gr_h[:, c], gr_l[:, c]), h_pair, TN)
        for i in range(2):
            c = slice(i * QUARTER, (i + 1) * QUARTER)
            at = add_to(acc_a, q + i, 0, [up[:, c]], first)
            add_to(acc_a, q + i, at, [rest[:, c]], first)
            at = add_to(acc_b, q + i, 0, packed_rows(down[c]), first)
            add_to(acc_b, q + i, at, packed_rows(hid[c]), first)
            out_a.start(q + i)
            out_b.start(q + i)
    out_a.wait()
    out_b.wait()


def backward_kernel(
    continued,
    place_ref,
    normed_ref,
    total_ref,
    v_h,
    v_l,
    vsil,
    rst,
    attr,
    weight_h,
    weight_l,
    slope_ref,
    zpre,
    grad_u_ref,
    grad_h_ref,
    scale_ref,
    shift_ref,
    omega_ref,
    wh_h,
    wh_l,
    wv_h_hbm,
    wv_l_hbm,
    wb_h_hbm,
    wb_l_hbm,
    *refs,
):
    (
        grad_ref,
        part_ref,
        qk_grad_ref,
        omega_grad_ref,
        send_ref,
        keep_ref,
        da_h,
        da_l,
        dv_h,
        dv_l,
        bz_h,
        bz_l,
        br_h,
        br_l,
        acc_b,
        acc_c,
        wv_h,
        wv_l,
        wb_h,
        wb_l,
        sems_b,
        sems_c,
        weight_sems,
    ) = refs[2 if continued else 0 :]
    tile = pl.program_id(0)
    first, last = tile == 0, tile == pl.num_programs(0) - 1
    groups = normed_ref.shape[0]
    width = groups * LANES
    zwidth = scale_ref.shape[1]
    values = vsil.shape[1]
    fetch = Fetch(
        [wv_h_hbm, wv_l_hbm, wb_h_hbm, wb_l_hbm],
        [wv_h, wv_l, wb_h, wb_l],
        weight_sems,
        first,
    )
    out_b = HandOut(place_ref[0], acc_b, send_ref, keep_ref, 0, sems_b, last)
    out_c = HandOut(place_ref[1], acc_c, send_ref, keep_ref, acc_b.shape[1], sems_c, last)

    @pl.when(first)
    def _():
        qk_grad_ref[...] = jnp.zeros_like(qk_grad_ref)
        omega_grad_ref[...] = jnp.zeros_like(omega_grad_ref)

    def put(high_ref, low_ref, where, value):
        high, low = split(value)
        high_ref[where] = high
        low_ref[where] = low

    u_pair = split(grad_u_ref[...])
    h_pair = split(grad_h_ref[...])
    for c in columns(values):
        got = mm3(h_pair, (wh_h[c, :], wh_l[c, :]), NT)
        put(da_h, da_l, (EVERY, c), got * rst[:, c])
        put(br_h, br_l, (EVERY, c), got * attr[:, c])
    pre = zpre[...]
    s = sigmoid(pre)
    z = pre * s
    zsil = silu_slope(z, s)
    query = split(z * scale_ref[0:1, :] + shift_ref[0:1, :])
    key = split(z * scale_ref[1:2, :] + shift_ref[1:2, :])
    weight = (weight_h[...], weight_l[...])
    grad_scores = split(mm3((da_h[...], da_l[...]), (v_h[...], v_l[...]), NT) * slope_ref[...])
    for c in columns(values):
        got = mm3(weight, (da_h[:, c], da_l[:, c]), TN)
        put(dv_h, dv_l, (EVERY, c), got * vsil[:, c])
    grad_q = mm3(grad_scores, key, NN)
    grad_k = mm3(grad_scores, query, TN)
    qk_grad_ref[0:1, :] += jnp.sum(grad_q * z, 0, keepdims=True)
    qk_grad_ref[1:2, :] += jnp.sum(grad_k * z, 0, keepdims=True)
    qk_grad_ref[2:3, :] += jnp.sum(grad_q, 0, keepdims=True)
    qk_grad_ref[3:4, :] += jnp.sum(grad_k, 0, keepdims=True)
    put(
        bz_h,
        bz_l,
        (EVERY, EVERY),
        (grad_q * scale_ref[0:1, :] + grad_k * scale_ref[1:2, :]) * zsil,
    )

    n_pair = split(joined(normed_ref))
    total = joined(total_ref)
    gate_here = sigmoid(total)
    mixed = total * gate_here
    m_pair = split(mixed)
    grad_bz = mm3(m_pair, (bz_h[...], bz_l[...]), TN)
    for q in range(0, 4, 2):
        c = slice(q * QUARTER, (q + 2) * QUARTER)
        value = mm3(n_pair, (dv_h[:, c], dv_l[:, c]), TN)
        reset = mm3(m_pair, (br_h[:, c], br_l[:, c]), TN)
        for i in range(2):
            c = slice(i * QUARTER, (i + 1) * QUARTER)
            at = add_to(acc_b, q + i, 0, [value[:, c]], first)
            got = grad_bz[(q + i) * width // 4 : (q + i + 1) * width // 4]
            half = got.shape[0] // 2
            add_to(acc_b, q + i, at, [jnp.concatenate([got[:half], got[half:]], 1)], first)
            add_to(acc_c, q + i, 0, [reset[:, c]], first)
            out_b.start(q + i)
            out_c.start(q + i)

    fetch.wait(0, 1, 2, 3)
    grad_n = mm3((dv_h[...], dv_l[...]), (wv_h[...], wv_l[...]), NT)
    at = [0, width, width + zwidth, width + zwidth + values, 2 * width + zwidth + values]
    w = [slice(i, j) for i, j in zip(at[:-1], at[1:])]
    grad = (
        mm3(u_pair, (wb_h[:, w[0]], wb_l[:, w[0]]), NT)
        + mm3_short((bz_h[...], bz_l[...]), (wb_h[:, w[1]], wb_l[:, w[1]]), NT)
        + mm3((br_h[...], br_l[...]), (wb_h[:, w[2]], wb_l[:, w[2]]), NT)
        + mm3(h_pair, (wb_h[:, w[3]], wb_l[:, w[3]]), NT)
    ) * silu_slope(mixed, gate_here)
    for g in range(groups):
        lanes = slice(g * LANES, (g + 1) * LANES)
        got = grad[:, lanes]
        grad_ref[g] = got
        part_ref[g] = grad_n[:, lanes] + got * omega_ref[g]
        omega_grad_ref[g] += jnp.sum(got * normed_ref[g], 0, keepdims=True)
    out_b.wait()
    out_c.wait()


def by_row(count, lowest=0):
    return pl.BlockSpec((TILE, count), lambda i: (lowest + i, 0))


def forward_call(info, place, key_mask, x4, normed4, total4, cot, qk_scale, qk_shift, ffn_gain, pairs, heights):
    groups, rows, _ = x4.shape
    width = groups * LANES
    wv, wb, wh, wu, wd = pairs
    values, units, zwidth = wv[0].shape[1], wu[0].shape[1], qk_scale.shape[1]
    flat = [part for pair in pairs for part in pair]
    by_group = pl.BlockSpec((groups, TILE, LANES), lambda i: (0, i, 0))
    macs = rows * (wv[0].size + wb[0].size + wh[0].size + 3 * wu[0].size + 3 * wd[0].size)
    return pl.pallas_call(
        forward_kernel,
        grid=(rows // TILE,),
        in_specs=[SMEM, SMEM, VMEM, by_group, by_group, by_group, by_row(width)]
        + [VMEM] * (3 + len(flat)),
        out_specs=[
            by_row(width),
            by_group,
            by_row(values),
            by_row(values),
            by_row(values),
            by_row(values),
            by_row(values),
            by_row(TILE),
            by_row(TILE),
            by_row(TILE),
            by_row(zwidth),
            by_row(width),
            by_row(width),
            pl.BlockSpec((1, width), lambda i: (0, 0)),
            HBM,
            HBM,
            HBM,
            HBM,
        ],
        out_shape=[
            shape_of(rows, width),
            shape_of(groups, rows, LANES),
            shape_of(rows, values, dtype=BF16),
            shape_of(rows, values, dtype=BF16),
            shape_of(rows, values),
            shape_of(rows, values),
            shape_of(rows, values),
            shape_of(rows, TILE, dtype=BF16),
            shape_of(rows, TILE, dtype=BF16),
            shape_of(rows, TILE),
            shape_of(rows, zwidth),
            shape_of(rows, width),
            shape_of(rows, width),
            shape_of(1, width),
        ]
        + [shape_of(2, height, QUARTER) for height in heights for _ in range(2)],
        scratch_shapes=[
            pltpu.VMEM((TILE, width), F32),
            pltpu.VMEM((TILE, width), F32),
            pltpu.VMEM((TILE, values), BF16),
            pltpu.VMEM((TILE, values), BF16),
            pltpu.VMEM((TILE, units), BF16),
            pltpu.VMEM((TILE, units), BF16),
            pltpu.VMEM((TILE, units), F32),
            pltpu.VMEM((TILE, units), BF16),
            pltpu.VMEM((TILE, units), BF16),
        ]
        + [pltpu.VMEM((4, height, QUARTER), F32) for height in heights]
        + [pltpu.SemaphoreType.DMA((4,))] * 2,
        compiler_params=params(FORWARD_MIB),
        cost_estimate=pl.CostEstimate(flops=6 * macs, bytes_accessed=48 << 20, transcendentals=0),
        name="forward",
    )(info, place, key_mask, x4, normed4, total4, cot, qk_scale, qk_shift, ffn_gain, *flat)


def backward_call(
    place, normed4, total4, saved, qk_scale, qk_shift, omega4, pairs, heights, lowest, tiles, before, tokens
):
    groups, rows, _ = normed4.shape
    width = groups * LANES
    wv, wb, wh = pairs[:3]
    values, zwidth = wv[0].shape[1], qk_scale.shape[1]
    by_group = pl.BlockSpec((groups, TILE, LANES), lambda i: (0, lowest + i, 0))
    fetched = [*wv, *wb]
    args = [place, normed4, total4, *saved, qk_scale, qk_shift, omega4, *wh, *fetched]
    quarters = [shape_of(2, sum(heights), QUARTER)] * 2
    return ordered_call(
        lambda *refs: backward_kernel(bool(before), *refs),
        tokens,
        grid=(tiles,),
        in_specs=[SMEM, by_group, by_group]
        + [by_row(s.shape[1], lowest) for s in saved]
        + [VMEM] * (3 + len(wh))
        + [HBM] * (len(fetched) + len(before)),
        out_specs=[
            by_group,
            by_group,
            pl.BlockSpec((8, zwidth), lambda i: (0, 0)),
            pl.BlockSpec((groups, 1, LANES), lambda i: (0, 0, 0)),
        ]
        + [HBM] * 2,
        out_shape=[
            shape_of(groups, rows, LANES),
            shape_of(groups, rows, LANES),
            shape_of(8, zwidth),
            shape_of(groups, 1, LANES),
        ]
        + quarters,
        input_output_aliases={len(args): 0, len(args) + 1: 1} if before else {},
        scratch_shapes=[pltpu.VMEM((TILE, values), BF16)] * 4
        + [pltpu.VMEM((TILE, zwidth), BF16)] * 2
        + [pltpu.VMEM((TILE, values), BF16)] * 2
        + [pltpu.VMEM((4, height, QUARTER), F32) for height in heights]
        + [pltpu.VMEM(w.shape, BF16) for w in fetched]
        + [pltpu.SemaphoreType.DMA((4,))] * 2
        + [pltpu.SemaphoreType.DMA((len(fetched),))],
        compiler_params=params(BACKWARD_MIB),
        cost_estimate=pl.CostEstimate(
            flops=12 * tiles * TILE * (wv[0].size + wb[0].size + wh[0].size),
            bytes_accessed=40 << 20,
            transcendentals=0,
        ),
        name="backward",
    )(*args, *before)


def swap(value, step):
    axis, distance = step
    size = lax.axis_size(axis)
    return lax.ppermute(value, axis, [(i, i ^ distance) for i in range(size)])


def side(step):
    axis, distance = step
    return (lax.axis_index(axis) // distance) % 2


def device_steps():
    def bits(axis):
        size = lax.axis_size(axis)
        return [(axis, 1 << i) for i in range(size.bit_length() - 1)]

    return bits("ch"), bits("seq")


def orders():
    ch, seq = device_steps()
    x, y, z, rest = ch[1:], seq[:1], seq[1:2], seq[2:]
    out = [
        y + z + x + rest,
        z + y + x + rest,
        z + y + x + rest,
        y + z + x + rest,
    ]
    back = [
        rest[::-1] + z + x + y,
        rest[::-1] + x + y + z,
        rest[::-1] + y + z + x,
        rest[::-1] + z + y + x,
    ]
    return [(ch[:1] + go, come + ch[:1]) for go, come in zip(out, back)]


TOKEN = shape_of(SUBS, LANES)


def gate(value, token):
    return lax.optimization_barrier((value, token))


def halve_kernel(count, first, own_ref, *refs):
    own = own_ref[0]
    parts, (send_ref, next_ref, token_ref) = refs[:count], refs[count:]
    rows = pl.ds(first, send_ref.shape[0])
    send_ref[...] = sum(part[1 - own, rows, :] for part in parts)
    next_ref[...] = sum(part[own, rows, :] for part in parts)
    token_ref[...] = jnp.zeros_like(token_ref)


def halve(parts, window, own, tokens):
    width = parts[0].shape[-1]
    height = parts[0].size // width // 2
    first, rows = window or (0, height)
    parts = [part.reshape(2, height, width) for part in parts]
    return ordered_call(
        lambda *refs: halve_kernel(len(parts), first, *refs),
        tokens,
        in_specs=[SMEM] + [VMEM] * len(parts),
        out_specs=[VMEM] * 3,
        out_shape=[shape_of(rows, width)] * 2 + [TOKEN],
        compiler_params=params(SMALL),
        cost_estimate=pl.CostEstimate(
            flops=2 * rows * width, bytes_accessed=1 << 10, transcendentals=0
        ),
        name="halve",
    )(own.reshape(1), *parts)


def add_kernel(left_ref, right_ref, out_ref, token_ref):
    out_ref[...] = left_ref[...] + right_ref[...]
    token_ref[...] = jnp.zeros_like(token_ref)


def add(left, right, tokens):
    return ordered_call(
        add_kernel,
        tokens,
        in_specs=[VMEM] * 2,
        out_specs=[VMEM] * 2,
        out_shape=[shape_of(*left.shape), TOKEN],
        compiler_params=params(SMALL),
        cost_estimate=pl.CostEstimate(flops=left.size, bytes_accessed=1 << 10, transcendentals=0),
        name="add",
    )(left, right)


def gather_kernel(counts, riders, *refs):
    parts, refs = refs[: len(counts)], refs[len(counts) :]
    out_ref, token_ref = refs[-2:]
    at = 0
    for part, rows in zip(parts, counts):
        out_ref[at : at + rows, :] = part[:rows, :]
        at += rows
    if riders:
        tails = [ref[ref.shape[0] - riders :, :] for ref in refs[:-2]]
        out_ref[at:, :] = sum(tails)
    token_ref[...] = jnp.zeros_like(token_ref)


def gather_parts(parts, counts, riders, rider_rows, tokens):
    total, width = sum(counts), parts[0].shape[1]
    shape = shape_of(total + (rider_rows if riders else 0), width)
    return ordered_call(
        lambda *refs: gather_kernel(counts, rider_rows if riders else 0, *refs),
        tokens,
        in_specs=[VMEM] * (len(parts) + len(riders)),
        out_specs=[VMEM] * 2,
        out_shape=[shape, TOKEN],
        compiler_params=params(SMALL),
        cost_estimate=pl.CostEstimate(flops=0, bytes_accessed=1 << 10, transcendentals=0),
        name="gather_parts",
    )(*parts, *riders)


def finish_kernel(plans, maps, given, outs_count, *refs):
    pieces = len(plans)
    places, refs = refs[:pieces], refs[pieces:]
    quarters, refs = refs[: 4 * pieces], refs[4 * pieces :]
    outs, refs = refs[given : given + outs_count], refs[given + outs_count :]
    token_ref, refs = refs[0], refs[1:]
    token_ref[...] = jnp.zeros_like(token_ref)
    scratch, sems = refs[:pieces], refs[pieces:]
    leave = []
    for p, plan in enumerate(plans):
        place_ref, out_sems = places[p], sems[p]
        bits = place_ref.shape[0] - 1
        blocks = 1 << bits
        rows = scratch[p].shape[1] // blocks
        relative = place_ref[1]
        for bit in range(1, bits):
            relative = relative * 2 + place_ref[1 + bit]
        for i in range(4):
            for r in range(blocks):
                quarter, k = maps[p](i, r)
                target = pl.ds(pl.multiple_of((relative ^ k) * rows, SUBS), rows)
                scratch[p][quarter, target, :] = quarters[4 * p + i][r * rows : (r + 1) * rows, :]
        for i in range(4):
            quarter = place_ref[0] ^ i
            number = 0
            for out, moves in plan:
                for row, count, column, width, out_row, out_column in moves(quarter):
                    copy = pltpu.make_async_copy(
                        scratch[p].at[i, pl.ds(row, count), pl.ds(column, width)],
                        outs[out].at[pl.ds(out_row, count), pl.ds(out_column, width)],
                        out_sems.at[i, number],
                    )
                    copy.start()
                    leave.append(copy)
                    number += 1
    for copy in leave:
        copy.wait()


def aligned(value, step):
    return pl.multiple_of(value, step)


def as_columns(first, rows, out_row, out_column):
    return lambda q: [(first, rows, 0, QUARTER, out_row, aligned(out_column(q), LANES))]


def as_rows(first, rows, start, stop):
    def moves(q):
        return [
            (first + (c - start) // QUARTER * rows, rows, 0, QUARTER, aligned(q * rows, SUBS), c)
            for c in range(start, stop, QUARTER)
        ]

    return moves


def as_halves(first, rows, out_column):
    def moves(q):
        at = q * (2 * rows)
        return [
            (first, rows, 0, LANES, aligned(at, SUBS), out_column),
            (first, rows, LANES, LANES, aligned(at + rows, SUBS), out_column),
        ]

    return moves


def finish(pieces, plans, shapes, name, tokens=(), into=None):
    args = [v for piece in pieces for v in piece.pair + list(piece.got)]
    places = [piece.place for piece in pieces]
    scratch = [pltpu.VMEM((4,) + piece.quarter_shape(), F32) for piece in pieces]
    sems = []
    for piece, plan in zip(pieces, plans):
        number = sum(len(moves(0)) for _, moves in plan)
        sems.append(pltpu.SemaphoreType.DMA((4, number)))
    extra = [] if into is None else [into]
    return ordered_call(
        lambda *refs: finish_kernel(plans, [p.quarter_and_block for p in pieces], len(extra), len(shapes), *refs),
        tokens,
        in_specs=[SMEM] * len(places) + [VMEM] * len(args) + [HBM] * len(extra),
        out_specs=[HBM] * len(shapes) + [VMEM],
        input_output_aliases={len(places) + len(args): len(shapes) - 1} if extra else {},
        out_shape=[shape_of(*shape) for shape in shapes] + [TOKEN],
        scratch_shapes=scratch + sems,
        compiler_params=params(SMALL),
        cost_estimate=pl.CostEstimate(
            flops=0, bytes_accessed=1 << 10, transcendentals=0
        ),
        name=name,
    )(*places, *args, *extra)


class Piece:
    def __init__(self, plan, back):
        self.plan, self.back = plan, back
        self.sides = [side(step).astype(jnp.int32) for step in plan]
        first, second = self.sides[0], self.sides[1]

        def quarter(a, b):
            return 2 * a + b

        self.own_quarter = quarter(first, second).reshape(1)
        self.place = jnp.concatenate([self.own_quarter, jnp.stack(self.sides[2:])])
        self.rider, self.waiting = None, []
        self.at, self.steps = 1, 2 * len(plan)

    def quarter_and_block(self, array, row):
        apart = {step: (row >> i) & 1 for i, step in enumerate(self.back[:-2])}
        apart[self.back[-2]] = array % 2
        block = 0
        for step in self.plan[2:]:
            block = 2 * block + apart[step]
        return 2 * (array // 2) + apart[self.plan[1]], block

    def quarter_shape(self):
        return (self.pair[0].shape[0] - (0 if self.rider is None else self.rider.shape[0]), QUARTER)

    def step(self, *tokens):
        last = len(self.plan)
        if self.at < last:
            own = self.sides[self.at] if self.at > 1 else jnp.ones((), jnp.int32)
            send, self.own, token = halve(self.waiting, self.window if self.at == 1 else None, own, tokens)
            self.got = swap(send, self.plan[self.at])
            self.waiting = [self.own, self.got]
            self.at += 1
            return token
        if self.at == last:
            total, token = add(self.own, self.got, tokens)
            self.parts = [total]
            self.riders = [] if self.rider is None else [self.rider]
        else:
            self.parts.append(self.got)
            if self.rider is not None:
                self.riders = [self.whole, self.got]
        index = self.at - last
        self.at += 1
        if index < last - 1:
            rows = self.parts[0].shape[0]
            counts = [rows << max(i - 1, 0) for i in range(len(self.parts))]
            if len(self.parts) == 1 and not self.riders:
                self.whole = self.parts[0]
            else:
                height = 0 if self.rider is None else self.rider.shape[0]
                self.whole, token = gather_parts(
                    self.parts, counts, self.riders, height, tokens
                )
            self.got = swap(self.whole, self.back[index])
            return token
        self.pair = [self.whole, self.parts[-1]]
        self.got = [swap(v, self.plan[0]) for v in self.pair]
        return tokens[0]


def open_pieces(pieces, heights, send, keep):
    got = swap(send, pieces[0].plan[0])
    first = 0
    for piece, rows in zip(pieces, heights):
        piece.window = (first, rows)
        piece.waiting += [keep, got]
        first += rows


def riders_of(piece):
    return piece.pair + piece.got


def copy_out_kernel(in_ref, out_ref, sem):
    copy = pltpu.make_async_copy(in_ref, out_ref, sem)
    copy.start()
    copy.wait()


def copy_out(value, token):
    return ordered_call(
        copy_out_kernel,
        [token],
        in_specs=[VMEM],
        out_specs=HBM,
        out_shape=shape_of(*value.shape),
        scratch_shapes=[pltpu.SemaphoreType.DMA(())],
        compiler_params=params(SMALL),
        cost_estimate=pl.CostEstimate(flops=0, bytes_accessed=1 << 10, transcendentals=0),
        name="copy_out",
    )(value)


def run(token, *pieces):
    tokens = token if isinstance(token, tuple) else (token,)
    for piece in pieces:
        if piece.at < piece.steps:
            tokens = (piece.step(*tokens),)
    return tokens[0]


def local(
    inputs,
    cotangent,
    norm_gain,
    delta,
    alpha,
    beta,
    eta,
    omega,
    w_value,
    w_base,
    qk_scale,
    qk_shift,
    w_hidden,
    ffn_gain,
    w_up,
    w_down,
    lengths,
    key_mask,
):
    ways = lax.axis_size("ch")
    place = lax.axis_index("ch").astype(jnp.int32)
    _, length, narrow = inputs.shape
    rows = length // ways
    width = narrow * ways
    groups = width // LANES
    states = delta.shape[1]
    span = rows // SUBS

    x4 = lax.all_to_all(inputs.reshape(ways, rows, narrow), "ch", 0, 0)
    pairs = split_weights((w_value, w_base, w_hidden, w_up, w_down))

    def grouped(table):
        return jnp.transpose(table.reshape(groups, LANES, states), (0, 2, 1))

    gates = jax.nn.sigmoid(delta)
    decay = jax.nn.sigmoid(alpha)
    keep = 1.0 - gates * decay
    root = math.sqrt(states)
    keep4 = grouped(keep)
    coef4 = grouped(gates * beta * (eta / root))
    log_keep = jnp.log(keep4)
    chunk_keep = jnp.exp(span * log_keep)
    device_keep = jnp.exp(rows * log_keep)
    gain4 = norm_gain.reshape(groups, 1, LANES)
    omega4 = omega.reshape(groups, 1, LANES)
    place_info = place.reshape(1)

    ends_shape = jax.ShapeDtypeStruct((groups, states * SUBS, LANES), F32)
    final_shape = jax.ShapeDtypeStruct((groups, states, LANES), F32)
    big = jax.ShapeDtypeStruct((groups, rows, LANES), F32)
    normed4, ends, final = pl.pallas_call(
        norm_kernel,
        in_specs=[VMEM] * 4,
        out_specs=[VMEM] * 3,
        out_shape=[big, ends_shape, final_shape],
        compiler_params=params(NORM_MIB),
        name="norm",
    )(x4, gain4, keep4, chunk_keep)
    finals = lax.all_gather(final, "ch", axis=0)
    total4, starts = pl.pallas_call(
        mix_kernel,
        in_specs=[SMEM] + [VMEM] * 8,
        out_specs=[VMEM] * 2,
        out_shape=[big, ends_shape],
        compiler_params=params(NORM_MIB),
        name="mix",
    )(place_info, normed4, ends, finals, keep4, coef4, chunk_keep, device_keep, omega4)

    info = jnp.stack([place * rows, lengths[0].astype(jnp.int32)])
    zwidth = qk_scale.shape[1]
    plans = orders()
    unit = SUBS << (len(plans[0][0]) - 2)
    one, other, two, three = [Piece(*plan) for plan in plans]

    def height(*counts):
        return -(-sum(counts) // QUARTER // unit) * unit

    early_heights = (
        height((w_up.size + 2 * width * width) // 4),
        height((w_down.size + w_hidden.size) // 4),
    )
    late_heights = (
        height((w_value.size + width * zwidth) // 4),
        height(width * w_value.shape[1] // 4),
    )
    (
        output,
        direct4,
        *forward_rest,
    ) = forward_call(
        info,
        jnp.concatenate([one.own_quarter, other.own_quarter]),
        key_mask,
        x4,
        normed4,
        total4,
        cotangent.reshape(rows, width),
        qk_scale,
        qk_shift,
        ffn_gain.reshape(1, width),
        pairs,
        early_heights,
    )
    saved, ffn_gain_part, ffn_parts = forward_rest[:11], forward_rest[11], forward_rest[12:]
    open_pieces((one,), early_heights[:1], *ffn_parts[:2])
    open_pieces((other,), early_heights[1:], *ffn_parts[2:])
    t = run(ffn_gain_part, one, other)
    own_quarters = jnp.concatenate([two.own_quarter, three.own_quarter])
    before, omega_parts, qk_parts = (), [], []
    tiles = rows // TILE
    for lowest, count in ((0, tiles),):
        *before, qk_part, omega_part, send, keep = backward_call(
            own_quarters,
            normed4,
            total4,
            saved,
            qk_scale,
            qk_shift,
            omega4,
            pairs,
            late_heights,
            lowest,
            count,
            before,
            [t],
        )
        omega_parts.append(omega_part)
        qk_parts.append(qk_part)
        t = run(qk_part, one, other)
        send, t = gate(send, t)
        open_pieces((two, three), late_heights, send, keep)
    grad4, part4 = before
    back_ends, back_final = scan_call(
        back_ends_kernel,
        "back_ends",
        [],
        [grad4, keep4, chunk_keep],
        [ends_shape, final_shape],
        [t],
        work=2,
    )
    back_finals = lax.all_gather(back_final, "ch", axis=0)
    t = run(back_finals, two, one, three, other)
    sums, coef_parts, keep_parts = [], [], []
    tables = (keep4, coef4, chunk_keep, device_keep)
    between = [(), (two, three, one, other), (two, three, one, other), (two, three)]
    for g in range(groups):
        done, coef_part, keep_part = back_call(
            g, 1, place_info, grad4, back_ends, back_finals, starts, normed4, part4, tables, [t]
        )
        sums.append(done)
        coef_parts.append(coef_part)
        keep_parts.append(keep_part)
        t = run((coef_part, t), *between[g % 4])
    back4, two.rider = unnorm_call(
        x4,
        sums,
        direct4,
        gain4,
        coef_parts,
        keep_parts,
        omega_parts,
        ffn_gain_part,
        qk_parts,
        [t],
    )
    back4, t = gate(back4, two.rider[:SUBS, :LANES])
    returned = lax.all_to_all(back4, "ch", 0, 0)
    t = run(t, one, other, two)
    t = run(t, one, other, three)
    t = run(t, two, three)
    t = run(t, two, three)
    t = run(t, one, other, two, three)
    while one.at < one.steps or other.at < other.steps:
        t = run(t, one, other)
    while three.at < three.steps or two.at < two.steps:
        t = run(t, two, three)
    up_rows, quarter_rows = w_up.shape[0], w_down.shape[0] // 4
    reset_at = width + zwidth
    hidden_in_at = reset_at + w_value.shape[1]

    def rest_column(q):
        return jnp.where(q < 2, q * QUARTER, hidden_in_at + (q - 2) * QUARTER)

    up_grad, down_grad, hidden_grad, base_grad, t = finish(
        [one, other],
        [
            [
                (0, as_columns(0, up_rows, 0, lambda q: q * QUARTER)),
                (3, as_columns(up_rows, width, 0, rest_column)),
            ],
            [
                (1, as_rows(0, quarter_rows, 0, w_down.shape[1])),
                (
                    2,
                    as_rows(
                        quarter_rows * w_down.shape[1] // QUARTER,
                        w_hidden.shape[0] // 4,
                        0,
                        w_hidden.shape[1],
                    ),
                ),
            ],
        ],
        [w_up.shape, w_down.shape, w_hidden.shape, w_base.shape],
        "finish_one",
        [t],
    )
    value_grad, base_grad, t = finish(
        [two, three],
        [
            [
                (0, as_columns(0, width, 0, lambda q: q * QUARTER)),
                (1, as_halves(w_value.shape[0], width * zwidth // QUARTER // 4, width)),
            ],
            [(1, as_columns(0, width, 0, lambda q: reset_at + q * QUARTER))],
        ],
        [w_value.shape, w_base.shape],
        "finish_rest",
        tokens=[t],
        into=base_grad,
    )
    input_grad = copy_out(returned, t).reshape(inputs.shape)

    tables = [grouped(table) for table in (gates, decay, beta, eta)]
    gains = small_call(riders_of(two), tables)
    return (
        output.reshape(cotangent.shape),
        input_grad,
        gains[0].reshape(width),
        gains[1].T,
        gains[2].T,
        gains[3].T,
        gains[4].T,
        gains[5].reshape(width),
        value_grad,
        base_grad,
        gains[7],
        gains[8],
        hidden_grad,
        gains[6].reshape(width),
        up_grad,
        down_grad,
    )


def solution(mesh):
    whole = P()
    placed = (
        (P("seq", None, "ch"), P("seq", "ch", None))
        + (whole,) * 14
        + (P("seq"), P("seq", None))
    )
    return jax.shard_map(
        local,
        mesh=mesh,
        in_specs=placed,
        out_specs=(P("seq", "ch", None), P("seq", None, "ch")) + (whole,) * 14,
        check_vma=False,
    )
```

```python
import math

import jax
import jax.numpy as jnp
from jax import lax
from jax.experimental import pallas as pl
from jax.experimental.pallas import tpu as pltpu
from jax.sharding import PartitionSpec as P

EPS = 1e-05
CENTER = math.sqrt(0.5)
SPREAD = math.sqrt(0.25 / math.pi)
F32 = jnp.float32
BF16 = jnp.bfloat16
NN = ((1,), (0,))
NT = ((1,), (1,))
TN = ((0,), (0,))
LANES = 128
SUBS = 8
TILE = 256
SMALL = 32
NORM_MIB = 24
FORWARD_MIB = 42
BACKWARD_MIB = 38
VMEM = pl.BlockSpec(memory_space=pltpu.VMEM)
SMEM = pl.BlockSpec(memory_space=pltpu.SMEM)
HBM = pl.BlockSpec(memory_space=pltpu.HBM)


def params(mib):
    return pltpu.CompilerParams(vmem_limit_bytes=mib << 20)


def ordered_call(kernel, tokens, *, in_specs, prefetch=0, grid=None, out_specs, scratch_shapes=(), **rest):
    count, extra = prefetch + len(in_specs), len(tokens)

    def body(*refs):
        kernel(*refs[:count], *refs[count + extra :])

    spec = pltpu.PrefetchScalarGridSpec(
        num_scalar_prefetch=prefetch,
        grid=grid or (1,),
        in_specs=list(in_specs) + [VMEM] * extra,
        out_specs=out_specs,
        scratch_shapes=scratch_shapes,
    )
    run = pl.pallas_call(body, grid_spec=spec, **rest)
    return lambda *args: run(*args, *tokens)


def shape_of(*shape, dtype=F32):
    return jax.ShapeDtypeStruct(shape, dtype)


def split(value):
    high = value.astype(BF16)
    return high, (value - high.astype(F32)).astype(BF16)


def dot(left, right, dims):
    return lax.dot_general(left, right, (dims, ((), ())), preferred_element_type=F32)


def mm3(left, right, dims):
    return (
        dot(left[0], right[0], dims)
        + dot(left[1], right[0], dims)
        + dot(left[0], right[1], dims)
    )


def mm3_short(left, right, dims):
    (left_axis,), (right_axis,) = dims
    return dot(
        jnp.concatenate([left[0], left[1], left[0]], left_axis),
        jnp.concatenate([right[0], right[0], right[1]], right_axis),
        dims,
    )


def sigmoid(value):
    return 0.5 * jnp.tanh(0.5 * value) + 0.5


def rows_sum(value):
    return jnp.sum(value, -1, keepdims=True)


def split_kernel(*refs):
    count = len(refs) // 3
    for index in range(count):
        high, low = split(refs[index][...])
        refs[count + 2 * index][...] = high
        refs[count + 2 * index + 1][...] = low


def split_weights(weights, steps=8):
    def spec(weight):
        return pl.BlockSpec((weight.shape[0] // steps, weight.shape[1]), lambda i: (i, 0))

    out = pl.pallas_call(
        split_kernel,
        grid=(steps,),
        in_specs=[spec(w) for w in weights],
        out_specs=[spec(w) for w in weights for _ in range(2)],
        out_shape=[jax.ShapeDtypeStruct(w.shape, BF16) for w in weights for _ in range(2)],
        compiler_params=params(SMALL),
        cost_estimate=pl.CostEstimate(
            flops=4 * sum(w.size for w in weights),
            bytes_accessed=8 * sum(w.size for w in weights),
            transcendentals=0,
        ),
        name="split_weights",
    )(*weights)
    return [(out[2 * i], out[2 * i + 1]) for i in range(len(weights))]


def turned(value):
    return jnp.transpose(value, (1, 0, 2))


def take_steps(ref, g, span, t):
    rows = jnp.stack([ref[g, pl.ds(c * span + t, SUBS), :] for c in range(SUBS)])
    rows = turned(rows)
    return [rows[i] for i in range(SUBS)]


def put_steps(ref, g, span, t, values):
    rows = turned(jnp.stack(values))
    for c in range(SUBS):
        ref[g, pl.ds(c * span + t, SUBS), :] = rows[c]


def rows_of(ref, g, these):
    return [jnp.broadcast_to(ref[g, n : n + 1, :], (SUBS, LANES)) for n in these]


def tree_sum(parts):
    while len(parts) > 1:
        parts = [sum(parts[i : i + 2]) for i in range(0, len(parts), 2)]
    return parts[0]


def scan_ends(source_ref, g, keep_ref, states, span, reverse):
    keeps = rows_of(keep_ref, g, range(states))

    def steps(i, state):
        t = pl.multiple_of((span // SUBS - 1 - i if reverse else i) * SUBS, SUBS)
        fresh = take_steps(source_ref, g, span, t)
        for value in reversed(fresh) if reverse else fresh:
            state = tuple(k * s + value for k, s in zip(keeps, state))
        return state

    zero = jnp.zeros((SUBS, LANES), F32)
    return lax.fori_loop(0, span // SUBS, steps, (zero,) * states, unroll=2)


def fold_ends(ends_ref, group, chunk_keep, states, order):
    total = jnp.zeros((states, LANES), F32)
    for chunk in order:
        total = chunk_keep * total + ends_ref[group, pl.ds(chunk, states, stride=SUBS), :]
    return total


def norm_kernel(x_ref, gain_ref, keep_ref, chunk_keep_ref, normed_ref, ends_ref, final_ref):
    groups, rows, _ = x_ref.shape
    states = keep_ref.shape[1]
    span = rows // SUBS
    width = groups * LANES

    def normalise(i, carry):
        here = pl.ds(pl.multiple_of(i * LANES, LANES), LANES)
        pieces = [x_ref[g, here, :] for g in range(groups)]
        mean = rows_sum(sum(pieces)) / width
        square = rows_sum(sum(p * p for p in pieces)) / width
        scale = lax.rsqrt(square - mean * mean + EPS)
        for g in range(groups):
            normed_ref[g, here, :] = (pieces[g] - mean) * scale * gain_ref[g]
        return carry

    lax.fori_loop(0, rows // LANES, normalise, 0)
    for g in range(groups):
        ends = scan_ends(normed_ref, g, keep_ref, states, span, False)
        for n in range(states):
            ends_ref[g, n * SUBS : (n + 1) * SUBS, :] = ends[n]
        final_ref[g] = fold_ends(ends_ref, g, chunk_keep_ref[g], states, range(SUBS))


def mix_kernel(
    place_ref,
    normed_ref,
    ends_ref,
    finals_ref,
    keep_ref,
    coef_ref,
    chunk_keep_ref,
    device_keep_ref,
    omega_ref,
    total_ref,
    start_ref,
):
    groups, rows, _ = normed_ref.shape
    states = keep_ref.shape[1]
    span = rows // SUBS
    ways = finals_ref.shape[0]
    place = place_ref[0]
    for g in range(groups):
        state = jnp.zeros((states, LANES), F32)
        for d in range(ways):
            state = jnp.where(d < place, device_keep_ref[g] * state + finals_ref[d, g], state)
        for chunk in range(SUBS):
            start_ref[g, pl.ds(chunk, states, stride=SUBS), :] = state
            state = chunk_keep_ref[g] * state + ends_ref[g, pl.ds(chunk, states, stride=SUBS), :]
        keeps = rows_of(keep_ref, g, range(states))
        coefs = rows_of(coef_ref, g, range(states))
        omega = jnp.broadcast_to(omega_ref[g], (SUBS, LANES))

        def steps(i, state):
            t = pl.multiple_of(i * SUBS, SUBS)
            totals = []
            for fresh in take_steps(normed_ref, g, span, t):
                state = tuple(k * s + fresh for k, s in zip(keeps, state))
                totals.append(tree_sum([c * s for c, s in zip(coefs, state)] + [omega * fresh]))
            put_steps(total_ref, g, span, t, totals)
            return state

        first = tuple(start_ref[g, n * SUBS : (n + 1) * SUBS, :] for n in range(states))
        lax.fori_loop(0, span // SUBS, steps, first, unroll=2)


def back_ends_kernel(grad_ref, keep_ref, chunk_keep_ref, ends_ref, final_ref):
    _, rows, _ = grad_ref.shape
    states = keep_ref.shape[1]
    span = rows // SUBS
    for g in range(1):
        ends = scan_ends(grad_ref, g, keep_ref, states, span, True)
        for n in range(states):
            ends_ref[g, n * SUBS : (n + 1) * SUBS, :] = ends[n]
        final_ref[g] = fold_ends(ends_ref, g, chunk_keep_ref[g], states, reversed(range(SUBS)))


def back_kernel(
    place_ref,
    grad_ref,
    ends_ref,
    finals_ref,
    start_ref,
    normed_ref,
    part_ref,
    keep_ref,
    coef_ref,
    chunk_keep_ref,
    device_keep_ref,
    sum_ref,
    coef_grad_ref,
    keep_grad_ref,
    init_ref,
):
    _, rows, _ = grad_ref.shape
    states = keep_ref.shape[1]
    span = rows // SUBS
    ways = finals_ref.shape[0]
    place = place_ref[0]
    half = states // 2
    zero = jnp.zeros((SUBS, LANES), F32)
    for g in range(1):
        whole_g = 0
        state = jnp.zeros((states, LANES), F32)
        for d in reversed(range(ways)):
            state = jnp.where(
                d > place, device_keep_ref[whole_g] * state + finals_ref[d, whole_g], state
            )
        for chunk in reversed(range(SUBS)):
            init_ref[pl.ds(chunk, states, stride=SUBS), :] = state
            state = (
                chunk_keep_ref[whole_g] * state
                + ends_ref[whole_g, pl.ds(chunk, states, stride=SUBS), :]
            )
        for part in range(2):
            these = range(part * half, (part + 1) * half)
            keeps = rows_of(keep_ref, whole_g, these)
            coefs = rows_of(coef_ref, whole_g, these)

            def steps(i, carry):
                lam, second, coef_acc, keep_acc = carry
                t = pl.multiple_of((span // SUBS - 1 - i) * SUBS, SUBS)
                fresh = take_steps(grad_ref, g, span, t)
                source = take_steps(normed_ref, g, span, t)
                outs = [None] * SUBS
                for j in reversed(range(SUBS)):
                    keep_acc = tuple(a + v * source[j] for a, v in zip(keep_acc, second))
                    lam = tuple(k * l + fresh[j] for k, l in zip(keeps, lam))
                    coef_acc = tuple(a + l * source[j] for a, l in zip(coef_acc, lam))
                    second = tuple(l + k * v for l, k, v in zip(lam, keeps, second))
                    outs[j] = tree_sum([c * l for c, l in zip(coefs, lam)])
                rows = turned(jnp.stack(outs))
                before = part_ref if part == 0 else sum_ref
                for c in range(SUBS):
                    here = pl.ds(c * span + t, SUBS)
                    sum_ref[g, here, :] = before[g, here, :] + rows[c]
                return lam, second, coef_acc, keep_acc

            first = tuple(init_ref[n * SUBS : (n + 1) * SUBS, :] for n in these)
            nothing = (zero,) * half
            lam, second, coef_acc, keep_acc = lax.fori_loop(
                0, span // SUBS, steps, (first, nothing, nothing, nothing)
            )
            for j, n in enumerate(these):
                start = start_ref[whole_g, n * SUBS : (n + 1) * SUBS, :]
                keep_acc_n = keep_acc[j] + start * second[j]
                coef_grad_ref[g, n : n + 1, :] = jnp.sum(coef_acc[j], 0, keepdims=True)
                keep_grad_ref[g, n : n + 1, :] = jnp.sum(keep_acc_n, 0, keepdims=True)


def unnorm_kernel(
    calls,
    x_ref,
    *refs,
):
    sums, refs = refs[:calls], refs[calls:]
    direct_ref, gain_ref, refs = refs[0], refs[1], refs[2:]
    coefs, keeps, refs = refs[:calls], refs[calls : 2 * calls], refs[2 * calls :]
    omega_ref, ffn_ref, qk_ref, out_ref, small_ref, gain_grad = refs
    groups, rows, _ = x_ref.shape
    width = groups * LANES
    share = groups // calls
    tile = pl.program_id(0)

    @pl.when(tile == 0)
    def _():
        gain_grad[...] = jnp.zeros_like(gain_grad)

    pieces = [x_ref[g] for g in range(groups)]
    mean = rows_sum(sum(pieces)) / width
    square = rows_sum(sum(p * p for p in pieces)) / width
    scale = lax.rsqrt(square - mean * mean + EPS)
    centered = [(p - mean) * scale for p in pieces]
    grads = [sums[g // share][g % share] for g in range(groups)]
    for g in range(groups):
        gain_grad[g : g + 1, :] += jnp.sum(grads[g] * centered[g], 0, keepdims=True)
    scaled = [grads[g] * gain_ref[g] for g in range(groups)]
    plain = rows_sum(sum(scaled)) / width
    cross = rows_sum(sum(s * c for s, c in zip(scaled, centered))) / width
    for g in range(groups):
        out_ref[g] = direct_ref[g] + scale * (scaled[g] - plain - centered[g] * cross)

    @pl.when(tile == pl.num_programs(0) - 1)
    def _():
        states = coefs[0].shape[1]
        for i, refs in enumerate((coefs, keeps)):
            for g in range(groups):
                at = slice(g * states, (g + 1) * states)
                small_ref[at, i * LANES : (i + 1) * LANES] = refs[g // share][g % share]
        at = groups * states
        small_ref[at:, :] = jnp.zeros((small_ref.shape[0] - at, 2 * LANES), F32)
        small_ref[at : at + groups, :LANES] = gain_grad[:groups]
        for g in range(groups):
            here = slice(at + groups + g, at + groups + g + 1)
            small_ref[here, :LANES] = omega_ref[g]
            small_ref[here, LANES:] = ffn_ref[:, g * LANES : (g + 1) * LANES]
        small_ref[at : at + 4, LANES:] = qk_ref[0:4, :]


def group_spec(array, lowest=0):
    axis = array.ndim - 3
    block = array.shape[:axis] + (1,) + array.shape[axis + 1 :]
    return pl.BlockSpec(block, lambda g: (0,) * axis + (lowest + g, 0, 0))


def scan_call(kernel, name, scalars, arrays, outs, tokens=(), lowest=0, count=None, scratch=(), work=4):
    count = count or arrays[0].shape[-3]
    states, rows = outs[-1].shape[-2], arrays[0].shape[-2]
    return ordered_call(
        kernel,
        tokens,
        grid=(count,),
        in_specs=[SMEM] * len(scalars) + [group_spec(v, lowest) for v in arrays],
        out_specs=[group_spec(v) for v in outs],
        scratch_shapes=scratch,
        out_shape=outs,
        compiler_params=params(SMALL),
        cost_estimate=pl.CostEstimate(
            flops=work * rows * count * LANES * 16,
            bytes_accessed=12 * rows * count * LANES,
            transcendentals=0,
        ),
        name=name,
    )(*scalars, *arrays)


def back_call(lowest, count, place_info, grad4, ends, finals, starts, normed4, part4, tables, tokens):
    rows, states = grad4.shape[1], starts.shape[1] // SUBS
    arrays = [grad4, ends, finals, starts, normed4, part4, *tables]
    outs = [shape_of(count, rows, LANES)] + [shape_of(count, states, LANES)] * 2
    return scan_call(
        back_kernel,
        "back",
        [place_info],
        arrays,
        outs,
        tokens,
        lowest,
        count,
        [pltpu.VMEM((states * SUBS, LANES), F32)],
        10,
    )


def unnorm_call(x4, sums, direct4, gain4, coefs, keeps, omega, ffn, qk, tokens):
    groups, rows, _ = x4.shape
    states = coefs[0].shape[1]
    by_group = pl.BlockSpec((groups, TILE, LANES), lambda i: (0, i, 0))
    halves = [pl.BlockSpec((s.shape[0], TILE, LANES), lambda i: (0, i, 0)) for s in sums]
    height = -(-(groups * states + 2 * groups) // 16) * 16
    return ordered_call(
        lambda *refs: unnorm_kernel(len(sums), *refs),
        tokens,
        grid=(rows // TILE,),
        in_specs=[by_group] + halves + [by_group] + [VMEM] * (4 + 2 * len(sums)),
        out_specs=[by_group, pl.BlockSpec((height, 2 * LANES), lambda i: (0, 0))],
        out_shape=[shape_of(*x4.shape), shape_of(height, 2 * LANES)],
        scratch_shapes=[pltpu.VMEM((SUBS, LANES), F32)],
        compiler_params=params(SMALL),
        cost_estimate=pl.CostEstimate(
            flops=20 * x4.size, bytes_accessed=16 * x4.size, transcendentals=0
        ),
        name="unnorm",
    )(x4, *sums, direct4, gain4, *coefs, *keeps, *omega, ffn, *qk)


def small_kernel(
    part_a,
    part_b,
    part_c,
    part_d,
    gate_ref,
    decay_ref,
    beta_ref,
    eta_ref,
    gain_out,
    delta_out,
    alpha_out,
    beta_out,
    eta_out,
    omega_out,
    ffn_out,
    scale_out,
    shift_out,
):
    groups, states, _ = gate_ref.shape
    root = math.sqrt(states)
    at = groups * states
    height = -(-(groups * states + 2 * groups) // 16) * 16
    tails = [ref[ref.shape[0] - height :, :] for ref in (part_a, part_b, part_c, part_d)]
    total = (tails[0] + tails[1]) + (tails[2] + tails[3])
    for g in range(groups):
        here = slice(g * states, (g + 1) * states)
        coef, keep = total[here, :LANES], total[here, LANES:]
        gate, decay, beta, eta = gate_ref[g], decay_ref[g], beta_ref[g], eta_ref[g]
        keep = keep * gate * beta * (eta / root)
        gate_grad = coef * beta * (eta / root) - keep * decay
        lanes = slice(g * LANES, (g + 1) * LANES)
        delta_out[:, lanes] = gate_grad * gate * (1.0 - gate)
        alpha_out[:, lanes] = -keep * gate * decay * (1.0 - decay)
        beta_out[:, lanes] = coef * gate * (eta / root)
        eta_out[:, lanes] = coef * gate * beta / root
    gain_out[...] = total[at : at + groups, :LANES]
    omega_out[...] = total[at + groups : at + 2 * groups, :LANES]
    ffn_out[...] = total[at + groups : at + 2 * groups, LANES:]
    scale_out[...] = total[at : at + 2, LANES:]
    shift_out[...] = total[at + 2 : at + 4, LANES:]


def small_call(parts, tables):
    groups, states, _ = tables[0].shape
    row, table = shape_of(groups, LANES), shape_of(states, groups * LANES)
    two = shape_of(2, LANES)
    return pl.pallas_call(
        small_kernel,
        in_specs=[VMEM] * 8,
        out_specs=[VMEM] * 9,
        out_shape=[row, table, table, table, table, row, row, two, two],
        compiler_params=params(SMALL),
        name="small_grads",
    )(*parts, *tables)


QUARTER = 256
EVERY = slice(None)


def columns(total, step=512):
    return [slice(i, min(i + step, total)) for i in range(0, total, step)]


def joined(ref):
    return jnp.concatenate([ref[g] for g in range(ref.shape[0])], 1)


def silu_slope(act, gate):
    return gate + act * (1.0 - gate)


class Attention:
    def __init__(self, z, scale_ref, shift_ref, mask_ref, base_row, length):
        rows, span = z.shape[0], mask_ref.shape[1]
        blocks = rows // span
        self.query = split(z * scale_ref[0:1, :] + shift_ref[0:1, :])
        self.key = split(z * scale_ref[1:2, :] + shift_ref[1:2, :])
        lane = lax.broadcasted_iota(jnp.int32, (1, span), 1)
        valids, counts = [], []
        for b in range(blocks):
            position = base_row + b * span + lane
            last_block = (base_row + b * span) // span == (length - 1) // span
            kept = (position < length) & (jnp.logical_not(last_block) | (mask_ref[...] == 1))
            valid = jnp.where(kept, 1.0, 0.0)
            count = jnp.maximum(rows_sum(valid), 1.0)
            valids.append(valid)
            counts.append(jnp.broadcast_to(count, (1, span)))
        row = lax.broadcasted_iota(jnp.int32, (rows, rows), 0)
        column = lax.broadcasted_iota(jnp.int32, (rows, rows), 1)
        near = (row >= column) & (row // span == column // span)
        self.mask = jnp.where(near, jnp.concatenate(valids, 1), 0.0)
        self.count = jnp.concatenate(counts, 1)
        self.spot = mm3_short(self.query, self.key, NT) / self.count - CENTER

    def weight(self):
        curve = lax.erf(self.spot * (1.0 / (SPREAD * math.sqrt(2.0))))
        return split((0.5 + 0.5 * curve) * self.mask)

    def slope(self):
        return (
            jnp.exp(self.spot * self.spot * (-1.0 / (2.0 * SPREAD * SPREAD)))
            * (self.mask / self.count)
            * (1.0 / (SPREAD * math.sqrt(2.0 * math.pi)))
        )


def add_to(total_ref, quarter, at, pieces, first):
    for piece in pieces:
        here = slice(at, at + piece.shape[0])
        at += piece.shape[0]
        total_ref[quarter, here, :] = jnp.where(first, 0.0, total_ref[quarter, here, :]) + piece
    return at


def packed_rows(value):
    return [value[:, i : i + QUARTER] for i in range(0, value.shape[1], QUARTER)]


class Fetch:
    def __init__(self, sources, targets, sems, first):
        self.first = first
        self.copies = [
            pltpu.make_async_copy(source, target, sems.at[i])
            for i, (source, target) in enumerate(zip(sources, targets))
        ]

        @pl.when(first)
        def _():
            for copy in self.copies:
                copy.start()

    def wait(self, *which):
        @pl.when(self.first)
        def _():
            for i in which:
                self.copies[i].wait()


class HandOut:
    def __init__(self, own, total, send, keep, row, sems, last, cut=None):
        self.own, self.total, self.send, self.keep = own, total, send, keep
        self.row, self.sems, self.last = row, sems, last
        rows = total.shape[1]
        self.parts = [(0, rows)] if cut is None else [(0, cut), (cut, rows - cut)]

    def each(self, quarter, part, act):
        apart = quarter ^ self.own
        first, count = self.parts[part]
        source = self.total.at[quarter, pl.ds(first, count)]
        rows = pl.ds(self.row + first, count)
        sem = self.sems.at[quarter, part]

        @pl.when(self.last & (apart >= 2))
        def _():
            act(pltpu.make_async_copy(source, self.send.at[3 - apart, rows], sem))

        @pl.when(self.last & (apart < 2))
        def _():
            act(pltpu.make_async_copy(source, self.keep.at[1 - apart, rows], sem))

    def start(self, quarter, part=0):
        self.each(quarter, part, lambda copy: copy.start())

    def wait(self):
        for quarter in range(4):
            for part in range(len(self.parts)):
                self.each(quarter, part, lambda copy: copy.wait())


def forward_kernel(
    info_ref,
    place_ref,
    mask_ref,
    x_ref,
    normed_ref,
    total_ref,
    cot_ref,
    scale_ref,
    shift_ref,
    gain_ref,
    wv_h,
    wv_l,
    wb_h,
    wb_l,
    wh_h,
    wh_l,
    wu_h,
    wu_l,
    wd_h,
    wd_l,
    out_ref,
    direct_ref,
    v_h,
    v_l,
    vsil,
    rst,
    attr,
    weight_h,
    weight_l,
    slope_ref,
    zpre,
    grad_u_ref,
    grad_h_ref,
    gain_grad_ref,
    send_a,
    keep_a,
    send_b,
    keep_b,
    upd,
    hpre,
    gr_h,
    gr_l,
    a_h,
    a_l,
    usil,
    du_h,
    du_l,
    acc_a,
    acc_b,
    sems_a,
    sems_b,
):
    tile = pl.program_id(0)
    first = tile == 0
    groups, rows, _ = x_ref.shape
    width = groups * LANES
    zwidth = scale_ref.shape[1]
    values = wv_h.shape[1]
    units = wu_h.shape[1]
    base_row, length = info_ref[0] + tile * rows, info_ref[1]
    last = tile == pl.num_programs(0) - 1
    out_a = HandOut(place_ref[0], acc_a, send_a, keep_a, 0, sems_a, last, width)
    out_b = HandOut(place_ref[1], acc_b, send_b, keep_b, 0, sems_b, last, width)

    @pl.when(first)
    def _():
        gain_grad_ref[...] = jnp.zeros_like(gain_grad_ref)

    def put(high_ref, low_ref, where, value):
        high, low = split(value)
        high_ref[where] = high
        low_ref[where] = low
        return high, low

    n_pair = split(joined(normed_ref))
    total = joined(total_ref)
    m_pair = split(total * sigmoid(total))
    for c in columns(values):
        pre = mm3(n_pair, (wv_h[:, c], wv_l[:, c]), NN)
        s = sigmoid(pre)
        act = pre * s
        put(v_h, v_l, (EVERY, c), act)
        vsil[:, c] = silu_slope(act, s)
    c = slice(width, width + zwidth)
    pre = mm3(m_pair, (wb_h[:, c], wb_l[:, c]), NN)
    zpre[...] = pre
    attention = Attention(
        pre * sigmoid(pre), scale_ref, shift_ref, mask_ref, base_row, length
    )
    c = slice(0, width)
    upd[...] = sigmoid(mm3(m_pair, (wb_h[:, c], wb_l[:, c]), NN))
    for c in columns(values):
        w = slice(width + zwidth + c.start, width + zwidth + c.stop)
        pre = mm3(m_pair, (wb_h[:, w], wb_l[:, w]), NN)
        s = sigmoid(pre)
        act = pre * s
        rst[:, c] = act
        attr[:, c] = silu_slope(act, s)
    w = slice(width + zwidth + values, width + zwidth + values + width)
    hpre[...] = mm3(m_pair, (wb_h[:, w], wb_l[:, w]), NN)
    weight = attention.weight()
    weight_h[...], weight_l[...] = weight
    slope_ref[...] = attention.slope()
    for c in columns(values):
        got = mm3(weight, (v_h[:, c], v_l[:, c]), NN)
        put(gr_h, gr_l, (EVERY, c), got * rst[:, c])
        attr[:, c] = got * attr[:, c]
    pre = hpre[...] + mm3((gr_h[...], gr_l[...]), (wh_h[...], wh_l[...]), NN)
    s = sigmoid(pre)
    hidden = pre * s
    hpre[...] = silu_slope(hidden, s)
    x = joined(x_ref)
    update = upd[...]
    apart = hidden - x
    gated = x + update * apart
    mean = rows_sum(gated) / width
    square = rows_sum(gated * gated) / width
    scale = lax.rsqrt(square - mean * mean + EPS)
    centered = (gated - mean) * scale
    f_pair = split(centered * gain_ref[...])
    for c in columns(units):
        pre = mm3(f_pair, (wu_h[:, c], wu_l[:, c]), NN)
        s = sigmoid(pre)
        act = pre * s
        put(a_h, a_l, (EVERY, c), act)
        usil[:, c] = silu_slope(act, s)
    live = (base_row + lax.broadcasted_iota(jnp.int32, (rows, 1), 0) < length).astype(F32)
    out_ref[...] = (gated + mm3((a_h[...], a_l[...]), (wd_h[...], wd_l[...]), NN)) * live

    grad_out = cot_ref[...] * live
    do_pair = split(grad_out)
    for q in range(0, 4, 2):
        c = slice(q * QUARTER, (q + 2) * QUARTER)
        down = mm3((a_h[:, c], a_l[:, c]), do_pair, TN)
        for i in range(2):
            c = slice(i * QUARTER, (i + 1) * QUARTER)
            add_to(acc_b, q + i, 0, packed_rows(down[c]), first)
            out_b.start(q + i)
    for c in columns(units):
        put(du_h, du_l, (EVERY, c), mm3(do_pair, (wd_h[c, :], wd_l[c, :]), NT) * usil[:, c])
    grad_f = mm3((du_h[...], du_l[...]), (wu_h[...], wu_l[...]), NT)
    for q in range(0, 4, 2):
        c = slice(q * QUARTER, (q + 2) * QUARTER)
        up = mm3(f_pair, (du_h[:, c], du_l[:, c]), TN)
        for i in range(2):
            add_to(acc_a, q + i, 0, [up[:, i * QUARTER : (i + 1) * QUARTER]], first)
            out_a.start(q + i)
    gain_grad_ref[...] += jnp.sum(grad_f * centered, 0, keepdims=True)
    scaled = grad_f * gain_ref[...]
    grad_gated = grad_out + scale * (
        scaled - rows_sum(scaled) / width - centered * (rows_sum(scaled * centered) / width)
    )
    grad_u = grad_gated * apart * update * (1.0 - update)
    grad_u_ref[...] = grad_u
    u_pair = split(grad_u)
    grad_h = grad_gated * update * hpre[...]
    grad_h_ref[...] = grad_h
    h_pair = split(grad_h)
    direct = grad_gated * (1.0 - update)
    for g in range(groups):
        direct_ref[g] = direct[:, g * LANES : (g + 1) * LANES]
    for q in range(0, 4, 2):
        c = slice(q * QUARTER, (q + 2) * QUARTER)
        rest = mm3(m_pair, u_pair if q == 0 else h_pair, TN)
        hid = mm3((gr_h[:, c], gr_l[:, c]), h_pair, TN)
        for i in range(2):
            c = slice(i * QUARTER, (i + 1) * QUARTER)
            add_to(acc_a, q + i, width, [rest[:, c]], first)
            add_to(acc_b, q + i, width, packed_rows(hid[c]), first)
            out_a.start(q + i, 1)
            out_b.start(q + i, 1)
    out_a.wait()
    out_b.wait()


def backward_kernel(
    continued,
    place_ref,
    normed_ref,
    total_ref,
    v_h,
    v_l,
    vsil,
    rst,
    attr,
    weight_h,
    weight_l,
    slope_ref,
    zpre,
    grad_u_ref,
    grad_h_ref,
    scale_ref,
    shift_ref,
    omega_ref,
    wh_h,
    wh_l,
    wv_h_hbm,
    wv_l_hbm,
    wb_h_hbm,
    wb_l_hbm,
    *refs,
):
    (
        grad_ref,
        part_ref,
        qk_grad_ref,
        omega_grad_ref,
        send_ref,
        keep_ref,
        da_h,
        da_l,
        dv_h,
        dv_l,
        bz_h,
        bz_l,
        br_h,
        br_l,
        acc_b,
        acc_c,
        wv_h,
        wv_l,
        wb_h,
        wb_l,
        sems_b,
        sems_c,
        weight_sems,
    ) = refs[2 if continued else 0 :]
    tile = pl.program_id(0)
    first, last = tile == 0, tile == pl.num_programs(0) - 1
    groups = normed_ref.shape[0]
    width = groups * LANES
    zwidth = scale_ref.shape[1]
    values = vsil.shape[1]
    fetch = Fetch(
        [wv_h_hbm, wv_l_hbm, wb_h_hbm, wb_l_hbm],
        [wv_h, wv_l, wb_h, wb_l],
        weight_sems,
        first,
    )
    out_b = HandOut(place_ref[0], acc_b, send_ref, keep_ref, 0, sems_b, last)
    out_c = HandOut(place_ref[1], acc_c, send_ref, keep_ref, acc_b.shape[1], sems_c, last)

    @pl.when(first)
    def _():
        qk_grad_ref[...] = jnp.zeros_like(qk_grad_ref)
        omega_grad_ref[...] = jnp.zeros_like(omega_grad_ref)

    def put(high_ref, low_ref, where, value):
        high, low = split(value)
        high_ref[where] = high
        low_ref[where] = low

    u_pair = split(grad_u_ref[...])
    h_pair = split(grad_h_ref[...])
    for c in columns(values):
        got = mm3(h_pair, (wh_h[c, :], wh_l[c, :]), NT)
        put(da_h, da_l, (EVERY, c), got * rst[:, c])
        put(br_h, br_l, (EVERY, c), got * attr[:, c])
    pre = zpre[...]
    s = sigmoid(pre)
    z = pre * s
    zsil = silu_slope(z, s)
    query = split(z * scale_ref[0:1, :] + shift_ref[0:1, :])
    key = split(z * scale_ref[1:2, :] + shift_ref[1:2, :])
    weight = (weight_h[...], weight_l[...])
    grad_scores = split(mm3((da_h[...], da_l[...]), (v_h[...], v_l[...]), NT) * slope_ref[...])
    for c in columns(values):
        got = mm3(weight, (da_h[:, c], da_l[:, c]), TN)
        put(dv_h, dv_l, (EVERY, c), got * vsil[:, c])
    grad_q = mm3(grad_scores, key, NN)
    grad_k = mm3(grad_scores, query, TN)
    qk_grad_ref[0:1, :] += jnp.sum(grad_q * z, 0, keepdims=True)
    qk_grad_ref[1:2, :] += jnp.sum(grad_k * z, 0, keepdims=True)
    qk_grad_ref[2:3, :] += jnp.sum(grad_q, 0, keepdims=True)
    qk_grad_ref[3:4, :] += jnp.sum(grad_k, 0, keepdims=True)
    put(
        bz_h,
        bz_l,
        (EVERY, EVERY),
        (grad_q * scale_ref[0:1, :] + grad_k * scale_ref[1:2, :]) * zsil,
    )

    n_pair = split(joined(normed_ref))
    total = joined(total_ref)
    gate_here = sigmoid(total)
    mixed = total * gate_here
    m_pair = split(mixed)
    grad_bz = mm3(m_pair, (bz_h[...], bz_l[...]), TN)
    for q in range(0, 4, 2):
        c = slice(q * QUARTER, (q + 2) * QUARTER)
        value = mm3(n_pair, (dv_h[:, c], dv_l[:, c]), TN)
        reset = mm3(m_pair, (br_h[:, c], br_l[:, c]), TN)
        for i in range(2):
            c = slice(i * QUARTER, (i + 1) * QUARTER)
            at = add_to(acc_b, q + i, 0, [value[:, c]], first)
            got = grad_bz[(q + i) * width // 4 : (q + i + 1) * width // 4]
            half = got.shape[0] // 2
            add_to(acc_b, q + i, at, [jnp.concatenate([got[:half], got[half:]], 1)], first)
            add_to(acc_c, q + i, 0, [reset[:, c]], first)
            out_b.start(q + i)
            out_c.start(q + i)

    fetch.wait(0, 1, 2, 3)
    grad_n = mm3((dv_h[...], dv_l[...]), (wv_h[...], wv_l[...]), NT)
    at = [0, width, width + zwidth, width + zwidth + values, 2 * width + zwidth + values]
    w = [slice(i, j) for i, j in zip(at[:-1], at[1:])]
    grad = (
        mm3(u_pair, (wb_h[:, w[0]], wb_l[:, w[0]]), NT)
        + mm3_short((bz_h[...], bz_l[...]), (wb_h[:, w[1]], wb_l[:, w[1]]), NT)
        + mm3((br_h[...], br_l[...]), (wb_h[:, w[2]], wb_l[:, w[2]]), NT)
        + mm3(h_pair, (wb_h[:, w[3]], wb_l[:, w[3]]), NT)
    ) * silu_slope(mixed, gate_here)
    for g in range(groups):
        lanes = slice(g * LANES, (g + 1) * LANES)
        got = grad[:, lanes]
        grad_ref[g] = got
        part_ref[g] = grad_n[:, lanes] + got * omega_ref[g]
        omega_grad_ref[g] += jnp.sum(got * normed_ref[g], 0, keepdims=True)
    out_b.wait()
    out_c.wait()


def by_row(count, lowest=0):
    return pl.BlockSpec((TILE, count), lambda i: (lowest + i, 0))


def forward_call(info, place, key_mask, x4, normed4, total4, cot, qk_scale, qk_shift, ffn_gain, pairs, heights):
    groups, rows, _ = x4.shape
    width = groups * LANES
    wv, wb, wh, wu, wd = pairs
    values, units, zwidth = wv[0].shape[1], wu[0].shape[1], qk_scale.shape[1]
    flat = [part for pair in pairs for part in pair]
    by_group = pl.BlockSpec((groups, TILE, LANES), lambda i: (0, i, 0))
    macs = rows * (wv[0].size + wb[0].size + wh[0].size + 3 * wu[0].size + 3 * wd[0].size)
    return pl.pallas_call(
        forward_kernel,
        grid=(rows // TILE,),
        in_specs=[SMEM, SMEM, VMEM, by_group, by_group, by_group, by_row(width)]
        + [VMEM] * (3 + len(flat)),
        out_specs=[
            by_row(width),
            by_group,
            by_row(values),
            by_row(values),
            by_row(values),
            by_row(values),
            by_row(values),
            by_row(TILE),
            by_row(TILE),
            by_row(TILE),
            by_row(zwidth),
            by_row(width),
            by_row(width),
            pl.BlockSpec((1, width), lambda i: (0, 0)),
            HBM,
            HBM,
            HBM,
            HBM,
        ],
        out_shape=[
            shape_of(rows, width),
            shape_of(groups, rows, LANES),
            shape_of(rows, values, dtype=BF16),
            shape_of(rows, values, dtype=BF16),
            shape_of(rows, values),
            shape_of(rows, values),
            shape_of(rows, values),
            shape_of(rows, TILE, dtype=BF16),
            shape_of(rows, TILE, dtype=BF16),
            shape_of(rows, TILE),
            shape_of(rows, zwidth),
            shape_of(rows, width),
            shape_of(rows, width),
            shape_of(1, width),
        ]
        + [shape_of(2, height, QUARTER) for height in heights for _ in range(2)],
        scratch_shapes=[
            pltpu.VMEM((TILE, width), F32),
            pltpu.VMEM((TILE, width), F32),
            pltpu.VMEM((TILE, values), BF16),
            pltpu.VMEM((TILE, values), BF16),
            pltpu.VMEM((TILE, units), BF16),
            pltpu.VMEM((TILE, units), BF16),
            pltpu.VMEM((TILE, units), F32),
            pltpu.VMEM((TILE, units), BF16),
            pltpu.VMEM((TILE, units), BF16),
        ]
        + [pltpu.VMEM((4, height, QUARTER), F32) for height in heights]
        + [pltpu.SemaphoreType.DMA((4, 2))] * 2,
        compiler_params=params(FORWARD_MIB),
        cost_estimate=pl.CostEstimate(flops=6 * macs, bytes_accessed=48 << 20, transcendentals=0),
        name="forward",
    )(info, place, key_mask, x4, normed4, total4, cot, qk_scale, qk_shift, ffn_gain, *flat)


def backward_call(
    place, normed4, total4, saved, qk_scale, qk_shift, omega4, pairs, heights, lowest, tiles, before, tokens
):
    groups, rows, _ = normed4.shape
    width = groups * LANES
    wv, wb, wh = pairs[:3]
    values, zwidth = wv[0].shape[1], qk_scale.shape[1]
    by_group = pl.BlockSpec((groups, TILE, LANES), lambda i: (0, lowest + i, 0))
    fetched = [*wv, *wb]
    args = [place, normed4, total4, *saved, qk_scale, qk_shift, omega4, *wh, *fetched]
    quarters = [shape_of(2, sum(heights), QUARTER)] * 2
    return ordered_call(
        lambda *refs: backward_kernel(bool(before), *refs),
        tokens,
        grid=(tiles,),
        in_specs=[SMEM, by_group, by_group]
        + [by_row(s.shape[1], lowest) for s in saved]
        + [VMEM] * (3 + len(wh))
        + [HBM] * (len(fetched) + len(before)),
        out_specs=[
            by_group,
            by_group,
            pl.BlockSpec((8, zwidth), lambda i: (0, 0)),
            pl.BlockSpec((groups, 1, LANES), lambda i: (0, 0, 0)),
        ]
        + [HBM] * 2,
        out_shape=[
            shape_of(groups, rows, LANES),
            shape_of(groups, rows, LANES),
            shape_of(8, zwidth),
            shape_of(groups, 1, LANES),
        ]
        + quarters,
        input_output_aliases={len(args): 0, len(args) + 1: 1} if before else {},
        scratch_shapes=[pltpu.VMEM((TILE, values), BF16)] * 4
        + [pltpu.VMEM((TILE, zwidth), BF16)] * 2
        + [pltpu.VMEM((TILE, values), BF16)] * 2
        + [pltpu.VMEM((4, height, QUARTER), F32) for height in heights]
        + [pltpu.VMEM(w.shape, BF16) for w in fetched]
        + [pltpu.SemaphoreType.DMA((4, 1))] * 2
        + [pltpu.SemaphoreType.DMA((len(fetched),))],
        compiler_params=params(BACKWARD_MIB),
        cost_estimate=pl.CostEstimate(
            flops=12 * tiles * TILE * (wv[0].size + wb[0].size + wh[0].size),
            bytes_accessed=40 << 20,
            transcendentals=0,
        ),
        name="backward",
    )(*args, *before)


def swap(value, step):
    axis, distance = step
    size = lax.axis_size(axis)
    return lax.ppermute(value, axis, [(i, i ^ distance) for i in range(size)])


def side(step):
    axis, distance = step
    return (lax.axis_index(axis) // distance) % 2


def device_steps():
    def bits(axis):
        size = lax.axis_size(axis)
        return [(axis, 1 << i) for i in range(size.bit_length() - 1)]

    return bits("ch"), bits("seq")


def orders():
    ch, seq = device_steps()
    x, y, z, rest = ch[1:], seq[:1], seq[1:2], seq[2:]
    out = [
        y + z + x + rest,
        z + y + x + rest,
        z + y + x + rest,
        y + z + x + rest,
    ]
    back = [
        rest[::-1] + z + x + y,
        rest[::-1] + x + y + z,
        rest[::-1] + y + z + x,
        rest[::-1] + z + y + x,
    ]
    return [(ch[:1] + go, come + ch[:1]) for go, come in zip(out, back)]


TOKEN = shape_of(SUBS, LANES)


def gate(value, token):
    return lax.optimization_barrier((value, token))


def halve_kernel(count, first, own_ref, *refs):
    own = own_ref[0]
    parts, (send_ref, next_ref, token_ref) = refs[:count], refs[count:]
    rows = pl.ds(first, send_ref.shape[0])
    send_ref[...] = sum(part[1 - own, rows, :] for part in parts)
    next_ref[...] = sum(part[own, rows, :] for part in parts)
    token_ref[...] = jnp.zeros_like(token_ref)


def halve(parts, window, own, tokens):
    width = parts[0].shape[-1]
    height = parts[0].size // width // 2
    first, rows = window or (0, height)
    parts = [part.reshape(2, height, width) for part in parts]
    return ordered_call(
        lambda *refs: halve_kernel(len(parts), first, *refs),
        tokens,
        in_specs=[SMEM] + [VMEM] * len(parts),
        out_specs=[VMEM] * 3,
        out_shape=[shape_of(rows, width)] * 2 + [TOKEN],
        compiler_params=params(SMALL),
        cost_estimate=pl.CostEstimate(
            flops=2 * rows * width, bytes_accessed=1 << 10, transcendentals=0
        ),
        name="halve",
    )(own.reshape(1), *parts)


def add_kernel(left_ref, right_ref, out_ref, token_ref):
    out_ref[...] = left_ref[...] + right_ref[...]
    token_ref[...] = jnp.zeros_like(token_ref)


def add(left, right, tokens):
    return ordered_call(
        add_kernel,
        tokens,
        in_specs=[VMEM] * 2,
        out_specs=[VMEM] * 2,
        out_shape=[shape_of(*left.shape), TOKEN],
        compiler_params=params(SMALL),
        cost_estimate=pl.CostEstimate(flops=left.size, bytes_accessed=1 << 10, transcendentals=0),
        name="add",
    )(left, right)


def gather_kernel(counts, riders, *refs):
    parts, refs = refs[: len(counts)], refs[len(counts) :]
    out_ref, token_ref = refs[-2:]
    at = 0
    for part, rows in zip(parts, counts):
        out_ref[at : at + rows, :] = part[:rows, :]
        at += rows
    if riders:
        tails = [ref[ref.shape[0] - riders :, :] for ref in refs[:-2]]
        out_ref[at:, :] = sum(tails)
    token_ref[...] = jnp.zeros_like(token_ref)


def gather_parts(parts, counts, riders, rider_rows, tokens):
    total, width = sum(counts), parts[0].shape[1]
    shape = shape_of(total + (rider_rows if riders else 0), width)
    return ordered_call(
        lambda *refs: gather_kernel(counts, rider_rows if riders else 0, *refs),
        tokens,
        in_specs=[VMEM] * (len(parts) + len(riders)),
        out_specs=[VMEM] * 2,
        out_shape=[shape, TOKEN],
        compiler_params=params(SMALL),
        cost_estimate=pl.CostEstimate(flops=0, bytes_accessed=1 << 10, transcendentals=0),
        name="gather_parts",
    )(*parts, *riders)


def finish_kernel(plans, maps, given, outs_count, *refs):
    pieces = len(plans)
    places, refs = refs[:pieces], refs[pieces:]
    quarters, refs = refs[: 4 * pieces], refs[4 * pieces :]
    outs, refs = refs[given : given + outs_count], refs[given + outs_count :]
    token_ref, refs = refs[0], refs[1:]
    token_ref[...] = jnp.zeros_like(token_ref)
    scratch, sems = refs[:pieces], refs[pieces:]
    leave = []
    for p, plan in enumerate(plans):
        place_ref, out_sems = places[p], sems[p]
        bits = place_ref.shape[0] - 1
        blocks = 1 << bits
        rows = scratch[p].shape[1] // blocks
        relative = place_ref[1]
        for bit in range(1, bits):
            relative = relative * 2 + place_ref[1 + bit]
        for i in range(4):
            for r in range(blocks):
                quarter, k = maps[p](i, r)
                target = pl.ds(pl.multiple_of((relative ^ k) * rows, SUBS), rows)
                scratch[p][quarter, target, :] = quarters[4 * p + i][r * rows : (r + 1) * rows, :]
        for i in range(4):
            quarter = place_ref[0] ^ i
            number = 0
            for out, moves in plan:
                for row, count, column, width, out_row, out_column in moves(quarter):
                    copy = pltpu.make_async_copy(
                        scratch[p].at[i, pl.ds(row, count), pl.ds(column, width)],
                        outs[out].at[pl.ds(out_row, count), pl.ds(out_column, width)],
                        out_sems.at[i, number],
                    )
                    copy.start()
                    leave.append(copy)
                    number += 1
    for copy in leave:
        copy.wait()


def aligned(value, step):
    return pl.multiple_of(value, step)


def as_columns(first, rows, out_row, out_column):
    return lambda q: [(first, rows, 0, QUARTER, out_row, aligned(out_column(q), LANES))]


def as_rows(first, rows, start, stop):
    def moves(q):
        return [
            (first + (c - start) // QUARTER * rows, rows, 0, QUARTER, aligned(q * rows, SUBS), c)
            for c in range(start, stop, QUARTER)
        ]

    return moves


def as_halves(first, rows, out_column):
    def moves(q):
        at = q * (2 * rows)
        return [
            (first, rows, 0, LANES, aligned(at, SUBS), out_column),
            (first, rows, LANES, LANES, aligned(at + rows, SUBS), out_column),
        ]

    return moves


def finish(pieces, plans, shapes, name, tokens=(), into=None):
    args = [v for piece in pieces for v in piece.pair + list(piece.got)]
    places = [piece.place for piece in pieces]
    scratch = [pltpu.VMEM((4,) + piece.quarter_shape(), F32) for piece in pieces]
    sems = []
    for piece, plan in zip(pieces, plans):
        number = sum(len(moves(0)) for _, moves in plan)
        sems.append(pltpu.SemaphoreType.DMA((4, number)))
    extra = [] if into is None else [into]
    return ordered_call(
        lambda *refs: finish_kernel(plans, [p.quarter_and_block for p in pieces], len(extra), len(shapes), *refs),
        tokens,
        in_specs=[SMEM] * len(places) + [VMEM] * len(args) + [HBM] * len(extra),
        out_specs=[HBM] * len(shapes) + [VMEM],
        input_output_aliases={len(places) + len(args): len(shapes) - 1} if extra else {},
        out_shape=[shape_of(*shape) for shape in shapes] + [TOKEN],
        scratch_shapes=scratch + sems,
        compiler_params=params(SMALL),
        cost_estimate=pl.CostEstimate(
            flops=0, bytes_accessed=1 << 10, transcendentals=0
        ),
        name=name,
    )(*places, *args, *extra)


class Piece:
    def __init__(self, plan, back):
        self.plan, self.back = plan, back
        self.sides = [side(step).astype(jnp.int32) for step in plan]
        first, second = self.sides[0], self.sides[1]

        def quarter(a, b):
            return 2 * a + b

        self.own_quarter = quarter(first, second).reshape(1)
        self.place = jnp.concatenate([self.own_quarter, jnp.stack(self.sides[2:])])
        self.rider, self.waiting = None, []
        self.at, self.steps = 1, 2 * len(plan)

    def quarter_and_block(self, array, row):
        apart = {step: (row >> i) & 1 for i, step in enumerate(self.back[:-2])}
        apart[self.back[-2]] = array % 2
        block = 0
        for step in self.plan[2:]:
            block = 2 * block + apart[step]
        return 2 * (array // 2) + apart[self.plan[1]], block

    def quarter_shape(self):
        return (self.pair[0].shape[0] - (0 if self.rider is None else self.rider.shape[0]), QUARTER)

    def step(self, *tokens):
        last = len(self.plan)
        if self.at < last:
            own = self.sides[self.at] if self.at > 1 else jnp.ones((), jnp.int32)
            send, self.own, token = halve(self.waiting, self.window if self.at == 1 else None, own, tokens)
            self.got = swap(send, self.plan[self.at])
            self.waiting = [self.own, self.got]
            self.at += 1
            return token
        if self.at == last:
            total, token = add(self.own, self.got, tokens)
            self.parts = [total]
            self.riders = [] if self.rider is None else [self.rider]
        else:
            self.parts.append(self.got)
            if self.rider is not None:
                self.riders = [self.whole, self.got]
        index = self.at - last
        self.at += 1
        if index < last - 1:
            rows = self.parts[0].shape[0]
            counts = [rows << max(i - 1, 0) for i in range(len(self.parts))]
            if len(self.parts) == 1 and not self.riders:
                self.whole = self.parts[0]
            else:
                height = 0 if self.rider is None else self.rider.shape[0]
                self.whole, token = gather_parts(
                    self.parts, counts, self.riders, height, tokens
                )
            self.got = swap(self.whole, self.back[index])
            return token
        self.pair = [self.whole, self.parts[-1]]
        self.got = [swap(v, self.plan[0]) for v in self.pair]
        return tokens[0]


def open_pieces(pieces, heights, send, keep):
    got = swap(send, pieces[0].plan[0])
    first = 0
    for piece, rows in zip(pieces, heights):
        piece.window = (first, rows)
        piece.waiting += [keep, got]
        first += rows


def riders_of(piece):
    return piece.pair + piece.got


def copy_out_kernel(in_ref, out_ref, sem):
    copy = pltpu.make_async_copy(in_ref, out_ref, sem)
    copy.start()
    copy.wait()


def copy_out(value, token):
    return ordered_call(
        copy_out_kernel,
        [token],
        in_specs=[VMEM],
        out_specs=HBM,
        out_shape=shape_of(*value.shape),
        scratch_shapes=[pltpu.SemaphoreType.DMA(())],
        compiler_params=params(SMALL),
        cost_estimate=pl.CostEstimate(flops=0, bytes_accessed=1 << 10, transcendentals=0),
        name="copy_out",
    )(value)


def run(token, *pieces):
    tokens = token if isinstance(token, tuple) else (token,)
    for piece in pieces:
        if piece.at < piece.steps:
            tokens = (piece.step(*tokens),)
    return tokens[0]


def local(
    inputs,
    cotangent,
    norm_gain,
    delta,
    alpha,
    beta,
    eta,
    omega,
    w_value,
    w_base,
    qk_scale,
    qk_shift,
    w_hidden,
    ffn_gain,
    w_up,
    w_down,
    lengths,
    key_mask,
):
    ways = lax.axis_size("ch")
    place = lax.axis_index("ch").astype(jnp.int32)
    _, length, narrow = inputs.shape
    rows = length // ways
    width = narrow * ways
    groups = width // LANES
    states = delta.shape[1]
    span = rows // SUBS

    x4 = lax.all_to_all(inputs.reshape(ways, rows, narrow), "ch", 0, 0)
    pairs = split_weights((w_value, w_base, w_hidden, w_up, w_down))

    def grouped(table):
        return jnp.transpose(table.reshape(groups, LANES, states), (0, 2, 1))

    gates = jax.nn.sigmoid(delta)
    decay = jax.nn.sigmoid(alpha)
    keep = 1.0 - gates * decay
    root = math.sqrt(states)
    keep4 = grouped(keep)
    coef4 = grouped(gates * beta * (eta / root))
    log_keep = jnp.log(keep4)
    chunk_keep = jnp.exp(span * log_keep)
    device_keep = jnp.exp(rows * log_keep)
    gain4 = norm_gain.reshape(groups, 1, LANES)
    omega4 = omega.reshape(groups, 1, LANES)
    place_info = place.reshape(1)

    ends_shape = jax.ShapeDtypeStruct((groups, states * SUBS, LANES), F32)
    final_shape = jax.ShapeDtypeStruct((groups, states, LANES), F32)
    big = jax.ShapeDtypeStruct((groups, rows, LANES), F32)
    normed4, ends, final = pl.pallas_call(
        norm_kernel,
        in_specs=[VMEM] * 4,
        out_specs=[VMEM] * 3,
        out_shape=[big, ends_shape, final_shape],
        compiler_params=params(NORM_MIB),
        name="norm",
    )(x4, gain4, keep4, chunk_keep)
    finals = lax.all_gather(final, "ch", axis=0)
    total4, starts = pl.pallas_call(
        mix_kernel,
        in_specs=[SMEM] + [VMEM] * 8,
        out_specs=[VMEM] * 2,
        out_shape=[big, ends_shape],
        compiler_params=params(NORM_MIB),
        name="mix",
    )(place_info, normed4, ends, finals, keep4, coef4, chunk_keep, device_keep, omega4)

    info = jnp.stack([place * rows, lengths[0].astype(jnp.int32)])
    zwidth = qk_scale.shape[1]
    plans = orders()
    unit = SUBS << (len(plans[0][0]) - 2)
    one, other, two, three = [Piece(*plan) for plan in plans]

    def height(*counts):
        return -(-sum(counts) // QUARTER // unit) * unit

    early_heights = (
        height((w_up.size + 2 * width * width) // 4),
        height((w_down.size + w_hidden.size) // 4),
    )
    late_heights = (
        height((w_value.size + width * zwidth) // 4),
        height(width * w_value.shape[1] // 4),
    )
    (
        output,
        direct4,
        *forward_rest,
    ) = forward_call(
        info,
        jnp.concatenate([one.own_quarter, other.own_quarter]),
        key_mask,
        x4,
        normed4,
        total4,
        cotangent.reshape(rows, width),
        qk_scale,
        qk_shift,
        ffn_gain.reshape(1, width),
        pairs,
        early_heights,
    )
    saved, ffn_gain_part, ffn_parts = forward_rest[:11], forward_rest[11], forward_rest[12:]
    open_pieces((one,), early_heights[:1], *ffn_parts[:2])
    open_pieces((other,), early_heights[1:], *ffn_parts[2:])
    t = run(ffn_gain_part, one, other)
    own_quarters = jnp.concatenate([two.own_quarter, three.own_quarter])
    before, omega_parts, qk_parts = (), [], []
    tiles = rows // TILE
    for lowest, count in ((0, tiles),):
        *before, qk_part, omega_part, send, keep = backward_call(
            own_quarters,
            normed4,
            total4,
            saved,
            qk_scale,
            qk_shift,
            omega4,
            pairs,
            late_heights,
            lowest,
            count,
            before,
            [t],
        )
        omega_parts.append(omega_part)
        qk_parts.append(qk_part)
        t = run(qk_part, one, other)
        send, t = gate(send, t)
        open_pieces((two, three), late_heights, send, keep)
    grad4, part4 = before
    back_ends, back_final = scan_call(
        back_ends_kernel,
        "back_ends",
        [],
        [grad4, keep4, chunk_keep],
        [ends_shape, final_shape],
        [t],
        work=2,
    )
    back_finals = lax.all_gather(back_final, "ch", axis=0)
    t = run(back_finals, two, one, three, other)
    sums, coef_parts, keep_parts = [], [], []
    tables = (keep4, coef4, chunk_keep, device_keep)
    between = [(), (two, three, one, other), (two, three, one, other), (two, three)]
    for g in range(groups):
        done, coef_part, keep_part = back_call(
            g, 1, place_info, grad4, back_ends, back_finals, starts, normed4, part4, tables, [t]
        )
        sums.append(done)
        coef_parts.append(coef_part)
        keep_parts.append(keep_part)
        t = run((coef_part, t), *between[g % 4])
    back4, two.rider = unnorm_call(
        x4,
        sums,
        direct4,
        gain4,
        coef_parts,
        keep_parts,
        omega_parts,
        ffn_gain_part,
        qk_parts,
        [t],
    )
    back4, t = gate(back4, two.rider[:SUBS, :LANES])
    returned = lax.all_to_all(back4, "ch", 0, 0)
    t = run(t, one, other, two)
    t = run(t, one, other, three)
    t = run(t, two, three)
    t = run(t, two, three)
    t = run(t, one, other, two, three)
    while one.at < one.steps or other.at < other.steps:
        t = run(t, one, other)
    while three.at < three.steps or two.at < two.steps:
        t = run(t, two, three)
    up_rows, quarter_rows = w_up.shape[0], w_down.shape[0] // 4
    reset_at = width + zwidth
    hidden_in_at = reset_at + w_value.shape[1]

    def rest_column(q):
        return jnp.where(q < 2, q * QUARTER, hidden_in_at + (q - 2) * QUARTER)

    up_grad, down_grad, hidden_grad, base_grad, t = finish(
        [one, other],
        [
            [
                (0, as_columns(0, up_rows, 0, lambda q: q * QUARTER)),
                (3, as_columns(up_rows, width, 0, rest_column)),
            ],
            [
                (1, as_rows(0, quarter_rows, 0, w_down.shape[1])),
                (
                    2,
                    as_rows(
                        quarter_rows * w_down.shape[1] // QUARTER,
                        w_hidden.shape[0] // 4,
                        0,
                        w_hidden.shape[1],
                    ),
                ),
            ],
        ],
        [w_up.shape, w_down.shape, w_hidden.shape, w_base.shape],
        "finish_one",
        [t],
    )
    value_grad, base_grad, t = finish(
        [two, three],
        [
            [
                (0, as_columns(0, width, 0, lambda q: q * QUARTER)),
                (1, as_halves(w_value.shape[0], width * zwidth // QUARTER // 4, width)),
            ],
            [(1, as_columns(0, width, 0, lambda q: reset_at + q * QUARTER))],
        ],
        [w_value.shape, w_base.shape],
        "finish_rest",
        tokens=[t],
        into=base_grad,
    )
    input_grad = copy_out(returned, t).reshape(inputs.shape)

    tables = [grouped(table) for table in (gates, decay, beta, eta)]
    gains = small_call(riders_of(two), tables)
    return (
        output.reshape(cotangent.shape),
        input_grad,
        gains[0].reshape(width),
        gains[1].T,
        gains[2].T,
        gains[3].T,
        gains[4].T,
        gains[5].reshape(width),
        value_grad,
        base_grad,
        gains[7],
        gains[8],
        hidden_grad,
        gains[6].reshape(width),
        up_grad,
        down_grad,
    )


def solution(mesh):
    whole = P()
    placed = (
        (P("seq", None, "ch"), P("seq", "ch", None))
        + (whole,) * 14
        + (P("seq"), P("seq", None))
    )
    return jax.shard_map(
        local,
        mesh=mesh,
        in_specs=placed,
        out_specs=(P("seq", "ch", None), P("seq", None, "ch")) + (whole,) * 14,
        check_vma=False,
    )
```
